256 devices in a mesh: fsdp: 64 (over x, y_hi, z), tp: 4 (over y_lo, core).
Axes of the slice: x: 4, y: 4 (y_hi: 2, y_lo: 2; y = y_hi * 2 + y_lo), z: 8, core: 2. Of those that a mesh axis runs over, the one named last changes fastest.
Arguments:
- weight_master: float32 [5120, 7168], P('fsdp', 'tp'), may hold values from -0.078125 to 0.078125
- gradient: float32 [5120, 7168], P('fsdp', 'tp'), may hold values from -6 to 6
- first_moment: float32 [5120, 7168], P('fsdp', 'tp'), may hold values from -2 to 2
- second_moment: float32 [5120, 7168], P('fsdp', 'tp'), may hold values from 0.02 to 0.2
- query_key_value_bias: bfloat16 [7168], P('tp'), may hold values from -3 to 3
- new_tokens: bfloat16 [4, 3072, 5120], P(None, 'fsdp', 'tp'), may hold values from -6 to 6
- norm_gain: bfloat16 [5120], P('tp'), may hold values from 0.25 to 1.75
- cache_len: int32 [3072], replicated, may hold values from 1 to 160, as said below
- key_cache: bfloat16 [64, 4, 96, 160, 128], P('fsdp', 'tp'), may hold values from -700 to 700
- value_cache: bfloat16 [64, 4, 96, 160, 128], P('fsdp', 'tp'), may hold values from -6 to 6
Outputs:
- new_master: float32 [5120, 7168], P('fsdp', 'tp')
- new_first: float32 [5120, 7168], P('fsdp', 'tp')
- new_second: float32 [5120, 7168], P('fsdp', 'tp')
- context: bfloat16 [4, 3072, 5120], P(None, 'fsdp', 'tp')
The draws below stay inside these ranges and needn't reach their ends.
Inputs may be any that keep to these rules, and one draw needn't show every extreme that they name: `cache_len`: among the 48 rows of each index of fsdp one has a full cache.
All inputs are finite; a program needn't handle non-finite values.
Results may differ from the reference program's by a relative error of at most 0.015.
The reference program's roundings to bfloat16 on the way count: a program that leaves them out, or rounds other values in their place, can miss the bound.
Values may be sent and summed in bfloat16 or wider, within the bound.
A program may use at most 128 MiB of HBM per device.

```python
import math
import jax
import jax.numpy as jnp
from jax import lax

D = 5120
HQ = 40
KEY_VALUE_HEADS = 8
HEAD_SIZE = 128
ROW_DEV = 48
CACHE = 160
NEW_TOKEN_COUNT = 4
QUERY_PER_GROUP = 5
QKV = 7168
TOTAL_ROWS = 3072
RG = 96
N_FSDP = 64
N_TP = 4


def draw_cache_len(key, part):
    key = jax.random.fold_in(key, 5)
    first_key, second_key = jax.random.split(key)
    drawn = jax.random.randint(first_key, (TOTAL_ROWS,), 1, CACHE + 1)
    chosen = jax.random.randint(second_key, (N_FSDP,), 0, ROW_DEV)
    row_ids = jnp.arange(TOTAL_ROWS, dtype=jnp.int32)
    full_rows = row_ids % ROW_DEV == chosen[row_ids // ROW_DEV]
    return jnp.where(full_rows, CACHE, drawn).astype(jnp.int32)


def draw_key_cache(key, part):
    key = jax.random.fold_in(key, 11)
    cache_shape = (N_FSDP, N_TP, RG, CACHE, HEAD_SIZE)
    base_keys = jax.random.normal(key, cache_shape, jnp.float32)
    return base_keys.astype(jnp.bfloat16)


def levels(own_key, dims, shards, low, largest):
    def one(dim, shards_of):
        heights = jax.random.uniform(jax.random.fold_in(jax.random.fold_in(own_key, 6), dim), (shards_of,), jnp.float32, low / len(shards), largest / len(shards))
        return jnp.repeat(jnp.exp(heights), dims[dim] // shards_of).reshape((-1,) + (1,) * (len(dims) - dim - 1))

    gain = one(*shards[0])
    for cut in shards[1:]:
        gain = gain * one(*cut)
    return gain


def gaussian(stream_key, dims, width, reach, pieces=(), kind=jnp.bfloat16):
    loudness = levels(stream_key, dims, pieces, -0.22, 0.18) if pieces else 1.0
    result = jax.random.normal(stream_key, dims, jnp.float32) * width * loudness
    return jnp.minimum(jnp.maximum(result, -reach), reach).astype(kind)


def setup_inputs(seed: int = 0) -> dict:
    key_list = jax.random.split(jax.random.key(seed), 11)
    return {
        "weight_master": gaussian(key_list[0], (D, QKV), D ** -0.5, 0.078125, ((0, 64), (1, 4)), jnp.float32),
        "gradient": gaussian(key_list[1], (D, QKV), 1.0, 6.0, ((0, 64), (1, 4)), jnp.float32),
        "first_moment": gaussian(key_list[2], (D, QKV), 0.3, 2.0, ((0, 64), (1, 4)), jnp.float32),
        "second_moment": jnp.clip(jnp.exp(math.log(0.2) - 2.3025851 * jax.random.uniform(key_list[3], (D, QKV), jnp.float32) ** levels(key_list[3], (D, QKV), ((0, 64), (1, 4)), -0.2, 0.2)), 0.02, 0.2),
        "query_key_value_bias": gaussian(key_list[4], (QKV,), 0.5, 3.0, ((0, 4),)),
        "new_tokens": gaussian(key_list[5], (NEW_TOKEN_COUNT, TOTAL_ROWS, D), 1.0, 6.0, ((1, 64), (2, 4))),
        "norm_gain": jnp.clip(1.0 + 0.15 * jax.random.normal(key_list[6], (D,), jnp.float32), 0.25, 1.75).astype(jnp.bfloat16),
        "cache_len": draw_cache_len(jax.random.fold_in(key_list[10], 71), 0),
        "key_cache": draw_key_cache(jax.random.fold_in(key_list[10], 71), 0),
        "value_cache": gaussian(key_list[9], (N_FSDP, N_TP, RG, CACHE, HEAD_SIZE), 1.0, 6.0, ((0, 64), (1, 4))),
    }


BETA_ONE = 0.9
BETA_TWO = 0.95
LEARN_RATE = 0.002
ADAM_EPS = 1e-08
CORR_ONE = 1.0 - 0.9 ** 10
CORR_TWO = 1.0 - 0.95 ** 10
NORM_EPS = 1e-06
ROPE_BASE = 1000000.0

def adam_update(weight_master, gradient, first_moment, second_moment):
    new_first = BETA_ONE * first_moment + (1.0 - BETA_ONE) * gradient
    new_second = BETA_TWO * second_moment + (1.0 - BETA_TWO) * gradient * gradient
    step_size = new_first / CORR_ONE / (jnp.sqrt(new_second / CORR_TWO) + ADAM_EPS)
    return (weight_master - LEARN_RATE * step_size, new_first, new_second)

def rms_scale(tokens, gain_row):
    floats = tokens.astype(jnp.float32)
    inverse = lax.rsqrt(lax.optimization_barrier(jnp.mean(floats * floats, axis=-1, keepdims=True)) + NORM_EPS)
    return (floats * inverse * gain_row.astype(jnp.float32)).astype(jnp.bfloat16)

def rotate(values, positions):
    half_width = values.shape[-1] // 2
    inverse = jnp.power(ROPE_BASE, -jnp.arange(half_width, dtype=jnp.float32) * (2.0 / (2 * half_width)))
    angles = positions.astype(jnp.float32)[..., None] * inverse
    cosine = jnp.cos(angles)
    sine_part = jnp.sin(angles)
    first_part = values[..., :half_width]
    second_part = values[..., half_width:]
    return jnp.concatenate([first_part * cosine - second_part * sine_part, second_part * cosine + first_part * sine_part], axis=-1)

def attend(queries, keys_new, values_new, cached_keys, cached_values, lengths):
    score_scale = 1.0 / jnp.sqrt(jnp.float32(queries.shape[-1]))
    query_f = queries.astype(jnp.float32)
    cached_scores = jnp.einsum('srbph,brlh->srbpl', query_f, cached_keys.astype(jnp.float32)) * score_scale
    position = jnp.arange(cached_keys.shape[2], dtype=jnp.int32)
    valid_mask = position[None, :] < lengths[:, None]
    cached_scores = jnp.where(valid_mask[None, :, None, None, :], cached_scores, -jnp.inf)
    fresh_scores = jnp.einsum('srbph,trbh->srbpt', query_f, keys_new.astype(jnp.float32)) * score_scale
    steps_here = queries.shape[0]
    causal = jnp.arange(steps_here)[:, None] >= jnp.arange(steps_here)[None, :]
    fresh_scores = jnp.where(causal[:, None, None, None, :], fresh_scores, -jnp.inf)
    row_max = jnp.maximum(lax.optimization_barrier(jnp.max(cached_scores, axis=-1)), lax.optimization_barrier(jnp.max(fresh_scores, axis=-1)))
    cached_exp = jnp.exp(cached_scores - row_max[..., None])
    fresh_exp = jnp.exp(fresh_scores - row_max[..., None])
    row_total = lax.optimization_barrier(jnp.sum(cached_exp, axis=-1)) + lax.optimization_barrier(jnp.sum(fresh_exp, axis=-1))
    cached_prob = (cached_exp / row_total[..., None]).astype(jnp.bfloat16)
    fresh_prob = (fresh_exp / row_total[..., None]).astype(jnp.bfloat16)
    mixed = jnp.einsum('srbpl,brlh->srbph', cached_prob.astype(jnp.float32), cached_values.astype(jnp.float32))
    mixed = mixed + jnp.einsum('srbpt,trbh->srbph', fresh_prob.astype(jnp.float32), values_new.astype(jnp.float32))
    return mixed.astype(jnp.bfloat16)

def reference(weight_master, gradient, first_moment, second_moment, query_key_value_bias, new_tokens, norm_gain, cache_len, key_cache, value_cache):
    new_master, new_first, new_second = adam_update(weight_master, gradient, first_moment, second_moment)
    weight = new_master.astype(jnp.bfloat16)
    normed = rms_scale(new_tokens, norm_gain)
    joined_projection = jnp.dot(normed.reshape(NEW_TOKEN_COUNT * TOTAL_ROWS, D), weight, preferred_element_type=jnp.float32)
    joined_projection = joined_projection.reshape(NEW_TOKEN_COUNT, TOTAL_ROWS, KEY_VALUE_HEADS, QUERY_PER_GROUP + 2, HEAD_SIZE) + query_key_value_bias.astype(jnp.float32).reshape(KEY_VALUE_HEADS, QUERY_PER_GROUP + 2, HEAD_SIZE)
    positions = cache_len[None, :] + jnp.arange(NEW_TOKEN_COUNT, dtype=jnp.int32)[:, None]
    queries = rotate(joined_projection[:, :, :, :QUERY_PER_GROUP], positions[:, :, None, None]).astype(jnp.bfloat16)
    keys_new = rotate(joined_projection[:, :, :, QUERY_PER_GROUP], positions[:, :, None]).astype(jnp.bfloat16)
    values_new = joined_projection[:, :, :, QUERY_PER_GROUP + 1].astype(jnp.bfloat16)

    def one_slot(slot_index):
        group_index = slot_index // 2
        parity = slot_index % 2
        head_index = (2 * jnp.arange(N_TP, dtype=jnp.int32) + parity).astype(jnp.int32)
        row_start = (group_index * RG).astype(jnp.int32)
        rows_query = jnp.take(lax.dynamic_slice_in_dim(queries, row_start, RG, 1), head_index, axis=2)
        rows_key = jnp.take(lax.dynamic_slice_in_dim(keys_new, row_start, RG, 1), head_index, axis=2)
        rows_value = jnp.take(lax.dynamic_slice_in_dim(values_new, row_start, RG, 1), head_index, axis=2)
        lengths = lax.dynamic_slice_in_dim(cache_len, row_start, RG, 0)
        return attend(rows_query, rows_key, rows_value, key_cache[slot_index], value_cache[slot_index], lengths)
    blocks = lax.map(one_slot, jnp.arange(N_FSDP, dtype=jnp.int32))
    blocks = blocks.reshape(N_FSDP // 2, 2, NEW_TOKEN_COUNT, RG, N_TP, QUERY_PER_GROUP, HEAD_SIZE)
    blocks = jnp.transpose(blocks, (2, 0, 3, 4, 1, 5, 6))
    context = blocks.reshape(NEW_TOKEN_COUNT, TOTAL_ROWS, HQ * HEAD_SIZE)
    return (new_master, new_first, new_second, context)
```

```python
import jax
import jax.numpy as jnp
from jax import lax
from jax.experimental import pallas as pl
from jax.experimental.pallas import tpu as pltpu
from jax.sharding import PartitionSpec as P

BETA_ONE = 0.9
BETA_TWO = 0.95
LEARN_RATE = 0.002
ADAM_EPS = 1e-08
CORR_ONE = 1.0 - 0.9**10
CORR_TWO = 1.0 - 0.95**10
NORM_EPS = 1e-06
ROPE_BASE = 1000000.0

MESH = pl.DeviceIdType.MESH
NX, NH, NZ = 4, 2, 8
NB = 4


def partner(block, axis, stride):
    count = lax.axis_size(axis)
    route = []
    for low in range(count):
        high = low | 1 << stride
        if high != low and high < count:
            route += [(low, high), (high, low)]
    return lax.ppermute(block, axis, route)


def adam_update(weight_master, gradient, first_moment, second_moment):
    new_first = BETA_ONE * first_moment + (1.0 - BETA_ONE) * gradient
    new_second = BETA_TWO * second_moment + (1.0 - BETA_TWO) * gradient * gradient
    step_size = new_first / CORR_ONE / (jnp.sqrt(new_second / CORR_TWO) + ADAM_EPS)
    return (weight_master - LEARN_RATE * step_size, new_first, new_second)


def projection_kernel(
    narrow, tokens, gain, out, W, A, N, ssq, psend, precv,
    z_send, z_recv, x_send, x_recv, q_send, q_recv,
    t_send, t_recv, s_send, s_recv, p_send, p_recv,
):
    heads, _, depth, lanes = W.shape
    rows = depth // NZ
    half = depth // 2
    f = lax.axis_index("fsdp")
    b = lax.axis_index("tp")
    x, h, z = f // (NH * NZ), (f // NZ) % NH, f % NZ
    lo, c = b // 2, b % 2
    s = z % 2

    def at(x_, h_, z_, lo_, c_):
        return {"fsdp": (x_ * NH + h_) * NZ + z_, "tp": lo_ * 2 + c_}

    x_up = at((x + 1) % NX, h, z, lo, c)
    x_down = at((x + NX - 1) % NX, h, z, lo, c)
    z_to = [at(x, h, (z + d) % NZ, lo, c) for d in range(NZ)]
    z_pair = at(x, h, z + 1 - 2 * s, lo, c)
    lo_pair = at(x, h, z, 1 - lo, c)
    sibling = at(x, h, z, lo, 1 - c)
    cross = at(x, h, z, 1 - lo, 1 - c)
    h_far = at(x, 1 - h, z, lo, c)
    h_near = at(x, 1 - h, z, 1 - lo, c)

    barrier = pltpu.get_barrier_semaphore()
    everyone = [x_up, x_down, lo_pair, sibling, cross, h_far, h_near] + z_to[1:]
    for other in everyone:
        pl.semaphore_signal(barrier, inc=1, device_id=other, device_id_type=MESH)

    flat = tokens[...].astype(jnp.float32)
    square = flat * flat
    part = square[:, :lanes]
    for k in range(1, square.shape[1] // lanes):
        part = part + square[:, k * lanes : (k + 1) * lanes]
    ssq[b] = part
    pl.semaphore_wait(barrier, len(everyone))

    sent = []

    def send(src, dst, send_sem, recv_sem, to):
        copy = pltpu.make_async_remote_copy(
            src_ref=src, dst_ref=dst, send_sem=send_sem, recv_sem=recv_sem,
            device_id=to, device_id_type=MESH,
        )
        copy.start()
        sent.append(copy)

    def arrive(dst, send_sem, recv_sem, to):
        pltpu.make_async_remote_copy(
            src_ref=dst, dst_ref=dst, send_sem=send_sem, recv_sem=recv_sem,
            device_id=to, device_id_type=MESH,
        ).wait_recv()

    def w_rows(j, x_, z_):
        return W.at[j, x_, pl.ds(pl.multiple_of(z_ * rows, 16), rows)]

    def w_group(j, x_, g):
        return W.at[j, x_, pl.ds(g * half, half)]

    own_copies = {}

    def z_out(j):
        own = pltpu.make_async_copy(narrow.at[s * heads + j], w_rows(j, x, z), z_recv.at[j, 0])
        own.start()
        own_copies[j] = own
        for d in (4, 3, 5, 2, 6, 1, 7):
            parity = (s + d) % 2
            send(narrow.at[parity * heads + j], w_rows(j, x, z), z_send.at[j, d],
                 z_recv.at[j, d], z_to[d])

    def x_out(j):
        own_copies[j].wait()
        for d in range(1, NZ):
            arrive(w_rows(j, x, (z + NZ - d) % NZ), z_send.at[j, d], z_recv.at[j, d], z_to[d])
        for g in (0, 1):
            for k, to in ((0, x_up), (1, x_down)):
                send(w_group(j, x, g), w_group(j, x, g), x_send.at[j, 2 * g + k],
                     x_recv.at[j, 2 * g + k], to)

    def x_on(j):
        for g, k in ((0, 0), (1, 1), (0, 1), (1, 0)):
            source = (x + NX - 1) % NX if k == 0 else (x + 1) % NX
            to = x_up if k == 0 else x_down
            arrive(w_group(j, source, g), x_send.at[j, 2 * g + k], x_recv.at[j, 2 * g + k], to)
            if g == k:
                send(w_group(j, source, g), w_group(j, source, g), x_send.at[j, 4 + g],
                     x_recv.at[j, 4 + g], to)

    def x_end(j):
        for g in (0, 1):
            arrive(w_group(j, (x + 2) % NX, g), x_send.at[j, 4 + g], x_recv.at[j, 4 + g],
                   x_up if g == 0 else x_down)

    def a_at(b_, h_, s_):
        return A.at[b_, 2 * h_ + s_]

    local = []
    b_lo = (1 - lo) * 2 + c

    def to_sibling(ref, kind, i):
        send(ref, ref, s_send.at[kind, i], s_recv.at[kind, i], sibling)

    def tokens_out(i, s_):
        send(N.at[1 - h, s_], a_at(b, h, s_), t_send.at[0, i], t_recv.at[0, i], h_near)
        send(N.at[h, s_], a_at(b, h, s_), t_send.at[1, i], t_recv.at[1, i], lo_pair)
        own = pltpu.make_async_copy(N.at[h, s_], a_at(b, h, s_), t_recv.at[4, i])
        own.start()
        local.append(own)
        send(N.at[h, s_], a_at(b, h, s_), s_send.at[0, i], s_recv.at[0, i], sibling)

    def tokens_on(i, s_):
        piece = a_at(b_lo, 1 - h, s_)
        arrive(piece, t_send.at[0, i], t_recv.at[0, i], h_near)
        send(piece, piece, t_send.at[2, i], t_recv.at[2, i], lo_pair)
        to_sibling(piece, 1, i)
        piece = a_at(b_lo, h, s_)
        arrive(piece, t_send.at[1, i], t_recv.at[1, i], lo_pair)
        to_sibling(piece, 2, i)

    def tokens_last(i, s_):
        piece = a_at(b, 1 - h, s_)
        arrive(piece, t_send.at[2, i], t_recv.at[2, i], lo_pair)
        to_sibling(piece, 3, i)

    def tokens_end():
        sib = lo * 2 + 1 - c
        sib_lo = (1 - lo) * 2 + 1 - c
        for i, s_ in ((0, s), (1, 1 - s)):
            local[i].wait()
            for kind, b_, h_ in ((0, sib, h), (1, sib_lo, 1 - h), (2, sib_lo, h), (3, sib, 1 - h)):
                arrive(a_at(b_, h_, s_), s_send.at[kind, i], s_recv.at[kind, i], sibling)

    def project(j):
        def block(m):
            total = jnp.dot(A[0, m], W[j, 0], preferred_element_type=jnp.float32)
            for b_ in range(1, NB):
                total = total + jnp.dot(A[b_, m], W[j, b_], preferred_element_type=jnp.float32)
            return total

        @pl.loop(0, 2)
        def _(s_):
            psend[j, s_] = block(2 * (1 - h) + s_).astype(jnp.bfloat16)

        send(psend.at[j], precv.at[j], p_send.at[j], p_recv.at[j], h_far)

        @pl.loop(0, 2)
        def _(s_):
            out[j, s_] = block(2 * h + s_)

    peers = ((sibling, 0), (lo_pair, 1), (cross, 2))
    for to, k in peers:
        send(ssq.at[b], ssq.at[b], q_send.at[k], q_recv.at[k], to)
    z_out(0)
    z_out(1)
    for to, k in peers:
        arrive(ssq.at[(b // 2 * 2 + 1 - c) if k == 0 else (b_lo if k == 1 else (1 - lo) * 2 + 1 - c)],
               q_send.at[k], q_recv.at[k], to)
    total = ssq[0] + ssq[1] + ssq[2] + ssq[3]
    width = NB * tokens.shape[1]
    inverse = lax.rsqrt(jnp.sum(total, axis=1, keepdims=True) * (1.0 / width) + NORM_EPS)
    gains = gain[...].astype(jnp.float32)
    scaled = (tokens[...].astype(jnp.float32) * inverse * gains).astype(jnp.bfloat16)
    N[0, s] = scaled[:, :depth]
    N[1, s] = scaled[:, depth:]
    tokens_out(0, s)
    send(N.at[1 - h, s], N.at[1 - h, s], t_send.at[3, 0], t_recv.at[3, 0], z_pair)
    send(N.at[h, s], N.at[h, s], t_send.at[3, 1], t_recv.at[3, 1], z_pair)
    x_out(0)
    z_out(2)
    x_out(1)
    x_on(0)
    z_out(3)
    tokens_on(0, s)
    for k, h_ in ((0, 1 - h), (1, h)):
        arrive(N.at[h_, 1 - s], t_send.at[3, k], t_recv.at[3, k], z_pair)
    tokens_out(1, 1 - s)
    x_out(2)
    x_on(1)
    z_out(4)
    tokens_last(0, s)
    x_out(3)
    x_on(2)
    z_out(5)
    tokens_on(1, 1 - s)
    x_out(4)
    x_on(3)
    z_out(6)
    x_out(5)
    x_on(4)
    tokens_last(1, 1 - s)
    x_out(6)
    tokens_end()
    for j in range(heads):
        if j == 3:
            x_on(5)
        if j == 5:
            x_on(6)
        x_end(j)
        project(j)
    for j in range(heads):
        arrive(precv.at[j], p_send.at[j], p_recv.at[j], h_far)
        out[j] = out[j] + precv[j].astype(jnp.float32)
    for copy in sent:
        copy.wait_send()


def project_tokens(narrow, tokens, gain):
    twice, rows, lanes = narrow.shape
    heads = twice // 2
    count, width = tokens.shape
    depth = width // 2
    assert depth == NZ * rows
    dma = pltpu.SemaphoreType.DMA
    vmem = pl.BlockSpec(memory_space=pltpu.VMEM)
    return pl.pallas_call(
        projection_kernel,
        name="gather_project",
        out_shape=jax.ShapeDtypeStruct((heads, 2, count, lanes), jnp.float32),
        in_specs=[vmem] * 3,
        out_specs=vmem,
        scratch_shapes=[
            pltpu.VMEM((heads, NX, depth, lanes), jnp.bfloat16),
            pltpu.VMEM((NB, 2 * NH, count, depth), jnp.bfloat16),
            pltpu.VMEM((NH, 2, count, depth), jnp.bfloat16),
            pltpu.VMEM((NB, count, lanes), jnp.float32),
            pltpu.VMEM((heads, 2, count, lanes), jnp.bfloat16),
            pltpu.VMEM((heads, 2, count, lanes), jnp.bfloat16),
            dma((heads, NZ)), dma((heads, NZ)),
            dma((heads, 6)), dma((heads, 6)),
            dma((3,)), dma((3,)),
            dma((5, 2)), dma((5, 2)),
            dma((4, 2)), dma((4, 2)),
            dma((heads,)), dma((heads,)),
        ],
        compiler_params=pltpu.CompilerParams(
            collective_id=0, has_side_effects=True, vmem_limit_bytes=40 << 20
        ),
        cost_estimate=pl.CostEstimate(
            flops=2 * 4 * count * 4 * depth * heads * lanes, bytes_accessed=4 << 20, transcendentals=0
        ),
    )(narrow, tokens, gain)


def rotate(values, positions):
    half_width = values.shape[-1] // 2
    inverse = jnp.power(
        ROPE_BASE, -jnp.arange(half_width, dtype=jnp.float32) * (2.0 / (2 * half_width))
    )
    angles = positions.astype(jnp.float32)[..., None] * inverse
    cosine = jnp.cos(angles)
    sine_part = jnp.sin(angles)
    first_part = values[..., :half_width]
    second_part = values[..., half_width:]
    return jnp.concatenate(
        [
            first_part * cosine - second_part * sine_part,
            second_part * cosine + first_part * sine_part,
        ],
        axis=-1,
    )


def attend(queries, keys_new, values_new, cached_keys, cached_values, lengths):
    score_scale = 1.0 / jnp.sqrt(jnp.float32(queries.shape[-1]))
    cached_scores = (
        jnp.einsum("srbph,brlh->srbpl", queries, cached_keys, preferred_element_type=jnp.float32)
        * score_scale
    )
    position = jnp.arange(cached_keys.shape[2], dtype=jnp.int32)
    valid_mask = position[None, :] < lengths[:, None]
    cached_scores = jnp.where(valid_mask[None, :, None, None, :], cached_scores, -jnp.inf)
    fresh_scores = (
        jnp.einsum("srbph,trbh->srbpt", queries, keys_new, preferred_element_type=jnp.float32)
        * score_scale
    )
    steps_here = queries.shape[0]
    causal = jnp.arange(steps_here)[:, None] >= jnp.arange(steps_here)[None, :]
    fresh_scores = jnp.where(causal[:, None, None, None, :], fresh_scores, -jnp.inf)
    row_max = jnp.maximum(jnp.max(cached_scores, axis=-1), jnp.max(fresh_scores, axis=-1))
    cached_exp = jnp.exp(cached_scores - row_max[..., None])
    fresh_exp = jnp.exp(fresh_scores - row_max[..., None])
    row_total = jnp.sum(cached_exp, axis=-1) + jnp.sum(fresh_exp, axis=-1)
    cached_prob = (cached_exp / row_total[..., None]).astype(jnp.bfloat16)
    fresh_prob = (fresh_exp / row_total[..., None]).astype(jnp.bfloat16)
    mixed = jnp.einsum(
        "srbpl,brlh->srbph", cached_prob, cached_values, preferred_element_type=jnp.float32
    )
    mixed = mixed + jnp.einsum(
        "srbpt,trbh->srbph", fresh_prob, values_new, preferred_element_type=jnp.float32
    )
    return mixed.astype(jnp.bfloat16)


def on_device(
    weight_master,
    gradient,
    first_moment,
    second_moment,
    query_key_value_bias,
    new_tokens,
    norm_gain,
    cache_len,
    key_cache,
    value_cache,
):
    new_master, new_first, new_second = adam_update(
        weight_master, gradient, first_moment, second_moment
    )
    head_dim = key_cache.shape[-1]
    rows_here, columns = new_master.shape
    half_cols = columns // 2
    per_group = half_cols // head_dim
    narrow = new_master.astype(jnp.bfloat16).reshape(rows_here, 2 * per_group, head_dim)
    narrow = narrow.transpose(1, 0, 2)
    fsdp_index = lax.axis_index("fsdp")
    parity = fsdp_index % 2
    own_bias = lax.dynamic_slice_in_dim(query_key_value_bias, parity * half_cols, half_cols, 0)
    is_first = parity == 0
    steps_here, own_rows, features = new_tokens.shape
    group_rows = 2 * own_rows
    group_start = fsdp_index // 2 * group_rows
    group_len = lax.dynamic_slice_in_dim(cache_len, group_start, group_rows, 0)
    joined = project_tokens(
        narrow, new_tokens.reshape(steps_here * own_rows, features), norm_gain.reshape(1, features)
    )
    joined = joined + own_bias.astype(jnp.float32).reshape(per_group, 1, 1, head_dim)
    joined = joined.reshape(per_group, 2, steps_here, own_rows, head_dim)
    joined = joined.transpose(2, 1, 3, 0, 4).reshape(
        steps_here, group_rows, 1, per_group, head_dim
    )
    positions = group_len[None, :] + jnp.arange(steps_here, dtype=jnp.int32)[:, None]
    queries = rotate(
        joined[:, :, :, : per_group - 2], positions[:, :, None, None]
    ).astype(jnp.bfloat16)
    keys_new = rotate(joined[:, :, :, per_group - 2], positions[:, :, None]).astype(
        jnp.bfloat16
    )
    values_new = joined[:, :, :, per_group - 1].astype(jnp.bfloat16)
    attended = attend(queries, keys_new, values_new, key_cache[0], value_cache[0], group_len)
    attended = attended.reshape(steps_here, group_rows, (per_group - 2) * head_dim)
    own_count = group_rows // 2
    own_context = lax.dynamic_slice_in_dim(attended, parity * own_count, own_count, 1)
    their_context = lax.dynamic_slice_in_dim(attended, (1 - parity) * own_count, own_count, 1)
    returned = partner(their_context, "fsdp", 0)
    output = jnp.concatenate(
        [jnp.where(is_first, own_context, returned), jnp.where(is_first, returned, own_context)],
        axis=2,
    )
    return (new_master, new_first, new_second, output)


def solution(mesh):
    in_specs = (
        P("fsdp", "tp"),
        P("fsdp", "tp"),
        P("fsdp", "tp"),
        P("fsdp", "tp"),
        P("tp"),
        P(None, "fsdp", "tp"),
        P("tp"),
        P(),
        P("fsdp", "tp", None, None, None),
        P("fsdp", "tp", None, None, None),
    )
    out_specs = (P("fsdp", "tp"), P("fsdp", "tp"), P("fsdp", "tp"), P(None, "fsdp", "tp"))
    return jax.shard_map(
        on_device, mesh=mesh, in_specs=in_specs, out_specs=out_specs, check_vma=False
    )
```

```python
import math

import jax
import jax.numpy as jnp
import numpy as np
from jax import lax
from jax.experimental import pallas as pl
from jax.experimental.pallas import tpu as pltpu
from jax.sharding import PartitionSpec as P

BETA_ONE = 0.9
BETA_TWO = 0.95
LEARN_RATE = 0.002
ADAM_EPS = 1e-08
CORR_ONE = 1.0 - 0.9**10
CORR_TWO = 1.0 - 0.95**10
NORM_EPS = 1e-06
ROPE_BASE = 1000000.0

MESH = pl.DeviceIdType.MESH
NX, NH, NZ = 4, 2, 8
NB = 4
NEW = 4
AT_ONCE = 4


def adam_update(weight_master, gradient, first_moment, second_moment):
    new_first = BETA_ONE * first_moment + (1.0 - BETA_ONE) * gradient
    new_second = BETA_TWO * second_moment + (1.0 - BETA_TWO) * gradient * gradient
    step_size = new_first / CORR_ONE / (jnp.sqrt(new_second / CORR_TWO) + ADAM_EPS)
    return (weight_master - LEARN_RATE * step_size, new_first, new_second)


def layer_kernel(
    lengths, frequency, narrow, tokens, gain, bias, keys_in, values_in, context,
    W, A, N, ssq, psend, precv, J, cosine, sine, keys, values, mine, theirs,
    z_send, z_recv, x_send, x_recv, q_send, q_recv,
    t_send, t_recv, s_send, s_recv, p_send, p_recv, e_send, e_recv, c_sem,
):
    heads, _, depth, lanes = W.shape
    rows = depth // NZ
    half = depth // 2
    f = lax.axis_index("fsdp")
    b = lax.axis_index("tp")
    x, h, z = f // (NH * NZ), (f // NZ) % NH, f % NZ
    lo, c = b // 2, b % 2
    s = z % 2

    def at(x_, h_, z_, lo_, c_):
        return {"fsdp": (x_ * NH + h_) * NZ + z_, "tp": lo_ * 2 + c_}

    x_up = at((x + 1) % NX, h, z, lo, c)
    x_down = at((x + NX - 1) % NX, h, z, lo, c)
    z_to = [at(x, h, (z + d) % NZ, lo, c) for d in range(NZ)]
    z_pair = at(x, h, z + 1 - 2 * s, lo, c)
    lo_pair = at(x, h, z, 1 - lo, c)
    sibling = at(x, h, z, lo, 1 - c)
    cross = at(x, h, z, 1 - lo, 1 - c)
    h_far = at(x, 1 - h, z, lo, c)
    h_near = at(x, 1 - h, z, 1 - lo, c)

    barrier = pltpu.get_barrier_semaphore()
    everyone = [x_up, x_down, lo_pair, sibling, cross, h_far, h_near] + z_to[1:]
    for other in everyone:
        pl.semaphore_signal(barrier, inc=1, device_id=other, device_id_type=MESH)

    loads = [
        pltpu.make_async_copy(keys_in, keys, c_sem.at[0]),
        pltpu.make_async_copy(values_in, values, c_sem.at[1]),
    ]
    for load in loads:
        load.start()

    count, width = tokens.shape
    own_rows = count // NEW
    to_row = lax.broadcasted_iota(jnp.int32, (count, count), 0)
    to_col = lax.broadcasted_iota(jnp.int32, (count, count), 1)
    order = (to_col == to_row % NEW * own_rows + to_row // NEW).astype(jnp.bfloat16)
    back = (to_row == to_col % NEW * own_rows + to_col // NEW).astype(jnp.bfloat16)
    flat = jnp.dot(order, tokens[...], preferred_element_type=jnp.float32)
    square = flat * flat
    part = square[:, :lanes]
    for k in range(1, square.shape[1] // lanes):
        part = part + square[:, k * lanes : (k + 1) * lanes]
    ssq[b] = part
    pl.semaphore_wait(barrier, len(everyone))

    sent = []

    def send(src, dst, send_sem, recv_sem, to):
        copy = pltpu.make_async_remote_copy(
            src_ref=src, dst_ref=dst, send_sem=send_sem, recv_sem=recv_sem,
            device_id=to, device_id_type=MESH,
        )
        copy.start()
        sent.append(copy)

    def arrive(dst, send_sem, recv_sem, to):
        pltpu.make_async_remote_copy(
            src_ref=dst, dst_ref=dst, send_sem=send_sem, recv_sem=recv_sem,
            device_id=to, device_id_type=MESH,
        ).wait_recv()

    def w_rows(j, x_, z_):
        return W.at[j, x_, pl.ds(pl.multiple_of(z_ * rows, 16), rows)]

    def w_group(j, x_, g):
        return W.at[j, x_, pl.ds(g * half, half)]

    own_copies = {}

    def z_out(j):
        own = pltpu.make_async_copy(narrow.at[s * heads + j], w_rows(j, x, z), z_recv.at[j, 0])
        own.start()
        own_copies[j] = own
        for d in (4, 3, 5, 2, 6, 1, 7):
            parity = (s + d) % 2
            send(narrow.at[parity * heads + j], w_rows(j, x, z), z_send.at[j, d],
                 z_recv.at[j, d], z_to[d])

    def x_out(j):
        own_copies[j].wait()
        for d in range(1, NZ):
            arrive(w_rows(j, x, (z + NZ - d) % NZ), z_send.at[j, d], z_recv.at[j, d], z_to[d])
        for g in (0, 1):
            for k, to in ((0, x_up), (1, x_down)):
                send(w_group(j, x, g), w_group(j, x, g), x_send.at[j, 2 * g + k],
                     x_recv.at[j, 2 * g + k], to)

    def x_on(j):
        for g, k in ((0, 0), (1, 1), (0, 1), (1, 0)):
            source = (x + NX - 1) % NX if k == 0 else (x + 1) % NX
            to = x_up if k == 0 else x_down
            arrive(w_group(j, source, g), x_send.at[j, 2 * g + k], x_recv.at[j, 2 * g + k], to)
            if g == k:
                send(w_group(j, source, g), w_group(j, source, g), x_send.at[j, 4 + g],
                     x_recv.at[j, 4 + g], to)

    def x_end(j):
        for g in (0, 1):
            arrive(w_group(j, (x + 2) % NX, g), x_send.at[j, 4 + g], x_recv.at[j, 4 + g],
                   x_up if g == 0 else x_down)

    def a_at(b_, h_, s_):
        return A.at[b_, 2 * h_ + s_]

    local = []
    b_lo = (1 - lo) * 2 + c

    def to_sibling(ref, kind, i):
        send(ref, ref, s_send.at[kind, i], s_recv.at[kind, i], sibling)

    def tokens_out(i, s_):
        send(N.at[1 - h, s_], a_at(b, h, s_), t_send.at[0, i], t_recv.at[0, i], h_near)
        send(N.at[h, s_], a_at(b, h, s_), t_send.at[1, i], t_recv.at[1, i], lo_pair)
        own = pltpu.make_async_copy(N.at[h, s_], a_at(b, h, s_), t_recv.at[4, i])
        own.start()
        local.append(own)
        send(N.at[h, s_], a_at(b, h, s_), s_send.at[0, i], s_recv.at[0, i], sibling)

    def tokens_on(i, s_):
        piece = a_at(b_lo, 1 - h, s_)
        arrive(piece, t_send.at[0, i], t_recv.at[0, i], h_near)
        send(piece, piece, t_send.at[2, i], t_recv.at[2, i], lo_pair)
        to_sibling(piece, 1, i)
        piece = a_at(b_lo, h, s_)
        arrive(piece, t_send.at[1, i], t_recv.at[1, i], lo_pair)
        to_sibling(piece, 2, i)

    def tokens_last(i, s_):
        piece = a_at(b, 1 - h, s_)
        arrive(piece, t_send.at[2, i], t_recv.at[2, i], lo_pair)
        to_sibling(piece, 3, i)

    def tokens_end():
        sib = lo * 2 + 1 - c
        sib_lo = (1 - lo) * 2 + 1 - c
        for i, s_ in ((0, s), (1, 1 - s)):
            local[i].wait()
            for kind, b_, h_ in ((0, sib, h), (1, sib_lo, 1 - h), (2, sib_lo, h), (3, sib, 1 - h)):
                arrive(a_at(b_, h_, s_), s_send.at[kind, i], s_recv.at[kind, i], sibling)

    def project(j):
        def block(m):
            total = jnp.dot(A[0, m], W[j, 0], preferred_element_type=jnp.float32)
            for b_ in range(1, NB):
                total = total + jnp.dot(A[b_, m], W[j, b_], preferred_element_type=jnp.float32)
            return total

        @pl.loop(0, 2)
        def _(s_):
            psend[j, s_] = block(2 * (1 - h) + s_).astype(jnp.bfloat16)

        send(psend.at[j], precv.at[j], p_send.at[j], p_recv.at[j], h_far)

        @pl.loop(0, 2)
        def _(s_):
            J[j, s_] = block(2 * h + s_)

    own_lens = f // 2 * (2 * own_rows)
    two_rows = 2 * NEW
    down = lax.broadcasted_iota(jnp.int32, (two_rows, 1), 0)
    sign = jnp.where(lax.broadcasted_iota(jnp.int32, (1, lanes), 1) < lanes // 2, -1.0, 1.0)

    def tables(s_):
        @pl.loop(0, own_rows // 2)
        def _(i):
            r = own_lens + s_ * own_rows + 2 * i
            position = jnp.where(down < NEW, lengths[r], lengths[r + 1]) + down % NEW
            angle = position.astype(jnp.float32) * frequency[...]
            here = pl.ds(pl.multiple_of(i * two_rows, two_rows), two_rows)
            cosine[s_, here] = jnp.cos(angle)
            sine[s_, here] = jnp.sin(angle) * sign

    peers = ((sibling, 0), (lo_pair, 1), (cross, 2))
    for to, k in peers:
        send(ssq.at[b], ssq.at[b], q_send.at[k], q_recv.at[k], to)
    z_out(0)
    z_out(1)
    for to, k in peers:
        arrive(ssq.at[(b // 2 * 2 + 1 - c) if k == 0 else (b_lo if k == 1 else (1 - lo) * 2 + 1 - c)],
               q_send.at[k], q_recv.at[k], to)
    total = ssq[0] + ssq[1] + ssq[2] + ssq[3]
    inverse = lax.rsqrt(jnp.sum(total, axis=1, keepdims=True) * (1.0 / (NB * width)) + NORM_EPS)
    gains = gain[...].astype(jnp.float32).reshape(1, width)
    scaled = (flat * inverse * gains).astype(jnp.bfloat16)
    N[0, s] = scaled[:, :depth]
    N[1, s] = scaled[:, depth:]
    tokens_out(0, s)
    send(N.at[1 - h, s], N.at[1 - h, s], t_send.at[3, 0], t_recv.at[3, 0], z_pair)
    send(N.at[h, s], N.at[h, s], t_send.at[3, 1], t_recv.at[3, 1], z_pair)
    x_out(0)
    z_out(2)
    x_out(1)
    x_on(0)
    z_out(3)
    tokens_on(0, s)
    for k, h_ in ((0, 1 - h), (1, h)):
        arrive(N.at[h_, 1 - s], t_send.at[3, k], t_recv.at[3, k], z_pair)
    tokens_out(1, 1 - s)
    x_out(2)
    tables(0)
    x_on(1)
    z_out(4)
    tokens_last(0, s)
    x_out(3)
    tables(1)
    x_on(2)
    z_out(5)
    tokens_on(1, 1 - s)
    x_out(4)
    x_on(3)
    z_out(6)
    x_out(5)
    x_on(4)
    tokens_last(1, 1 - s)
    x_out(6)
    tokens_end()
    for j in range(heads):
        if j == 3:
            x_on(5)
        if j == 5:
            x_on(6)
        x_end(j)
        project(j)
    lens_at = f // 2 * (2 * own_rows)
    queries = heads - 2
    offsets = bias[...].astype(jnp.float32).reshape(1, 2 * heads * lanes)
    offsets = jnp.where(s == 0, offsets[:, : heads * lanes], offsets[:, heads * lanes :])
    for j in range(heads):
        arrive(precv.at[j], p_send.at[j], p_recv.at[j], h_far)
        offset = offsets[:, j * lanes : (j + 1) * lanes]
        for s_ in (0, 1):
            full = J[j, s_] + precv[j, s_].astype(jnp.float32) + offset
            if j <= queries:
                full = full * cosine[s_] + pltpu.roll(full, lanes // 2, 1) * sine[s_]
            J[j, s_] = full.astype(jnp.bfloat16).astype(jnp.float32)

    for load in loads:
        load.wait()
    slots = keys.shape[1]
    two = 2 * NEW
    wide = -(-(2 * slots + two) // 128) * 128
    col = lax.broadcasted_iota(jnp.int32, (two, wide), 1)
    row = lax.broadcasted_iota(jnp.int32, (two, wide), 0)
    never = 1 << 20
    second = (col >= slots).astype(jnp.int32)
    place = jnp.where(second == row // NEW, col - second * slots, never)
    new = col - 2 * slots
    seen = (new // NEW == row // NEW) & (new % NEW <= row % NEW) & (new < two)
    place = jnp.where(col < 2 * slots, place, jnp.where(seen, -1, never))
    first_row = lax.broadcasted_iota(jnp.int32, (two, 1), 0) < NEW
    scale = 1.0 / math.sqrt(lanes)

    def extend(cached, fresh):
        rest = jnp.zeros((wide - 2 * slots - two, lanes), jnp.float32)
        tail = jnp.concatenate([fresh, rest], axis=0).astype(jnp.bfloat16)
        return jnp.concatenate([cached.reshape(2 * slots, lanes), tail], axis=0)

    def pair(s_, i):
        rows_here = pl.ds(pl.multiple_of(i * two, two), two)
        r = s_ * own_rows + 2 * i
        q = jnp.concatenate([J[j, s_, rows_here] for j in range(queries)], axis=0)
        k = extend(keys[pl.ds(r, 2)], J[queries, s_, rows_here])
        scores = lax.dot_general(
            q.astype(jnp.bfloat16), k, (((1,), (1,)), ((), ())),
            preferred_element_type=jnp.float32,
        ) * scale
        limit = jnp.where(first_row, lengths[lens_at + r], lengths[lens_at + r + 1])
        scores = scores.reshape(queries, two, wide)
        scores = jnp.where((place < limit)[None], scores, -jnp.inf)
        grown = jnp.exp(scores - jnp.max(scores, axis=-1, keepdims=True))
        probs = grown * (1.0 / jnp.sum(grown, axis=-1, keepdims=True))
        probs = probs.reshape(queries * two, wide).astype(jnp.bfloat16)
        v = extend(values[pl.ds(r, 2)], J[queries + 1, s_, rows_here])
        return jnp.dot(probs, v, preferred_element_type=jnp.float32)

    block_rows = AT_ONCE * two

    def attend(s_, blocks, into):
        @pl.loop(*blocks)
        def _(t):
            done = [pair(s_, t * AT_ONCE + k) for k in range(AT_ONCE)]
            for j in range(queries):
                tile = jnp.concatenate([d[j * two : (j + 1) * two] for d in done], axis=0)
                into[pl.ds(pl.multiple_of(t * block_rows, 16), block_rows),
                     j * lanes : (j + 1) * lanes] = tile.astype(jnp.bfloat16)

    blocks = count // block_rows
    cut = blocks // 2
    for k, (start, stop) in enumerate(((0, cut), (cut, blocks))):
        attend(1 - s, (start, stop), mine.at[0])
        span = pl.ds(start * block_rows, (stop - start) * block_rows)
        send(mine.at[0, span], theirs.at[span], e_send.at[k], e_recv.at[k], z_pair)
    attend(s, (0, blocks), mine.at[1])
    piece = queries * lanes
    context[:, pl.ds(pl.multiple_of(s * piece, 128), piece)] = jnp.dot(
        back, mine[1], preferred_element_type=jnp.float32
    ).astype(jnp.bfloat16)
    for k, (start, stop) in enumerate(((0, cut), (cut, blocks))):
        span = pl.ds(start * block_rows, (stop - start) * block_rows)
        arrive(theirs.at[span], e_send.at[k], e_recv.at[k], z_pair)
    context[:, pl.ds(pl.multiple_of((1 - s) * piece, 128), piece)] = jnp.dot(
        back, theirs[...], preferred_element_type=jnp.float32
    ).astype(jnp.bfloat16)
    for copy in sent:
        copy.wait_send()


def project_tokens(lengths, narrow, tokens, gain, bias, keys, values):
    twice, rows, lanes = narrow.shape
    heads = twice // 2
    count, width = tokens.shape
    depth = width // 2
    assert depth == NZ * rows
    piece = (heads - 2) * lanes
    half_lanes = lanes // 2
    frequency = ROPE_BASE ** (-(np.arange(lanes) % half_lanes) / half_lanes)
    frequency = jnp.asarray(frequency.reshape(1, lanes), jnp.float32)
    dma = pltpu.SemaphoreType.DMA
    vmem = pl.BlockSpec(memory_space=pltpu.VMEM)
    hbm = pl.BlockSpec(memory_space=pl.ANY)
    return pl.pallas_call(
        layer_kernel,
        name="gather_project",
        out_shape=jax.ShapeDtypeStruct((count, 2 * piece), jnp.bfloat16),
        in_specs=[pl.BlockSpec(memory_space=pltpu.SMEM)] + [vmem] * 5 + [hbm] * 2,
        out_specs=vmem,
        scratch_shapes=[
            pltpu.VMEM((heads, NX, depth, lanes), jnp.bfloat16),
            pltpu.VMEM((NB, 2 * NH, count, depth), jnp.bfloat16),
            pltpu.VMEM((NH, 2, count, depth), jnp.bfloat16),
            pltpu.VMEM((NB, count, lanes), jnp.float32),
            pltpu.VMEM((heads, 2, count, lanes), jnp.bfloat16),
            pltpu.VMEM((heads, 2, count, lanes), jnp.bfloat16),
            pltpu.VMEM((heads, 2, count, lanes), jnp.float32),
            pltpu.VMEM((2, count, lanes), jnp.float32),
            pltpu.VMEM((2, count, lanes), jnp.float32),
            pltpu.VMEM(keys.shape, keys.dtype),
            pltpu.VMEM(values.shape, values.dtype),
            pltpu.VMEM((2, count, piece), jnp.bfloat16),
            pltpu.VMEM((count, piece), jnp.bfloat16),
            dma((heads, NZ)), dma((heads, NZ)),
            dma((heads, 6)), dma((heads, 6)),
            dma((3,)), dma((3,)),
            dma((5, 2)), dma((5, 2)),
            dma((4, 2)), dma((4, 2)),
            dma((heads,)), dma((heads,)),
            dma((2,)), dma((2,)), dma((2,)),
        ],
        compiler_params=pltpu.CompilerParams(
            collective_id=0, has_side_effects=True, vmem_limit_bytes=48 << 20
        ),
        cost_estimate=pl.CostEstimate(
            flops=2 * 4 * count * 4 * depth * heads * lanes, bytes_accessed=12 << 20, transcendentals=0
        ),
    )(lengths, frequency, narrow, tokens, gain, bias, keys, values)


def on_device(
    weight_master,
    gradient,
    first_moment,
    second_moment,
    query_key_value_bias,
    new_tokens,
    norm_gain,
    cache_len,
    key_cache,
    value_cache,
):
    new_master, new_first, new_second = adam_update(
        weight_master, gradient, first_moment, second_moment
    )
    head_dim = key_cache.shape[-1]
    rows_here, columns = new_master.shape
    half_cols = columns // 2
    per_group = half_cols // head_dim
    narrow = new_master.astype(jnp.bfloat16).reshape(rows_here, 2 * per_group, head_dim)
    narrow = narrow.transpose(1, 0, 2)
    steps_here, own_rows, features = new_tokens.shape
    output = project_tokens(
        cache_len, narrow, new_tokens.reshape(steps_here * own_rows, features), norm_gain,
        query_key_value_bias, key_cache[0, 0], value_cache[0, 0],
    )
    output = output.reshape(steps_here, own_rows, features)
    return (new_master, new_first, new_second, output)


def solution(mesh):
    in_specs = (
        P("fsdp", "tp"),
        P("fsdp", "tp"),
        P("fsdp", "tp"),
        P("fsdp", "tp"),
        P("tp"),
        P(None, "fsdp", "tp"),
        P("tp"),
        P(),
        P("fsdp", "tp", None, None, None),
        P("fsdp", "tp", None, None, None),
    )
    out_specs = (P("fsdp", "tp"), P("fsdp", "tp"), P("fsdp", "tp"), P(None, "fsdp", "tp"))
    return jax.shard_map(
        on_device, mesh=mesh, in_specs=in_specs, out_specs=out_specs, check_vma=False
    )
```

```python
import math

import jax
import jax.numpy as jnp
import numpy as np
from jax import lax
from jax.experimental import pallas as pl
from jax.experimental.pallas import tpu as pltpu
from jax.sharding import PartitionSpec as P

BETA_ONE = 0.9
BETA_TWO = 0.95
LEARN_RATE = 0.002
ADAM_EPS = 1e-08
CORR_ONE = 1.0 - 0.9**10
CORR_TWO = 1.0 - 0.95**10
NORM_EPS = 1e-06
ROPE_BASE = 1000000.0

MESH = pl.DeviceIdType.MESH
NX, NH, NZ = 4, 2, 8
NB = 4
NEW = 4
CUTS = 2
AT_ONCE = 8


def adam_update(weight_master, gradient, first_moment, second_moment):
    new_first = BETA_ONE * first_moment + (1.0 - BETA_ONE) * gradient
    new_second = BETA_TWO * second_moment + (1.0 - BETA_TWO) * gradient * gradient
    step_size = new_first / CORR_ONE / (jnp.sqrt(new_second / CORR_TWO) + ADAM_EPS)
    return (weight_master - LEARN_RATE * step_size, new_first, new_second)


def layer_kernel(
    lengths, frequency, narrow, tokens, gain, bias, keys_in, values_in, context,
    W, A, N, ssq, psend, precv, J, cosine, sine, keys, values, mine, theirs,
    z_send, z_recv, x_send, x_recv, q_send, q_recv,
    t1_send, t1_recv, t_send, t_recv, l_sem, s_send, s_recv, p_send, p_recv, e_send, e_recv, c_sem,
):
    heads, _, depth, lanes = W.shape
    rows = depth // NZ
    half = depth // 2
    f = lax.axis_index("fsdp")
    b = lax.axis_index("tp")
    x, h, z = f // (NH * NZ), (f // NZ) % NH, f % NZ
    lo, c = b // 2, b % 2
    s = z % 2

    def at(x_, h_, z_, lo_, c_):
        return {"fsdp": (x_ * NH + h_) * NZ + z_, "tp": lo_ * 2 + c_}

    x_up = at((x + 1) % NX, h, z, lo, c)
    x_down = at((x + NX - 1) % NX, h, z, lo, c)
    z_to = [at(x, h, (z + d) % NZ, lo, c) for d in range(NZ)]
    z_pair = at(x, h, z + 1 - 2 * s, lo, c)
    lo_pair = at(x, h, z, 1 - lo, c)
    sibling = at(x, h, z, lo, 1 - c)
    cross = at(x, h, z, 1 - lo, 1 - c)
    h_far = at(x, 1 - h, z, lo, c)
    h_near = at(x, 1 - h, z, 1 - lo, c)

    barrier = pltpu.get_barrier_semaphore()
    everyone = [x_up, x_down, lo_pair, sibling, cross, h_far, h_near] + z_to[1:]
    for other in everyone:
        pl.semaphore_signal(barrier, inc=1, device_id=other, device_id_type=MESH)

    loads = [
        pltpu.make_async_copy(keys_in, keys, c_sem.at[0]),
        pltpu.make_async_copy(values_in, values, c_sem.at[1]),
    ]
    for load in loads:
        load.start()

    count, width = tokens.shape
    own_rows = count // NEW
    flat = tokens[...].astype(jnp.float32)
    square = flat * flat
    part = square[:, :lanes]
    for k in range(1, square.shape[1] // lanes):
        part = part + square[:, k * lanes : (k + 1) * lanes]
    ssq[b] = part
    pl.semaphore_wait(barrier, len(everyone))

    sent = []

    def send(src, dst, send_sem, recv_sem, to):
        copy = pltpu.make_async_remote_copy(
            src_ref=src, dst_ref=dst, send_sem=send_sem, recv_sem=recv_sem,
            device_id=to, device_id_type=MESH,
        )
        copy.start()
        sent.append(copy)

    def arrive(dst, send_sem, recv_sem, to):
        pltpu.make_async_remote_copy(
            src_ref=dst, dst_ref=dst, send_sem=send_sem, recv_sem=recv_sem,
            device_id=to, device_id_type=MESH,
        ).wait_recv()

    def w_rows(j, x_, z_):
        return W.at[j, x_, pl.ds(pl.multiple_of(z_ * rows, 16), rows)]

    def w_group(j, x_, g):
        return W.at[j, x_, pl.ds(g * half, half)]

    own_copies = {}

    def z_out(j):
        own = pltpu.make_async_copy(narrow.at[s * heads + j], w_rows(j, x, z), z_recv.at[j, 0])
        own.start()
        own_copies[j] = own
        for d in (4, 3, 5, 2, 6, 1, 7):
            parity = (s + d) % 2
            send(narrow.at[parity * heads + j], w_rows(j, x, z), z_send.at[j, d],
                 z_recv.at[j, d], z_to[d])

    def x_out(j):
        own_copies[j].wait()
        for d in range(1, NZ):
            arrive(w_rows(j, x, (z + NZ - d) % NZ), z_send.at[j, d], z_recv.at[j, d], z_to[d])
        for g in (0, 1):
            for k, to in ((0, x_up), (1, x_down)):
                send(w_group(j, x, g), w_group(j, x, g), x_send.at[j, 2 * g + k],
                     x_recv.at[j, 2 * g + k], to)

    def x_on(j):
        for g, k in ((0, 0), (1, 1), (0, 1), (1, 0)):
            source = (x + NX - 1) % NX if k == 0 else (x + 1) % NX
            to = x_up if k == 0 else x_down
            arrive(w_group(j, source, g), x_send.at[j, 2 * g + k], x_recv.at[j, 2 * g + k], to)
            if g == k:
                send(w_group(j, source, g), w_group(j, source, g), x_send.at[j, 4 + g],
                     x_recv.at[j, 4 + g], to)

    def x_end(j):
        for g in (0, 1):
            arrive(w_group(j, (x + 2) % NX, g), x_send.at[j, 4 + g], x_recv.at[j, 4 + g],
                   x_up if g == 0 else x_down)

    cut_rows = count // CUTS

    def a_at(b_, h_, s_, g=None):
        rows_ = pl.ds(0, count) if g is None else pl.ds(g * cut_rows, cut_rows)
        return A.at[2 * h_ + s_, rows_, pl.ds(pl.multiple_of(b_ * depth, 128), depth)]

    def n_at(h_, s_, g):
        return N.at[h_, s_, pl.ds(g * cut_rows, cut_rows)]

    local = []
    b_lo = (1 - lo) * 2 + c

    def far_out(i, s_):
        for g in range(CUTS):
            send(n_at(1 - h, s_, g), a_at(b, h, s_, g), t_send.at[0, i, g], t_recv.at[0, i, g], h_near)

    def near_out(i, s_, g):
        send(n_at(h, s_, g), a_at(b, h, s_, g), t_send.at[1, i, g], t_recv.at[1, i, g], lo_pair)

    def own_out(i, s_):
        own = pltpu.make_async_copy(N.at[h, s_], a_at(b, h, s_), l_sem.at[i])
        own.start()
        local.append(own)
        send(N.at[h, s_], a_at(b, h, s_), s_send.at[0, i, 0], s_recv.at[0, i, 0], sibling)

    def to_sibling(ref, kind, i, g):
        send(ref, ref, s_send.at[kind, i, g], s_recv.at[kind, i, g], sibling)

    def far_on(i, s_):
        for g in range(CUTS):
            piece = a_at(b_lo, 1 - h, s_, g)
            arrive(piece, t_send.at[0, i, g], t_recv.at[0, i, g], h_near)
            send(piece, piece, t_send.at[2, i, g], t_recv.at[2, i, g], lo_pair)
            to_sibling(piece, 1, i, g)

    def last_on(i, s_):
        for kind, b_, h_ in ((1, b_lo, h), (2, b, 1 - h)):
            for g in range(CUTS):
                piece = a_at(b_, h_, s_, g)
                arrive(piece, t_send.at[kind, i, g], t_recv.at[kind, i, g], lo_pair)
                to_sibling(piece, kind + 1, i, g)

    def tokens_end():
        sib = lo * 2 + 1 - c
        sib_lo = (1 - lo) * 2 + 1 - c
        for i, s_ in ((0, s), (1, 1 - s)):
            local[i].wait()
            arrive(a_at(sib, h, s_), s_send.at[0, i, 0], s_recv.at[0, i, 0], sibling)
            for kind, b_, h_ in ((1, sib_lo, 1 - h), (2, sib_lo, h), (3, sib, 1 - h)):
                for g in range(CUTS):
                    arrive(a_at(b_, h_, s_, g), s_send.at[kind, i, g], s_recv.at[kind, i, g], sibling)

    full_depth = NB * depth

    def project(group):
        weights = [W[j].reshape(full_depth, lanes) for j in group]
        weights = weights[0] if len(group) == 1 else jnp.concatenate(weights, axis=1)

        def block(h_):
            part = A[pl.ds(2 * h_, 2)].reshape(2 * count, full_depth)
            return jnp.dot(part, weights, preferred_element_type=jnp.float32)

        far = block(1 - h).astype(jnp.bfloat16)
        for k, j in enumerate(group):
            psend[j] = far[:, k * lanes : (k + 1) * lanes].reshape(2, count, lanes)
            send(psend.at[j], precv.at[j], p_send.at[j], p_recv.at[j], h_far)
        near = block(h)
        for k, j in enumerate(group):
            J[j] = near[:, k * lanes : (k + 1) * lanes].reshape(2, count, lanes)

    queries = heads - 2
    offsets = bias[...].astype(jnp.float32).reshape(1, 2 * heads * lanes)
    offsets = jnp.where(s == 0, offsets[:, : heads * lanes], offsets[:, heads * lanes :])

    def finish(j):
        arrive(precv.at[j], p_send.at[j], p_recv.at[j], h_far)
        offset = offsets[:, j * lanes : (j + 1) * lanes]
        for s_ in (0, 1):
            full = J[j, s_] + precv[j, s_].astype(jnp.float32) + offset
            if j <= queries:
                full = full * cosine[s_] + pltpu.roll(full, lanes // 2, 1) * sine[s_]
            J[j, s_] = full.astype(jnp.bfloat16).astype(jnp.float32)

    own_lens = f // 2 * (2 * own_rows)
    two_rows = 2 * NEW
    down = lax.broadcasted_iota(jnp.int32, (two_rows, 1), 0)
    sign = jnp.where(lax.broadcasted_iota(jnp.int32, (1, lanes), 1) < lanes // 2, -1.0, 1.0)

    def tables(s_):
        @pl.loop(0, own_rows // 2)
        def _(i):
            r = own_lens + s_ * own_rows + 2 * i
            position = jnp.where(down < NEW, lengths[r], lengths[r + 1]) + down % NEW
            angle = position.astype(jnp.float32) * frequency[...]
            here = pl.ds(pl.multiple_of(i * two_rows, two_rows), two_rows)
            cosine[s_, here] = jnp.cos(angle)
            sine[s_, here] = jnp.sin(angle) * sign

    peers = ((sibling, 0), (lo_pair, 1), (cross, 2))
    for to, k in peers:
        send(ssq.at[b], ssq.at[b], q_send.at[k], q_recv.at[k], to)
    z_out(0)
    to_row = lax.broadcasted_iota(jnp.int32, (count, count), 0)
    to_col = lax.broadcasted_iota(jnp.int32, (count, count), 1)
    order = (to_col == to_row % NEW * own_rows + to_row // NEW).astype(jnp.bfloat16)
    back = (to_row == to_col % NEW * own_rows + to_col // NEW).astype(jnp.bfloat16)
    for to, k in peers:
        arrive(ssq.at[(b // 2 * 2 + 1 - c) if k == 0 else (b_lo if k == 1 else (1 - lo) * 2 + 1 - c)],
               q_send.at[k], q_recv.at[k], to)
    total = ssq[0] + ssq[1] + ssq[2] + ssq[3]
    inverse = lax.rsqrt(jnp.sum(total, axis=1, keepdims=True) * (1.0 / (NB * width)) + NORM_EPS)
    gains = gain[...].astype(jnp.float32).reshape(1, width)
    scaled = (tokens[...].astype(jnp.float32) * inverse * gains).astype(jnp.bfloat16)
    scaled = jnp.dot(order, scaled, preferred_element_type=jnp.float32).astype(jnp.bfloat16)
    N[0, s] = scaled[:, :depth]
    N[1, s] = scaled[:, depth:]
    send(N.at[1 - h, s], N.at[1 - h, s], t1_send.at[0], t1_recv.at[0], z_pair)
    far_out(0, s)
    send(N.at[h, s], N.at[h, s], t1_send.at[1], t1_recv.at[1], z_pair)
    near_out(0, s, 0)
    z_out(1)
    own_out(0, s)
    x_out(0)
    far_on(0, s)
    near_out(0, s, 1)
    z_out(2)
    x_out(1)
    x_on(0)
    arrive(N.at[1 - h, 1 - s], t1_send.at[0], t1_recv.at[0], z_pair)
    far_out(1, 1 - s)
    arrive(N.at[h, 1 - s], t1_send.at[1], t1_recv.at[1], z_pair)
    near_out(1, 1 - s, 0)
    own_out(1, 1 - s)
    z_out(3)
    last_on(0, s)
    x_out(2)
    x_on(1)
    z_out(4)
    far_on(1, 1 - s)
    near_out(1, 1 - s, 1)
    tables(0)
    x_out(3)
    x_on(2)
    z_out(5)
    tables(1)
    last_on(1, 1 - s)
    x_out(4)
    x_on(3)
    z_out(6)
    x_out(5)
    x_on(4)
    tokens_end()
    x_end(0)
    x_end(1)
    project((0, 1))
    x_out(6)
    x_on(5)
    x_end(2)
    x_end(3)
    project((2, 3))
    x_on(6)
    x_end(4)
    x_end(5)
    project((4, 5))
    for j in (0, 1, 2, 3):
        finish(j)
    x_end(6)
    project((6,))
    for j in (4, 5, 6):
        finish(j)
    lens_at = f // 2 * (2 * own_rows)

    for load in loads:
        load.wait()
    slots = keys.shape[1]
    two = 2 * NEW
    wide = -(-(2 * slots + two) // 128) * 128
    col = lax.broadcasted_iota(jnp.int32, (two, wide), 1)
    row = lax.broadcasted_iota(jnp.int32, (two, wide), 0)
    never = 1 << 20
    second = (col >= slots).astype(jnp.int32)
    place = jnp.where(second == row // NEW, col - second * slots, never)
    new = col - 2 * slots
    seen = (new // NEW == row // NEW) & (new % NEW <= row % NEW) & (new < two)
    place = jnp.where(col < 2 * slots, place, jnp.where(seen, -1, never))
    first_row = lax.broadcasted_iota(jnp.int32, (two, 1), 0) < NEW
    scale = 1.0 / math.sqrt(lanes)

    def extend(cached, fresh):
        rest = jnp.zeros((wide - 2 * slots - two, lanes), jnp.float32)
        tail = jnp.concatenate([fresh, rest], axis=0).astype(jnp.bfloat16)
        return jnp.concatenate([cached.reshape(2 * slots, lanes), tail], axis=0)

    def pair(s_, i):
        rows_here = pl.ds(pl.multiple_of(i * two, two), two)
        r = s_ * own_rows + 2 * i
        q = jnp.concatenate([J[j, s_, rows_here] for j in range(queries)], axis=0)
        k = extend(keys[pl.ds(r, 2)], J[queries, s_, rows_here])
        scores = lax.dot_general(
            q.astype(jnp.bfloat16), k, (((1,), (1,)), ((), ())),
            preferred_element_type=jnp.float32,
        ) * scale
        limit = jnp.where(first_row, lengths[lens_at + r], lengths[lens_at + r + 1])
        scores = scores.reshape(queries, two, wide)
        scores = jnp.where((place < limit)[None], scores, -jnp.inf)
        grown = jnp.exp(scores - jnp.max(scores, axis=-1, keepdims=True))
        probs = grown * (1.0 / jnp.sum(grown, axis=-1, keepdims=True))
        probs = probs.reshape(queries * two, wide).astype(jnp.bfloat16)
        v = extend(values[pl.ds(r, 2)], J[queries + 1, s_, rows_here])
        return jnp.dot(probs, v, preferred_element_type=jnp.float32)

    block_rows = AT_ONCE * two

    def attend(s_, blocks, into):
        @pl.loop(*blocks)
        def _(t):
            done = [pair(s_, t * AT_ONCE + k) for k in range(AT_ONCE)]
            for j in range(queries):
                tile = jnp.concatenate([d[j * two : (j + 1) * two] for d in done], axis=0)
                into[pl.ds(pl.multiple_of(t * block_rows, 16), block_rows),
                     j * lanes : (j + 1) * lanes] = tile.astype(jnp.bfloat16)

    blocks = count // block_rows
    cut = blocks // 2
    for k, (start, stop) in enumerate(((0, cut), (cut, blocks))):
        attend(1 - s, (start, stop), mine.at[0])
        span = pl.ds(start * block_rows, (stop - start) * block_rows)
        send(mine.at[0, span], theirs.at[span], e_send.at[k], e_recv.at[k], z_pair)
    attend(s, (0, blocks), mine.at[1])
    piece = queries * lanes
    context[:, pl.ds(pl.multiple_of(s * piece, 128), piece)] = jnp.dot(
        back, mine[1], preferred_element_type=jnp.float32
    ).astype(jnp.bfloat16)
    for k, (start, stop) in enumerate(((0, cut), (cut, blocks))):
        span = pl.ds(start * block_rows, (stop - start) * block_rows)
        arrive(theirs.at[span], e_send.at[k], e_recv.at[k], z_pair)
    context[:, pl.ds(pl.multiple_of((1 - s) * piece, 128), piece)] = jnp.dot(
        back, theirs[...], preferred_element_type=jnp.float32
    ).astype(jnp.bfloat16)
    for copy in sent:
        copy.wait_send()


def project_tokens(lengths, narrow, tokens, gain, bias, keys, values):
    twice, rows, lanes = narrow.shape
    heads = twice // 2
    count, width = tokens.shape
    depth = width // 2
    assert depth == NZ * rows
    piece = (heads - 2) * lanes
    half_lanes = lanes // 2
    frequency = ROPE_BASE ** (-(np.arange(lanes) % half_lanes) / half_lanes)
    frequency = jnp.asarray(frequency.reshape(1, lanes), jnp.float32)
    dma = pltpu.SemaphoreType.DMA
    vmem = pl.BlockSpec(memory_space=pltpu.VMEM)
    hbm = pl.BlockSpec(memory_space=pl.ANY)
    return pl.pallas_call(
        layer_kernel,
        name="gather_project",
        out_shape=jax.ShapeDtypeStruct((count, 2 * piece), jnp.bfloat16),
        in_specs=[pl.BlockSpec(memory_space=pltpu.SMEM)] + [vmem] * 5 + [hbm] * 2,
        out_specs=vmem,
        scratch_shapes=[
            pltpu.VMEM((heads, NX, depth, lanes), jnp.bfloat16),
            pltpu.VMEM((2 * NH, count, NB * depth), jnp.bfloat16),
            pltpu.VMEM((NH, 2, count, depth), jnp.bfloat16),
            pltpu.VMEM((NB, count, lanes), jnp.float32),
            pltpu.VMEM((heads, 2, count, lanes), jnp.bfloat16),
            pltpu.VMEM((heads, 2, count, lanes), jnp.bfloat16),
            pltpu.VMEM((heads, 2, count, lanes), jnp.float32),
            pltpu.VMEM((2, count, lanes), jnp.float32),
            pltpu.VMEM((2, count, lanes), jnp.float32),
            pltpu.VMEM(keys.shape, keys.dtype),
            pltpu.VMEM(values.shape, values.dtype),
            pltpu.VMEM((2, count, piece), jnp.bfloat16),
            pltpu.VMEM((count, piece), jnp.bfloat16),
            dma((heads, NZ)), dma((heads, NZ)),
            dma((heads, 6)), dma((heads, 6)),
            dma((3,)), dma((3,)),
            dma((2,)), dma((2,)),
            dma((3, 2, CUTS)), dma((3, 2, CUTS)),
            dma((2,)),
            dma((4, 2, CUTS)), dma((4, 2, CUTS)),
            dma((heads,)), dma((heads,)),
            dma((2,)), dma((2,)), dma((2,)),
        ],
        compiler_params=pltpu.CompilerParams(
            collective_id=0, has_side_effects=True, vmem_limit_bytes=48 << 20
        ),
        cost_estimate=pl.CostEstimate(
            flops=2 * 4 * count * 4 * depth * heads * lanes, bytes_accessed=12 << 20, transcendentals=0
        ),
    )(lengths, frequency, narrow, tokens, gain, bias, keys, values)


def on_device(
    weight_master,
    gradient,
    first_moment,
    second_moment,
    query_key_value_bias,
    new_tokens,
    norm_gain,
    cache_len,
    key_cache,
    value_cache,
):
    new_master, new_first, new_second = adam_update(
        weight_master, gradient, first_moment, second_moment
    )
    head_dim = key_cache.shape[-1]
    rows_here, columns = new_master.shape
    half_cols = columns // 2
    per_group = half_cols // head_dim
    narrow = new_master.astype(jnp.bfloat16).reshape(rows_here, 2 * per_group, head_dim)
    narrow = narrow.transpose(1, 0, 2)
    steps_here, own_rows, features = new_tokens.shape
    output = project_tokens(
        cache_len, narrow, new_tokens.reshape(steps_here * own_rows, features), norm_gain,
        query_key_value_bias, key_cache[0, 0], value_cache[0, 0],
    )
    output = output.reshape(steps_here, own_rows, features)
    return (new_master, new_first, new_second, output)


def solution(mesh):
    in_specs = (
        P("fsdp", "tp"),
        P("fsdp", "tp"),
        P("fsdp", "tp"),
        P("fsdp", "tp"),
        P("tp"),
        P(None, "fsdp", "tp"),
        P("tp"),
        P(),
        P("fsdp", "tp", None, None, None),
        P("fsdp", "tp", None, None, None),
    )
    out_specs = (P("fsdp", "tp"), P("fsdp", "tp"), P("fsdp", "tp"), P(None, "fsdp", "tp"))
    return jax.shard_map(
        on_device, mesh=mesh, in_specs=in_specs, out_specs=out_specs, check_vma=False
    )
```

```python
import math

import jax
import jax.numpy as jnp
import numpy as np
from jax import lax
from jax.experimental import pallas as pl
from jax.experimental.pallas import tpu as pltpu
from jax.sharding import PartitionSpec as P

BETA_ONE = 0.9
BETA_TWO = 0.95
LEARN_RATE = 0.002
ADAM_EPS = 1e-08
CORR_ONE = 1.0 - 0.9**10
CORR_TWO = 1.0 - 0.95**10
NORM_EPS = 1e-06
ROPE_BASE = 1000000.0

MESH = pl.DeviceIdType.MESH
NX, NH, NZ = 4, 2, 8
NB = 4
NEW = 4
CUTS = 2
AT_ONCE = 8


def adam_update(weight_master, gradient, first_moment, second_moment):
    new_first = BETA_ONE * first_moment + (1.0 - BETA_ONE) * gradient
    new_second = BETA_TWO * second_moment + (1.0 - BETA_TWO) * gradient * gradient
    step_size = new_first / CORR_ONE / (jnp.sqrt(new_second / CORR_TWO) + ADAM_EPS)
    return (weight_master - LEARN_RATE * step_size, new_first, new_second)


def layer_kernel(
    lengths, frequency, narrow, tokens, gain, bias, keys_in, values_in, context,
    W, A, N, R, ssq, tot, psend, precv, J, cosine, sine, keys, values, mine, theirs,
    z_send, z_recv, x_send, x_recv, q_send, q_recv,
    t1_send, t1_recv, t_send, t_recv, l_sem, s_send, s_recv, p_send, p_recv, e_send, e_recv, c_sem,
):
    heads, _, depth, lanes = W.shape
    rows = depth // NZ
    half = depth // 2
    f = lax.axis_index("fsdp")
    b = lax.axis_index("tp")
    x, h, z = f // (NH * NZ), (f // NZ) % NH, f % NZ
    lo, c = b // 2, b % 2
    s = z % 2

    def at(x_, h_, z_, lo_, c_):
        return {"fsdp": (x_ * NH + h_) * NZ + z_, "tp": lo_ * 2 + c_}

    x_up = at((x + 1) % NX, h, z, lo, c)
    x_down = at((x + NX - 1) % NX, h, z, lo, c)
    z_to = [at(x, h, (z + d) % NZ, lo, c) for d in range(NZ)]
    z_pair = at(x, h, z + 1 - 2 * s, lo, c)
    lo_pair = at(x, h, z, 1 - lo, c)
    sibling = at(x, h, z, lo, 1 - c)
    cross = at(x, h, z, 1 - lo, 1 - c)
    h_far = at(x, 1 - h, z, lo, c)
    h_near = at(x, 1 - h, z, 1 - lo, c)

    barrier = pltpu.get_barrier_semaphore()
    everyone = [x_up, x_down, lo_pair, sibling, cross, h_far, h_near] + z_to[1:]
    for other in everyone:
        pl.semaphore_signal(barrier, inc=1, device_id=other, device_id_type=MESH)

    loads = [
        pltpu.make_async_copy(keys_in, keys, c_sem.at[0]),
        pltpu.make_async_copy(values_in, values, c_sem.at[1]),
    ]
    for load in loads:
        load.start()

    count, width = tokens.shape
    own_rows = count // NEW
    flat = tokens[...].astype(jnp.float32)
    square = flat * flat
    part = square[:, :lanes]
    for k in range(1, square.shape[1] // lanes):
        part = part + square[:, k * lanes : (k + 1) * lanes]
    padded = ssq.shape[2]
    part = jnp.concatenate([part, jnp.zeros((padded - count, lanes), jnp.float32)], axis=0)
    ssq[b] = jnp.broadcast_to(jnp.sum(part.T, axis=0, keepdims=True), (8, padded))
    pl.semaphore_wait(barrier, len(everyone))

    sent = []

    def send(src, dst, send_sem, recv_sem, to):
        copy = pltpu.make_async_remote_copy(
            src_ref=src, dst_ref=dst, send_sem=send_sem, recv_sem=recv_sem,
            device_id=to, device_id_type=MESH,
        )
        copy.start()
        sent.append(copy)

    def arrive(dst, send_sem, recv_sem, to):
        pltpu.make_async_remote_copy(
            src_ref=dst, dst_ref=dst, send_sem=send_sem, recv_sem=recv_sem,
            device_id=to, device_id_type=MESH,
        ).wait_recv()

    def w_rows(j, x_, z_):
        return W.at[j, x_, pl.ds(pl.multiple_of(z_ * rows, 16), rows)]

    def w_group(j, x_, g):
        return W.at[j, x_, pl.ds(g * half, half)]

    own_copies = {}

    def z_out(j):
        own = pltpu.make_async_copy(narrow.at[s * heads + j], w_rows(j, x, z), z_recv.at[j, 0])
        own.start()
        own_copies[j] = own
        for d in (4, 3, 5, 2, 6, 1, 7):
            parity = (s + d) % 2
            send(narrow.at[parity * heads + j], w_rows(j, x, z), z_send.at[j, d],
                 z_recv.at[j, d], z_to[d])

    def x_out(j):
        own_copies[j].wait()
        for d in range(1, NZ):
            arrive(w_rows(j, x, (z + NZ - d) % NZ), z_send.at[j, d], z_recv.at[j, d], z_to[d])
        for g in (0, 1):
            for k, to in ((0, x_up), (1, x_down)):
                send(w_group(j, x, g), w_group(j, x, g), x_send.at[j, 2 * g + k],
                     x_recv.at[j, 2 * g + k], to)

    def x_on(j):
        for g, k in ((0, 0), (1, 1), (0, 1), (1, 0)):
            source = (x + NX - 1) % NX if k == 0 else (x + 1) % NX
            to = x_up if k == 0 else x_down
            arrive(w_group(j, source, g), x_send.at[j, 2 * g + k], x_recv.at[j, 2 * g + k], to)
            if g == k:
                send(w_group(j, source, g), w_group(j, source, g), x_send.at[j, 4 + g],
                     x_recv.at[j, 4 + g], to)

    def x_end(j):
        for g in (0, 1):
            arrive(w_group(j, (x + 2) % NX, g), x_send.at[j, 4 + g], x_recv.at[j, 4 + g],
                   x_up if g == 0 else x_down)

    cut_rows = count // CUTS

    def a_at(b_, h_, s_, g=None):
        rows_ = pl.ds(0, count) if g is None else pl.ds(g * cut_rows, cut_rows)
        return A.at[2 * h_ + s_, rows_, pl.ds(pl.multiple_of(b_ * depth, 128), depth)]

    def n_at(h_, s_, g):
        return N.at[h_, s_, pl.ds(g * cut_rows, cut_rows)]

    local = []
    b_lo = (1 - lo) * 2 + c

    def far_out(i, s_):
        for g in range(CUTS):
            send(n_at(1 - h, s_, g), a_at(b, h, s_, g), t_send.at[0, i, g], t_recv.at[0, i, g], h_near)

    def near_out(i, s_, g):
        send(n_at(h, s_, g), a_at(b, h, s_, g), t_send.at[1, i, g], t_recv.at[1, i, g], lo_pair)

    def own_out(i, s_):
        own = pltpu.make_async_copy(N.at[h, s_], a_at(b, h, s_), l_sem.at[i])
        own.start()
        local.append(own)
        send(N.at[h, s_], a_at(b, h, s_), s_send.at[0, i, 0], s_recv.at[0, i, 0], sibling)

    def to_sibling(ref, kind, i, g):
        send(ref, ref, s_send.at[kind, i, g], s_recv.at[kind, i, g], sibling)

    def far_on(i, s_):
        for g in range(CUTS):
            piece = a_at(b_lo, 1 - h, s_, g)
            arrive(piece, t_send.at[0, i, g], t_recv.at[0, i, g], h_near)
            send(piece, piece, t_send.at[2, i, g], t_recv.at[2, i, g], lo_pair)
            to_sibling(piece, 1, i, g)

    def last_on(i, s_):
        for kind, b_, h_ in ((1, b_lo, h), (2, b, 1 - h)):
            for g in range(CUTS):
                piece = a_at(b_, h_, s_, g)
                arrive(piece, t_send.at[kind, i, g], t_recv.at[kind, i, g], lo_pair)
                to_sibling(piece, kind + 1, i, g)

    def tokens_end():
        sib = lo * 2 + 1 - c
        sib_lo = (1 - lo) * 2 + 1 - c
        for i, s_ in ((0, s), (1, 1 - s)):
            local[i].wait()
            arrive(a_at(sib, h, s_), s_send.at[0, i, 0], s_recv.at[0, i, 0], sibling)
            for kind, b_, h_ in ((1, sib_lo, 1 - h), (2, sib_lo, h), (3, sib, 1 - h)):
                for g in range(CUTS):
                    arrive(a_at(b_, h_, s_, g), s_send.at[kind, i, g], s_recv.at[kind, i, g], sibling)

    full_depth = NB * depth

    def project(group):
        weights = [W[j].reshape(full_depth, lanes) for j in group]
        weights = weights[0] if len(group) == 1 else jnp.concatenate(weights, axis=1)

        def block(h_):
            part = A[pl.ds(2 * h_, 2)].reshape(2 * count, full_depth)
            return jnp.dot(part, weights, preferred_element_type=jnp.float32)

        far = block(1 - h).astype(jnp.bfloat16)
        for k, j in enumerate(group):
            psend[j] = far[:, k * lanes : (k + 1) * lanes].reshape(2, count, lanes)
            send(psend.at[j], precv.at[j], p_send.at[j], p_recv.at[j], h_far)
        near = block(h)
        for k, j in enumerate(group):
            J[j] = near[:, k * lanes : (k + 1) * lanes].reshape(2, count, lanes)

    queries = heads - 2
    offsets = bias[...].astype(jnp.float32).reshape(1, 2 * heads * lanes)
    offsets = jnp.where(s == 0, offsets[:, : heads * lanes], offsets[:, heads * lanes :])

    def finish(j):
        arrive(precv.at[j], p_send.at[j], p_recv.at[j], h_far)
        offset = offsets[:, j * lanes : (j + 1) * lanes]
        for s_ in (0, 1):
            full = J[j, s_] + precv[j, s_].astype(jnp.float32) + offset
            if j <= queries:
                full = full * cosine[s_] + pltpu.roll(full, lanes // 2, 1) * sine[s_]
            J[j, s_] = full.astype(jnp.bfloat16).astype(jnp.float32)

    own_lens = f // 2 * (2 * own_rows)
    two_rows = 2 * NEW
    down = lax.broadcasted_iota(jnp.int32, (two_rows, 1), 0)
    sign = jnp.where(lax.broadcasted_iota(jnp.int32, (1, lanes), 1) < lanes // 2, -1.0, 1.0)

    def tables(s_):
        @pl.loop(0, own_rows // 2)
        def _(i):
            r = own_lens + s_ * own_rows + 2 * i
            position = jnp.where(down < NEW, lengths[r], lengths[r + 1]) + down % NEW
            angle = position.astype(jnp.float32) * frequency[...]
            here = pl.ds(pl.multiple_of(i * two_rows, two_rows), two_rows)
            cosine[s_, here] = jnp.cos(angle)
            sine[s_, here] = jnp.sin(angle) * sign

    peers = ((sibling, 0), (lo_pair, 1), (cross, 2))
    for to, k in peers:
        send(ssq.at[b], ssq.at[b], q_send.at[k], q_recv.at[k], to)
    z_out(0)
    for k, h_ in ((0, 1 - h), (1, h)):
        raw = tokens.at[:, pl.ds(pl.multiple_of(h_ * depth, 128), depth)]
        send(raw, R.at[h_], t1_send.at[k], t1_recv.at[k], z_pair)
    to_row = lax.broadcasted_iota(jnp.int32, (count, count), 0)
    to_col = lax.broadcasted_iota(jnp.int32, (count, count), 1)
    order = (to_col == to_row % NEW * own_rows + to_row // NEW).astype(jnp.bfloat16)
    back = (to_row == to_col % NEW * own_rows + to_col // NEW).astype(jnp.bfloat16)
    for to, k in peers:
        arrive(ssq.at[(b // 2 * 2 + 1 - c) if k == 0 else (b_lo if k == 1 else (1 - lo) * 2 + 1 - c)],
               q_send.at[k], q_recv.at[k], to)
    tot[0] = ssq[0] + ssq[1] + ssq[2] + ssq[3]
    send(tot.at[0], tot.at[1], t1_send.at[2], t1_recv.at[2], z_pair)

    def inverse_of(total):
        inverse = lax.rsqrt(total * (1.0 / (NB * width)) + NORM_EPS)
        return inverse.T[:count, :1]

    gains = gain[...].astype(jnp.float32).reshape(1, width)

    def normalise(raw, inverse, gains_here):
        scaled = (raw.astype(jnp.float32) * inverse * gains_here).astype(jnp.bfloat16)
        return jnp.dot(order, scaled, preferred_element_type=jnp.float32).astype(jnp.bfloat16)

    inverse = inverse_of(tot[0])
    N[0, s] = normalise(tokens[:, :depth], inverse, gains[:, :depth])
    N[1, s] = normalise(tokens[:, depth:], inverse, gains[:, depth:])
    far_out(0, s)
    near_out(0, s, 0)
    own_out(0, s)
    x_out(0)
    z_out(1)
    far_on(0, s)
    near_out(0, s, 1)
    arrive(tot.at[1], t1_send.at[2], t1_recv.at[2], z_pair)
    inverse = inverse_of(tot[1])
    gains_near = jnp.where(h == 0, gains[:, :depth], gains[:, depth:])
    gains_far = jnp.where(h == 0, gains[:, depth:], gains[:, :depth])
    arrive(R.at[1 - h], t1_send.at[0], t1_recv.at[0], z_pair)
    N[1 - h, 1 - s] = normalise(R[1 - h], inverse, gains_far)
    far_out(1, 1 - s)
    x_out(1)
    x_on(0)
    z_out(2)
    arrive(R.at[h], t1_send.at[1], t1_recv.at[1], z_pair)
    N[h, 1 - s] = normalise(R[h], inverse, gains_near)
    near_out(1, 1 - s, 0)
    own_out(1, 1 - s)
    z_out(3)
    last_on(0, s)
    x_out(2)
    x_on(1)
    z_out(4)
    far_on(1, 1 - s)
    near_out(1, 1 - s, 1)
    tables(0)
    x_out(3)
    x_on(2)
    z_out(5)
    tables(1)
    last_on(1, 1 - s)
    x_out(4)
    x_on(3)
    z_out(6)
    x_out(5)
    x_on(4)
    tokens_end()
    x_out(6)
    x_end(0)
    x_end(1)
    project((0, 1))
    x_on(5)
    x_end(2)
    x_end(3)
    project((2, 3))
    x_on(6)
    x_end(4)
    x_end(5)
    project((4, 5))
    for j in (0, 1, 2, 3):
        finish(j)
    x_end(6)
    project((6,))
    for j in (4, 5, 6):
        finish(j)
    lens_at = f // 2 * (2 * own_rows)

    for load in loads:
        load.wait()
    slots = keys.shape[1]
    two = 2 * NEW
    wide = -(-(2 * slots + two) // 128) * 128
    col = lax.broadcasted_iota(jnp.int32, (two, wide), 1)
    row = lax.broadcasted_iota(jnp.int32, (two, wide), 0)
    never = 1 << 20
    second = (col >= slots).astype(jnp.int32)
    place = jnp.where(second == row // NEW, col - second * slots, never)
    new = col - 2 * slots
    seen = (new // NEW == row // NEW) & (new % NEW <= row % NEW) & (new < two)
    place = jnp.where(col < 2 * slots, place, jnp.where(seen, -1, never))
    first_row = lax.broadcasted_iota(jnp.int32, (two, 1), 0) < NEW
    scale = 1.0 / math.sqrt(lanes)

    def extend(cached, fresh):
        rest = jnp.zeros((wide - 2 * slots - two, lanes), jnp.float32)
        tail = jnp.concatenate([fresh, rest], axis=0).astype(jnp.bfloat16)
        return jnp.concatenate([cached.reshape(2 * slots, lanes), tail], axis=0)

    def pair(s_, i):
        rows_here = pl.ds(pl.multiple_of(i * two, two), two)
        r = s_ * own_rows + 2 * i
        q = jnp.concatenate([J[j, s_, rows_here] for j in range(queries)], axis=0)
        k = extend(keys[pl.ds(r, 2)], J[queries, s_, rows_here])
        scores = lax.dot_general(
            q.astype(jnp.bfloat16), k, (((1,), (1,)), ((), ())),
            preferred_element_type=jnp.float32,
        ) * scale
        limit = jnp.where(first_row, lengths[lens_at + r], lengths[lens_at + r + 1])
        scores = scores.reshape(queries, two, wide)
        scores = jnp.where((place < limit)[None], scores, -jnp.inf)
        grown = jnp.exp(scores - jnp.max(scores, axis=-1, keepdims=True))
        probs = grown * (1.0 / jnp.sum(grown, axis=-1, keepdims=True))
        probs = probs.reshape(queries * two, wide).astype(jnp.bfloat16)
        v = extend(values[pl.ds(r, 2)], J[queries + 1, s_, rows_here])
        return jnp.dot(probs, v, preferred_element_type=jnp.float32)

    block_rows = AT_ONCE * two

    def attend(s_, blocks, into):
        @pl.loop(*blocks)
        def _(t):
            done = [pair(s_, t * AT_ONCE + k) for k in range(AT_ONCE)]
            for j in range(queries):
                tile = jnp.concatenate([d[j * two : (j + 1) * two] for d in done], axis=0)
                into[pl.ds(pl.multiple_of(t * block_rows, 16), block_rows),
                     j * lanes : (j + 1) * lanes] = tile.astype(jnp.bfloat16)

    blocks = count // block_rows
    cut = blocks // 2
    for k, (start, stop) in enumerate(((0, cut), (cut, blocks))):
        attend(1 - s, (start, stop), mine.at[0])
        span = pl.ds(start * block_rows, (stop - start) * block_rows)
        send(mine.at[0, span], theirs.at[span], e_send.at[k], e_recv.at[k], z_pair)
    attend(s, (0, blocks), mine.at[1])
    piece = queries * lanes
    context[:, pl.ds(pl.multiple_of(s * piece, 128), piece)] = jnp.dot(
        back, mine[1], preferred_element_type=jnp.float32
    ).astype(jnp.bfloat16)
    for k, (start, stop) in enumerate(((0, cut), (cut, blocks))):
        span = pl.ds(start * block_rows, (stop - start) * block_rows)
        arrive(theirs.at[span], e_send.at[k], e_recv.at[k], z_pair)
    context[:, pl.ds(pl.multiple_of((1 - s) * piece, 128), piece)] = jnp.dot(
        back, theirs[...], preferred_element_type=jnp.float32
    ).astype(jnp.bfloat16)
    for copy in sent:
        copy.wait_send()


def project_tokens(lengths, narrow, tokens, gain, bias, keys, values):
    twice, rows, lanes = narrow.shape
    heads = twice // 2
    count, width = tokens.shape
    depth = width // 2
    assert depth == NZ * rows
    piece = (heads - 2) * lanes
    half_lanes = lanes // 2
    padded = -(-count // 128) * 128
    frequency = ROPE_BASE ** (-(np.arange(lanes) % half_lanes) / half_lanes)
    frequency = jnp.asarray(frequency.reshape(1, lanes), jnp.float32)
    dma = pltpu.SemaphoreType.DMA
    vmem = pl.BlockSpec(memory_space=pltpu.VMEM)
    hbm = pl.BlockSpec(memory_space=pl.ANY)
    return pl.pallas_call(
        layer_kernel,
        name="gather_project",
        out_shape=jax.ShapeDtypeStruct((count, 2 * piece), jnp.bfloat16),
        in_specs=[pl.BlockSpec(memory_space=pltpu.SMEM)] + [vmem] * 5 + [hbm] * 2,
        out_specs=vmem,
        scratch_shapes=[
            pltpu.VMEM((heads, NX, depth, lanes), jnp.bfloat16),
            pltpu.VMEM((2 * NH, count, NB * depth), jnp.bfloat16),
            pltpu.VMEM((NH, 2, count, depth), jnp.bfloat16),
            pltpu.VMEM((NH, count, depth), jnp.bfloat16),
            pltpu.VMEM((NB, 8, padded), jnp.float32),
            pltpu.VMEM((2, 8, padded), jnp.float32),
            pltpu.VMEM((heads, 2, count, lanes), jnp.bfloat16),
            pltpu.VMEM((heads, 2, count, lanes), jnp.bfloat16),
            pltpu.VMEM((heads, 2, count, lanes), jnp.float32),
            pltpu.VMEM((2, count, lanes), jnp.float32),
            pltpu.VMEM((2, count, lanes), jnp.float32),
            pltpu.VMEM(keys.shape, keys.dtype),
            pltpu.VMEM(values.shape, values.dtype),
            pltpu.VMEM((2, count, piece), jnp.bfloat16),
            pltpu.VMEM((count, piece), jnp.bfloat16),
            dma((heads, NZ)), dma((heads, NZ)),
            dma((heads, 6)), dma((heads, 6)),
            dma((3,)), dma((3,)),
            dma((3,)), dma((3,)),
            dma((3, 2, CUTS)), dma((3, 2, CUTS)),
            dma((2,)),
            dma((4, 2, CUTS)), dma((4, 2, CUTS)),
            dma((heads,)), dma((heads,)),
            dma((2,)), dma((2,)), dma((2,)),
        ],
        compiler_params=pltpu.CompilerParams(
            collective_id=0, has_side_effects=True, vmem_limit_bytes=48 << 20
        ),
        cost_estimate=pl.CostEstimate(
            flops=2 * 4 * count * 4 * depth * heads * lanes, bytes_accessed=12 << 20, transcendentals=0
        ),
    )(lengths, frequency, narrow, tokens, gain, bias, keys, values)


def on_device(
    weight_master,
    gradient,
    first_moment,
    second_moment,
    query_key_value_bias,
    new_tokens,
    norm_gain,
    cache_len,
    key_cache,
    value_cache,
):
    new_master, new_first, new_second = adam_update(
        weight_master, gradient, first_moment, second_moment
    )
    head_dim = key_cache.shape[-1]
    rows_here, columns = new_master.shape
    half_cols = columns // 2
    per_group = half_cols // head_dim
    narrow = new_master.astype(jnp.bfloat16).reshape(rows_here, 2 * per_group, head_dim)
    narrow = narrow.transpose(1, 0, 2)
    steps_here, own_rows, features = new_tokens.shape
    output = project_tokens(
        cache_len, narrow, new_tokens.reshape(steps_here * own_rows, features), norm_gain,
        query_key_value_bias, key_cache[0, 0], value_cache[0, 0],
    )
    output = output.reshape(steps_here, own_rows, features)
    return (new_master, new_first, new_second, output)


def solution(mesh):
    in_specs = (
        P("fsdp", "tp"),
        P("fsdp", "tp"),
        P("fsdp", "tp"),
        P("fsdp", "tp"),
        P("tp"),
        P(None, "fsdp", "tp"),
        P("tp"),
        P(),
        P("fsdp", "tp", None, None, None),
        P("fsdp", "tp", None, None, None),
    )
    out_specs = (P("fsdp", "tp"), P("fsdp", "tp"), P("fsdp", "tp"), P(None, "fsdp", "tp"))
    return jax.shard_map(
        on_device, mesh=mesh, in_specs=in_specs, out_specs=out_specs, check_vma=False
    )
```

```python
import math

import jax
import jax.numpy as jnp
import numpy as np
from jax import lax
from jax.experimental import pallas as pl
from jax.experimental.pallas import tpu as pltpu
from jax.sharding import PartitionSpec as P

BETA_ONE = 0.9
BETA_TWO = 0.95
LEARN_RATE = 0.002
ADAM_EPS = 1e-08
CORR_ONE = 1.0 - 0.9**10
CORR_TWO = 1.0 - 0.95**10
NORM_EPS = 1e-06
ROPE_BASE = 1000000.0

MESH = pl.DeviceIdType.MESH
NX, NH, NZ = 4, 2, 8
NB = 4
NEW = 4
CUTS = 2
AT_ONCE = 8


def adam_update(weight_master, gradient, first_moment, second_moment):
    new_first = BETA_ONE * first_moment + (1.0 - BETA_ONE) * gradient
    new_second = BETA_TWO * second_moment + (1.0 - BETA_TWO) * gradient * gradient
    step_size = new_first / CORR_ONE / (jnp.sqrt(new_second / CORR_TWO) + ADAM_EPS)
    return (weight_master - LEARN_RATE * step_size, new_first, new_second)


def layer_kernel(
    lengths, frequency, narrow, tokens, gain, bias, keys_in, values_in, context,
    W, A, N, R, ssq, tot, psend, precv, J, cosine, sine, keys, values, mine, theirs,
    z_send, z_recv, x_send, x_recv, q_send, q_recv,
    t1_send, t1_recv, t_send, t_recv, l_sem, s_send, s_recv, p_send, p_recv, e_send, e_recv, c_sem,
):
    heads, _, depth, lanes = W.shape
    rows = depth // NZ
    half = depth // 2
    f = lax.axis_index("fsdp")
    b = lax.axis_index("tp")
    x, h, z = f // (NH * NZ), (f // NZ) % NH, f % NZ
    lo, c = b // 2, b % 2
    s = z % 2

    def at(x_, h_, z_, lo_, c_):
        return {"fsdp": (x_ * NH + h_) * NZ + z_, "tp": lo_ * 2 + c_}

    x_up = at((x + 1) % NX, h, z, lo, c)
    x_down = at((x + NX - 1) % NX, h, z, lo, c)
    z_to = [at(x, h, (z + d) % NZ, lo, c) for d in range(NZ)]
    z_pair = at(x, h, z + 1 - 2 * s, lo, c)
    lo_pair = at(x, h, z, 1 - lo, c)
    sibling = at(x, h, z, lo, 1 - c)
    cross = at(x, h, z, 1 - lo, 1 - c)
    h_far = at(x, 1 - h, z, lo, c)
    h_near = at(x, 1 - h, z, 1 - lo, c)

    barrier = pltpu.get_barrier_semaphore()
    everyone = [x_up, x_down, lo_pair, sibling, cross, h_far, h_near] + z_to[1:]
    for other in everyone:
        pl.semaphore_signal(barrier, inc=1, device_id=other, device_id_type=MESH)

    loads = [
        pltpu.make_async_copy(keys_in, keys, c_sem.at[0]),
        pltpu.make_async_copy(values_in, values, c_sem.at[1]),
    ]
    for load in loads:
        load.start()

    count, width = tokens.shape
    own_rows = count // NEW
    flat = tokens[...].astype(jnp.float32)
    square = flat * flat
    part = square[:, :lanes]
    for k in range(1, square.shape[1] // lanes):
        part = part + square[:, k * lanes : (k + 1) * lanes]
    padded = ssq.shape[2]
    part = jnp.concatenate([part, jnp.zeros((padded - count, lanes), jnp.float32)], axis=0)
    ssq[b] = jnp.broadcast_to(jnp.sum(part.T, axis=0, keepdims=True), (8, padded))
    pl.semaphore_wait(barrier, len(everyone))

    sent = []

    def send(src, dst, send_sem, recv_sem, to):
        copy = pltpu.make_async_remote_copy(
            src_ref=src, dst_ref=dst, send_sem=send_sem, recv_sem=recv_sem,
            device_id=to, device_id_type=MESH,
        )
        copy.start()
        sent.append(copy)

    def arrive(dst, send_sem, recv_sem, to):
        pltpu.make_async_remote_copy(
            src_ref=dst, dst_ref=dst, send_sem=send_sem, recv_sem=recv_sem,
            device_id=to, device_id_type=MESH,
        ).wait_recv()

    def w_rows(j, x_, z_):
        return W.at[j, x_, pl.ds(pl.multiple_of(z_ * rows, 16), rows)]

    def w_group(j, x_, g):
        return W.at[j, x_, pl.ds(g * half, half)]

    own_copies = {}

    def z_out(j):
        own = pltpu.make_async_copy(narrow.at[s * heads + j], w_rows(j, x, z), z_recv.at[j, 0])
        own.start()
        own_copies[j] = own
        for d in (4, 3, 5, 2, 6, 1, 7):
            parity = (s + d) % 2
            send(narrow.at[parity * heads + j], w_rows(j, x, z), z_send.at[j, d],
                 z_recv.at[j, d], z_to[d])

    def x_out(j):
        own_copies[j].wait()
        for d in range(1, NZ):
            arrive(w_rows(j, x, (z + NZ - d) % NZ), z_send.at[j, d], z_recv.at[j, d], z_to[d])
        for g in (0, 1):
            for k, to in ((0, x_up), (1, x_down)):
                send(w_group(j, x, g), w_group(j, x, g), x_send.at[j, 2 * g + k],
                     x_recv.at[j, 2 * g + k], to)

    def x_on(j):
        for g, k in ((0, 0), (1, 1), (0, 1), (1, 0)):
            source = (x + NX - 1) % NX if k == 0 else (x + 1) % NX
            to = x_up if k == 0 else x_down
            arrive(w_group(j, source, g), x_send.at[j, 2 * g + k], x_recv.at[j, 2 * g + k], to)
            if g == k:
                send(w_group(j, source, g), w_group(j, source, g), x_send.at[j, 4 + g],
                     x_recv.at[j, 4 + g], to)

    def x_end(j):
        for g in (0, 1):
            arrive(w_group(j, (x + 2) % NX, g), x_send.at[j, 4 + g], x_recv.at[j, 4 + g],
                   x_up if g == 0 else x_down)

    cut_rows = count // CUTS

    def a_at(b_, h_, s_, g=None):
        rows_ = pl.ds(0, count) if g is None else pl.ds(g * cut_rows, cut_rows)
        return A.at[b_, 2 * h_ + s_, rows_]

    def n_at(h_, s_, g):
        return N.at[h_, s_, pl.ds(g * cut_rows, cut_rows)]

    local = []
    b_lo = (1 - lo) * 2 + c

    def far_out(i, s_):
        for g in range(CUTS):
            send(n_at(1 - h, s_, g), a_at(b, h, s_, g), t_send.at[0, i, g], t_recv.at[0, i, g], h_near)

    def near_out(i, s_, g):
        send(n_at(h, s_, g), a_at(b, h, s_, g), t_send.at[1, i, g], t_recv.at[1, i, g], lo_pair)

    def own_out(i, s_):
        own = pltpu.make_async_copy(N.at[h, s_], a_at(b, h, s_), l_sem.at[i])
        own.start()
        local.append(own)
        send(N.at[h, s_], a_at(b, h, s_), s_send.at[0, i, 0], s_recv.at[0, i, 0], sibling)

    def to_sibling(ref, kind, i, g):
        send(ref, ref, s_send.at[kind, i, g], s_recv.at[kind, i, g], sibling)

    def far_on(i, s_):
        for g in range(CUTS):
            piece = a_at(b_lo, 1 - h, s_, g)
            arrive(piece, t_send.at[0, i, g], t_recv.at[0, i, g], h_near)
            send(piece, piece, t_send.at[2, i, g], t_recv.at[2, i, g], lo_pair)
            to_sibling(piece, 1, i, g)

    def last_on(i, s_):
        for kind, b_, h_ in ((1, b_lo, h), (2, b, 1 - h)):
            for g in range(CUTS):
                piece = a_at(b_, h_, s_, g)
                arrive(piece, t_send.at[kind, i, g], t_recv.at[kind, i, g], lo_pair)
                to_sibling(piece, kind + 1, i, g)

    def tokens_end():
        sib = lo * 2 + 1 - c
        sib_lo = (1 - lo) * 2 + 1 - c
        for i, s_ in ((0, s), (1, 1 - s)):
            local[i].wait()
            arrive(a_at(sib, h, s_), s_send.at[0, i, 0], s_recv.at[0, i, 0], sibling)
            for kind, b_, h_ in ((1, sib_lo, 1 - h), (2, sib_lo, h), (3, sib, 1 - h)):
                for g in range(CUTS):
                    arrive(a_at(b_, h_, s_, g), s_send.at[kind, i, g], s_recv.at[kind, i, g], sibling)

    def project(group):
        weights = [W[j].reshape(NB * depth, lanes) for j in group]
        weights = weights[0] if len(group) == 1 else jnp.concatenate(weights, axis=1)

        def block(h_):
            total = None
            for b_ in range(NB):
                part = A[b_, pl.ds(2 * h_, 2)].reshape(2 * count, depth)
                term = jnp.dot(part, weights[b_ * depth : (b_ + 1) * depth], preferred_element_type=jnp.float32)
                total = term if total is None else total + term
            return total

        far = block(1 - h).astype(jnp.bfloat16)
        for k, j in enumerate(group):
            psend[j] = far[:, k * lanes : (k + 1) * lanes].reshape(2, count, lanes)
            send(psend.at[j], precv.at[j], p_send.at[j], p_recv.at[j], h_far)
        near = block(h)
        for k, j in enumerate(group):
            J[j] = near[:, k * lanes : (k + 1) * lanes].reshape(2, count, lanes)

    queries = heads - 2
    offsets = bias[...].astype(jnp.float32).reshape(1, 2 * heads * lanes)
    offsets = jnp.where(s == 0, offsets[:, : heads * lanes], offsets[:, heads * lanes :])

    def finish(j):
        arrive(precv.at[j], p_send.at[j], p_recv.at[j], h_far)
        offset = offsets[:, j * lanes : (j + 1) * lanes]
        for s_ in (0, 1):
            full = J[j, s_] + precv[j, s_].astype(jnp.float32) + offset
            if j <= queries:
                full = full * cosine[s_] + pltpu.roll(full, lanes // 2, 1) * sine[s_]
            J[j, s_] = full.astype(jnp.bfloat16).astype(jnp.float32)

    own_lens = f // 2 * (2 * own_rows)
    two_rows = 2 * NEW
    down = lax.broadcasted_iota(jnp.int32, (two_rows, 1), 0)
    sign = jnp.where(lax.broadcasted_iota(jnp.int32, (1, lanes), 1) < lanes // 2, -1.0, 1.0)

    def tables(s_):
        @pl.loop(0, own_rows // 2)
        def _(i):
            r = own_lens + s_ * own_rows + 2 * i
            position = jnp.where(down < NEW, lengths[r], lengths[r + 1]) + down % NEW
            angle = position.astype(jnp.float32) * frequency[...]
            here = pl.ds(pl.multiple_of(i * two_rows, two_rows), two_rows)
            cosine[s_, here] = jnp.cos(angle)
            sine[s_, here] = jnp.sin(angle) * sign

    peers = ((sibling, 0), (lo_pair, 1), (cross, 2))
    for to, k in peers:
        send(ssq.at[b], ssq.at[b], q_send.at[k], q_recv.at[k], to)
    z_out(0)
    for k, h_ in ((0, 1 - h), (1, h)):
        raw = tokens.at[:, pl.ds(pl.multiple_of(h_ * depth, 128), depth)]
        send(raw, R.at[h_], t1_send.at[k], t1_recv.at[k], z_pair)
    to_row = lax.broadcasted_iota(jnp.int32, (count, count), 0)
    to_col = lax.broadcasted_iota(jnp.int32, (count, count), 1)
    order = (to_col == to_row % NEW * own_rows + to_row // NEW).astype(jnp.bfloat16)
    back = (to_row == to_col % NEW * own_rows + to_col // NEW).astype(jnp.bfloat16)
    for to, k in peers:
        arrive(ssq.at[(b // 2 * 2 + 1 - c) if k == 0 else (b_lo if k == 1 else (1 - lo) * 2 + 1 - c)],
               q_send.at[k], q_recv.at[k], to)
    tot[0] = ssq[0] + ssq[1] + ssq[2] + ssq[3]
    send(tot.at[0], tot.at[1], t1_send.at[2], t1_recv.at[2], z_pair)

    def inverse_of(total):
        inverse = lax.rsqrt(total * (1.0 / (NB * width)) + NORM_EPS)
        return inverse.T[:count, :1]

    gains = gain[...].astype(jnp.float32).reshape(1, width)

    def normalise(raw, inverse, gains_here):
        scaled = (raw.astype(jnp.float32) * inverse * gains_here).astype(jnp.bfloat16)
        return jnp.dot(order, scaled, preferred_element_type=jnp.float32).astype(jnp.bfloat16)

    inverse = inverse_of(tot[0])
    gains_near = jnp.where(h == 0, gains[:, :depth], gains[:, depth:])
    gains_far = jnp.where(h == 0, gains[:, depth:], gains[:, :depth])

    def half_of(h_):
        return tokens[:, pl.ds(pl.multiple_of(h_ * depth, 128), depth)]

    N[1 - h, s] = normalise(half_of(1 - h), inverse, gains_far)
    far_out(0, s)
    N[h, s] = normalise(half_of(h), inverse, gains_near)
    near_out(0, s, 0)
    own_out(0, s)
    z_out(1)
    x_out(0)
    far_on(0, s)
    near_out(0, s, 1)
    z_out(2)
    x_out(1)
    arrive(tot.at[1], t1_send.at[2], t1_recv.at[2], z_pair)
    inverse = inverse_of(tot[1])
    arrive(R.at[1 - h], t1_send.at[0], t1_recv.at[0], z_pair)
    N[1 - h, 1 - s] = normalise(R[1 - h], inverse, gains_far)
    far_out(1, 1 - s)
    z_out(3)
    arrive(R.at[h], t1_send.at[1], t1_recv.at[1], z_pair)
    N[h, 1 - s] = normalise(R[h], inverse, gains_near)
    near_out(1, 1 - s, 0)
    own_out(1, 1 - s)
    x_on(0)
    x_out(2)
    last_on(0, s)
    z_out(4)
    far_on(1, 1 - s)
    near_out(1, 1 - s, 1)
    x_on(1)
    x_out(3)
    z_out(5)
    tables(0)
    x_on(2)
    x_out(4)
    z_out(6)
    last_on(1, 1 - s)
    x_on(3)
    x_out(5)
    tables(1)
    x_on(4)
    x_out(6)
    tokens_end()
    x_end(0)
    x_end(1)
    project((0, 1))
    x_end(2)
    x_end(3)
    project((2, 3))
    x_on(5)
    finish(0)
    finish(1)
    x_on(6)
    x_end(4)
    x_end(5)
    project((4, 5))
    finish(2)
    finish(3)
    x_end(6)
    project((6,))
    finish(4)
    finish(5)
    finish(6)
    lens_at = f // 2 * (2 * own_rows)

    for load in loads:
        load.wait()
    slots = keys.shape[1]
    two = 2 * NEW
    wide = -(-(2 * slots + two) // 128) * 128
    col = lax.broadcasted_iota(jnp.int32, (two, wide), 1)
    row = lax.broadcasted_iota(jnp.int32, (two, wide), 0)
    never = 1 << 20
    second = (col >= slots).astype(jnp.int32)
    place = jnp.where(second == row // NEW, col - second * slots, never)
    new = col - 2 * slots
    seen = (new // NEW == row // NEW) & (new % NEW <= row % NEW) & (new < two)
    place = jnp.where(col < 2 * slots, place, jnp.where(seen, -1, never))
    first_row = lax.broadcasted_iota(jnp.int32, (two, 1), 0) < NEW
    scale = 1.0 / math.sqrt(lanes)

    def extend(cached, fresh):
        rest = jnp.zeros((wide - 2 * slots - two, lanes), jnp.float32)
        tail = jnp.concatenate([fresh, rest], axis=0).astype(jnp.bfloat16)
        return jnp.concatenate([cached.reshape(2 * slots, lanes), tail], axis=0)

    def pair(s_, i):
        rows_here = pl.ds(pl.multiple_of(i * two, two), two)
        r = s_ * own_rows + 2 * i
        q = jnp.concatenate([J[j, s_, rows_here] for j in range(queries)], axis=0)
        k = extend(keys[pl.ds(r, 2)], J[queries, s_, rows_here])
        scores = lax.dot_general(
            q.astype(jnp.bfloat16), k, (((1,), (1,)), ((), ())),
            preferred_element_type=jnp.float32,
        ) * scale
        limit = jnp.where(first_row, lengths[lens_at + r], lengths[lens_at + r + 1])
        scores = scores.reshape(queries, two, wide)
        scores = jnp.where((place < limit)[None], scores, -jnp.inf)
        grown = jnp.exp(scores - jnp.max(scores, axis=-1, keepdims=True))
        probs = grown * (1.0 / jnp.sum(grown, axis=-1, keepdims=True))
        probs = probs.reshape(queries * two, wide).astype(jnp.bfloat16)
        v = extend(values[pl.ds(r, 2)], J[queries + 1, s_, rows_here])
        return jnp.dot(probs, v, preferred_element_type=jnp.float32)

    block_rows = AT_ONCE * two

    def attend(s_, blocks, into):
        @pl.loop(*blocks)
        def _(t):
            done = [pair(s_, t * AT_ONCE + k) for k in range(AT_ONCE)]
            for j in range(queries):
                tile = jnp.concatenate([d[j * two : (j + 1) * two] for d in done], axis=0)
                into[pl.ds(pl.multiple_of(t * block_rows, 16), block_rows),
                     j * lanes : (j + 1) * lanes] = tile.astype(jnp.bfloat16)

    blocks = count // block_rows
    cut = blocks // 2
    for k, (start, stop) in enumerate(((0, cut), (cut, blocks))):
        attend(1 - s, (start, stop), mine.at[0])
        span = pl.ds(start * block_rows, (stop - start) * block_rows)
        send(mine.at[0, span], theirs.at[span], e_send.at[k], e_recv.at[k], z_pair)
    attend(s, (0, blocks), mine.at[1])
    piece = queries * lanes
    context[:, pl.ds(pl.multiple_of(s * piece, 128), piece)] = jnp.dot(
        back, mine[1], preferred_element_type=jnp.float32
    ).astype(jnp.bfloat16)
    for k, (start, stop) in enumerate(((0, cut), (cut, blocks))):
        span = pl.ds(start * block_rows, (stop - start) * block_rows)
        arrive(theirs.at[span], e_send.at[k], e_recv.at[k], z_pair)
    context[:, pl.ds(pl.multiple_of((1 - s) * piece, 128), piece)] = jnp.dot(
        back, theirs[...], preferred_element_type=jnp.float32
    ).astype(jnp.bfloat16)
    for copy in sent:
        copy.wait_send()


def project_tokens(lengths, narrow, tokens, gain, bias, keys, values):
    twice, rows, lanes = narrow.shape
    heads = twice // 2
    count, width = tokens.shape
    depth = width // 2
    assert depth == NZ * rows
    piece = (heads - 2) * lanes
    half_lanes = lanes // 2
    padded = -(-count // 128) * 128
    frequency = ROPE_BASE ** (-(np.arange(lanes) % half_lanes) / half_lanes)
    frequency = jnp.asarray(frequency.reshape(1, lanes), jnp.float32)
    dma = pltpu.SemaphoreType.DMA
    vmem = pl.BlockSpec(memory_space=pltpu.VMEM)
    hbm = pl.BlockSpec(memory_space=pl.ANY)
    return pl.pallas_call(
        layer_kernel,
        name="gather_project",
        out_shape=jax.ShapeDtypeStruct((count, 2 * piece), jnp.bfloat16),
        in_specs=[pl.BlockSpec(memory_space=pltpu.SMEM)] + [vmem] * 5 + [hbm] * 2,
        out_specs=vmem,
        scratch_shapes=[
            pltpu.VMEM((heads, NX, depth, lanes), jnp.bfloat16),
            pltpu.VMEM((NB, 2 * NH, count, depth), jnp.bfloat16),
            pltpu.VMEM((NH, 2, count, depth), jnp.bfloat16),
            pltpu.VMEM((NH, count, depth), jnp.bfloat16),
            pltpu.VMEM((NB, 8, padded), jnp.float32),
            pltpu.VMEM((2, 8, padded), jnp.float32),
            pltpu.VMEM((heads, 2, count, lanes), jnp.bfloat16),
            pltpu.VMEM((heads, 2, count, lanes), jnp.bfloat16),
            pltpu.VMEM((heads, 2, count, lanes), jnp.float32),
            pltpu.VMEM((2, count, lanes), jnp.float32),
            pltpu.VMEM((2, count, lanes), jnp.float32),
            pltpu.VMEM(keys.shape, keys.dtype),
            pltpu.VMEM(values.shape, values.dtype),
            pltpu.VMEM((2, count, piece), jnp.bfloat16),
            pltpu.VMEM((count, piece), jnp.bfloat16),
            dma((heads, NZ)), dma((heads, NZ)),
            dma((heads, 6)), dma((heads, 6)),
            dma((3,)), dma((3,)),
            dma((3,)), dma((3,)),
            dma((3, 2, CUTS)), dma((3, 2, CUTS)),
            dma((2,)),
            dma((4, 2, CUTS)), dma((4, 2, CUTS)),
            dma((heads,)), dma((heads,)),
            dma((2,)), dma((2,)), dma((2,)),
        ],
        compiler_params=pltpu.CompilerParams(
            collective_id=0, has_side_effects=True, vmem_limit_bytes=48 << 20
        ),
        cost_estimate=pl.CostEstimate(
            flops=2 * 4 * count * 4 * depth * heads * lanes, bytes_accessed=12 << 20, transcendentals=0
        ),
    )(lengths, frequency, narrow, tokens, gain, bias, keys, values)


def on_device(
    weight_master,
    gradient,
    first_moment,
    second_moment,
    query_key_value_bias,
    new_tokens,
    norm_gain,
    cache_len,
    key_cache,
    value_cache,
):
    new_master, new_first, new_second = adam_update(
        weight_master, gradient, first_moment, second_moment
    )
    head_dim = key_cache.shape[-1]
    rows_here, columns = new_master.shape
    half_cols = columns // 2
    per_group = half_cols // head_dim
    narrow = new_master.astype(jnp.bfloat16).reshape(rows_here, 2 * per_group, head_dim)
    narrow = narrow.transpose(1, 0, 2)
    steps_here, own_rows, features = new_tokens.shape
    output = project_tokens(
        cache_len, narrow, new_tokens.reshape(steps_here * own_rows, features), norm_gain,
        query_key_value_bias, key_cache[0, 0], value_cache[0, 0],
    )
    output = output.reshape(steps_here, own_rows, features)
    return (new_master, new_first, new_second, output)


def solution(mesh):
    in_specs = (
        P("fsdp", "tp"),
        P("fsdp", "tp"),
        P("fsdp", "tp"),
        P("fsdp", "tp"),
        P("tp"),
        P(None, "fsdp", "tp"),
        P("tp"),
        P(),
        P("fsdp", "tp", None, None, None),
        P("fsdp", "tp", None, None, None),
    )
    out_specs = (P("fsdp", "tp"), P("fsdp", "tp"), P("fsdp", "tp"), P(None, "fsdp", "tp"))
    return jax.shard_map(
        on_device, mesh=mesh, in_specs=in_specs, out_specs=out_specs, check_vma=False
    )
```

```python
import math

import jax
import jax.numpy as jnp
import numpy as np
from jax import lax
from jax.experimental import pallas as pl
from jax.experimental.pallas import tpu as pltpu
from jax.sharding import PartitionSpec as P

BETA_ONE = 0.9
BETA_TWO = 0.95
LEARN_RATE = 0.002
ADAM_EPS = 1e-08
CORR_ONE = 1.0 - 0.9**10
CORR_TWO = 1.0 - 0.95**10
NORM_EPS = 1e-06
ROPE_BASE = 1000000.0

MESH = pl.DeviceIdType.MESH
NX, NH, NZ = 4, 2, 8
NB = 4
NEW = 4
AT_ONCE = 8


def adam_update(weight_master, gradient, first_moment, second_moment):
    new_first = BETA_ONE * first_moment + (1.0 - BETA_ONE) * gradient
    new_second = BETA_TWO * second_moment + (1.0 - BETA_TWO) * gradient * gradient
    step_size = new_first / CORR_ONE / (jnp.sqrt(new_second / CORR_TWO) + ADAM_EPS)
    return (weight_master - LEARN_RATE * step_size, new_first, new_second)


def layer_kernel(
    lengths, frequency, narrow, tokens, gain, bias, keys_in, values_in, context,
    W, A, N, ssq, psend, precv, J, cosine, sine, keys, values, mine, theirs,
    z_send, z_recv, x_send, x_recv, q_send, q_recv,
    t_send, t_recv, s_send, s_recv, p_send, p_recv, e_send, e_recv, c_sem,
):
    heads, _, depth, lanes = W.shape
    rows = depth // NZ
    half = depth // 2
    f = lax.axis_index("fsdp")
    b = lax.axis_index("tp")
    x, h, z = f // (NH * NZ), (f // NZ) % NH, f % NZ
    lo, c = b // 2, b % 2
    s = z % 2

    def at(x_, h_, z_, lo_, c_):
        return {"fsdp": (x_ * NH + h_) * NZ + z_, "tp": lo_ * 2 + c_}

    x_up = at((x + 1) % NX, h, z, lo, c)
    x_down = at((x + NX - 1) % NX, h, z, lo, c)
    z_to = [at(x, h, (z + d) % NZ, lo, c) for d in range(NZ)]
    z_pair = at(x, h, z + 1 - 2 * s, lo, c)
    lo_pair = at(x, h, z, 1 - lo, c)
    sibling = at(x, h, z, lo, 1 - c)
    cross = at(x, h, z, 1 - lo, 1 - c)
    h_far = at(x, 1 - h, z, lo, c)
    h_near = at(x, 1 - h, z, 1 - lo, c)

    barrier = pltpu.get_barrier_semaphore()
    everyone = [x_up, x_down, lo_pair, sibling, cross, h_far, h_near] + z_to[1:]
    for other in everyone:
        pl.semaphore_signal(barrier, inc=1, device_id=other, device_id_type=MESH)

    loads = [
        pltpu.make_async_copy(keys_in, keys, c_sem.at[0]),
        pltpu.make_async_copy(values_in, values, c_sem.at[1]),
    ]
    for load in loads:
        load.start()

    count, width = tokens.shape
    own_rows = count // NEW
    flat = tokens[...].astype(jnp.float32)
    square = flat * flat
    part = square[:, :lanes]
    for k in range(1, square.shape[1] // lanes):
        part = part + square[:, k * lanes : (k + 1) * lanes]
    padded = ssq.shape[2]
    part = jnp.concatenate([part, jnp.zeros((padded - count, lanes), jnp.float32)], axis=0)
    ssq[b] = jnp.broadcast_to(jnp.sum(part.T, axis=0, keepdims=True), (8, padded))
    pl.semaphore_wait(barrier, len(everyone))

    sent = []

    def send(src, dst, send_sem, recv_sem, to):
        copy = pltpu.make_async_remote_copy(
            src_ref=src, dst_ref=dst, send_sem=send_sem, recv_sem=recv_sem,
            device_id=to, device_id_type=MESH,
        )
        copy.start()
        sent.append(copy)

    def arrive(dst, send_sem, recv_sem, to):
        pltpu.make_async_remote_copy(
            src_ref=dst, dst_ref=dst, send_sem=send_sem, recv_sem=recv_sem,
            device_id=to, device_id_type=MESH,
        ).wait_recv()

    def w_rows(j, x_, z_):
        return W.at[j, x_, pl.ds(pl.multiple_of(z_ * rows, 16), rows)]

    def w_group(j, x_, g):
        return W.at[j, x_, pl.ds(g * half, half)]

    own_copies = {}

    def z_out(j):
        own = pltpu.make_async_copy(narrow.at[s * heads + j], w_rows(j, x, z), z_recv.at[j, 0])
        own.start()
        own_copies[j] = own
        for d in (4, 3, 5, 2, 6, 1, 7):
            parity = (s + d) % 2
            send(narrow.at[parity * heads + j], w_rows(j, x, z), z_send.at[j, d],
                 z_recv.at[j, d], z_to[d])

    def x_out(j):
        own_copies[j].wait()
        for d in range(1, NZ):
            arrive(w_rows(j, x, (z + NZ - d) % NZ), z_send.at[j, d], z_recv.at[j, d], z_to[d])
        for g in (0, 1):
            for k, to in ((0, x_up), (1, x_down)):
                send(w_group(j, x, g), w_group(j, x, g), x_send.at[j, 2 * g + k],
                     x_recv.at[j, 2 * g + k], to)

    def x_on(j):
        for g, k in ((0, 0), (1, 1), (0, 1), (1, 0)):
            source = (x + NX - 1) % NX if k == 0 else (x + 1) % NX
            to = x_up if k == 0 else x_down
            arrive(w_group(j, source, g), x_send.at[j, 2 * g + k], x_recv.at[j, 2 * g + k], to)
            if g == k:
                send(w_group(j, source, g), w_group(j, source, g), x_send.at[j, 4 + g],
                     x_recv.at[j, 4 + g], to)

    def x_end(j):
        for g in (0, 1):
            arrive(w_group(j, (x + 2) % NX, g), x_send.at[j, 4 + g], x_recv.at[j, 4 + g],
                   x_up if g == 0 else x_down)

    def a_at(b_, h_, s_):
        return A.at[b_, 2 * h_ + s_]

    local = []
    b_lo = (1 - lo) * 2 + c

    def to_sibling(ref, kind, i):
        send(ref, ref, s_send.at[kind, i], s_recv.at[kind, i], sibling)

    def tokens_out(i, s_):
        send(N.at[1 - h, s_], a_at(b, h, s_), t_send.at[0, i], t_recv.at[0, i], h_near)
        send(N.at[h, s_], a_at(b, h, s_), t_send.at[1, i], t_recv.at[1, i], lo_pair)
        own = pltpu.make_async_copy(N.at[h, s_], a_at(b, h, s_), t_recv.at[4, i])
        own.start()
        local.append(own)
        send(N.at[h, s_], a_at(b, h, s_), s_send.at[0, i], s_recv.at[0, i], sibling)

    def tokens_on(i, s_):
        piece = a_at(b_lo, 1 - h, s_)
        arrive(piece, t_send.at[0, i], t_recv.at[0, i], h_near)
        send(piece, piece, t_send.at[2, i], t_recv.at[2, i], lo_pair)
        to_sibling(piece, 1, i)
        piece = a_at(b_lo, h, s_)
        arrive(piece, t_send.at[1, i], t_recv.at[1, i], lo_pair)
        to_sibling(piece, 2, i)

    def tokens_last(i, s_):
        piece = a_at(b, 1 - h, s_)
        arrive(piece, t_send.at[2, i], t_recv.at[2, i], lo_pair)
        to_sibling(piece, 3, i)

    def tokens_end():
        sib = lo * 2 + 1 - c
        sib_lo = (1 - lo) * 2 + 1 - c
        for i, s_ in ((0, s), (1, 1 - s)):
            local[i].wait()
            for kind, b_, h_ in ((0, sib, h), (1, sib_lo, 1 - h), (2, sib_lo, h), (3, sib, 1 - h)):
                arrive(a_at(b_, h_, s_), s_send.at[kind, i], s_recv.at[kind, i], sibling)

    def project(group):
        weights = [W[j].reshape(NB * depth, lanes) for j in group]
        weights = weights[0] if len(group) == 1 else jnp.concatenate(weights, axis=1)

        def block(h_):
            total = None
            for b_ in range(NB):
                part = A[b_, pl.ds(2 * h_, 2)].reshape(2 * count, depth)
                term = jnp.dot(part, weights[b_ * depth : (b_ + 1) * depth], preferred_element_type=jnp.float32)
                total = term if total is None else total + term
            return total

        far = block(1 - h).astype(jnp.bfloat16)
        for k, j in enumerate(group):
            psend[j] = far[:, k * lanes : (k + 1) * lanes].reshape(2, count, lanes)
            send(psend.at[j], precv.at[j], p_send.at[j], p_recv.at[j], h_far)
        near = block(h)
        for k, j in enumerate(group):
            J[j] = near[:, k * lanes : (k + 1) * lanes].reshape(2, count, lanes)

    queries = heads - 2
    offsets = bias[...].astype(jnp.float32).reshape(1, 2 * heads * lanes)
    offsets = jnp.where(s == 0, offsets[:, : heads * lanes], offsets[:, heads * lanes :])

    def finish(j):
        arrive(precv.at[j], p_send.at[j], p_recv.at[j], h_far)
        offset = offsets[:, j * lanes : (j + 1) * lanes]
        for s_ in (0, 1):
            full = J[j, s_] + precv[j, s_].astype(jnp.float32) + offset
            if j <= queries:
                full = full * cosine[s_] + pltpu.roll(full, lanes // 2, 1) * sine[s_]
            J[j, s_] = full.astype(jnp.bfloat16).astype(jnp.float32)

    own_lens = f // 2 * (2 * own_rows)
    two_rows = 2 * NEW
    down = lax.broadcasted_iota(jnp.int32, (two_rows, 1), 0)
    sign = jnp.where(lax.broadcasted_iota(jnp.int32, (1, lanes), 1) < lanes // 2, -1.0, 1.0)

    def tables(s_):
        @pl.loop(0, own_rows // 2)
        def _(i):
            r = own_lens + s_ * own_rows + 2 * i
            position = jnp.where(down < NEW, lengths[r], lengths[r + 1]) + down % NEW
            angle = position.astype(jnp.float32) * frequency[...]
            here = pl.ds(pl.multiple_of(i * two_rows, two_rows), two_rows)
            cosine[s_, here] = jnp.cos(angle)
            sine[s_, here] = jnp.sin(angle) * sign

    peers = ((sibling, 0), (lo_pair, 1), (cross, 2))
    for to, k in peers:
        send(ssq.at[b], ssq.at[b], q_send.at[k], q_recv.at[k], to)
    z_out(0)
    z_out(1)
    to_row = lax.broadcasted_iota(jnp.int32, (count, count), 0)
    to_col = lax.broadcasted_iota(jnp.int32, (count, count), 1)
    order = (to_col == to_row % NEW * own_rows + to_row // NEW).astype(jnp.bfloat16)
    back = (to_row == to_col % NEW * own_rows + to_col // NEW).astype(jnp.bfloat16)
    for to, k in peers:
        arrive(ssq.at[(b // 2 * 2 + 1 - c) if k == 0 else (b_lo if k == 1 else (1 - lo) * 2 + 1 - c)],
               q_send.at[k], q_recv.at[k], to)
    total = ssq[0] + ssq[1] + ssq[2] + ssq[3]
    inverse = lax.rsqrt(total * (1.0 / (NB * width)) + NORM_EPS).T[:count, :1]
    gains = gain[...].astype(jnp.float32).reshape(1, width)
    scaled = (tokens[...].astype(jnp.float32) * inverse * gains).astype(jnp.bfloat16)
    scaled = jnp.dot(order, scaled, preferred_element_type=jnp.float32).astype(jnp.bfloat16)
    N[0, s] = scaled[:, :depth]
    N[1, s] = scaled[:, depth:]
    tokens_out(0, s)
    send(N.at[1 - h, s], N.at[1 - h, s], t_send.at[3, 0], t_recv.at[3, 0], z_pair)
    send(N.at[h, s], N.at[h, s], t_send.at[3, 1], t_recv.at[3, 1], z_pair)
    x_out(0)
    z_out(2)
    x_out(1)
    x_on(0)
    z_out(3)
    tokens_on(0, s)
    for k, h_ in ((0, 1 - h), (1, h)):
        arrive(N.at[h_, 1 - s], t_send.at[3, k], t_recv.at[3, k], z_pair)
    tokens_out(1, 1 - s)
    x_out(2)
    tables(0)
    x_on(1)
    z_out(4)
    tokens_last(0, s)
    x_out(3)
    tables(1)
    x_on(2)
    z_out(5)
    tokens_on(1, 1 - s)
    x_out(4)
    x_on(3)
    z_out(6)
    x_out(5)
    x_on(4)
    tokens_last(1, 1 - s)
    x_out(6)
    tokens_end()
    x_end(0)
    x_end(1)
    project((0, 1))
    x_on(5)
    x_end(2)
    x_end(3)
    project((2, 3))
    finish(0)
    finish(1)
    x_on(6)
    x_end(4)
    x_end(5)
    project((4, 5))
    finish(2)
    finish(3)
    x_end(6)
    project((6,))
    finish(4)
    finish(5)
    finish(6)
    lens_at = f // 2 * (2 * own_rows)

    for load in loads:
        load.wait()
    slots = keys.shape[1]
    two = 2 * NEW
    wide = -(-(2 * slots + two) // 128) * 128
    col = lax.broadcasted_iota(jnp.int32, (two, wide), 1)
    row = lax.broadcasted_iota(jnp.int32, (two, wide), 0)
    never = 1 << 20
    second = (col >= slots).astype(jnp.int32)
    place = jnp.where(second == row // NEW, col - second * slots, never)
    new = col - 2 * slots
    seen = (new // NEW == row // NEW) & (new % NEW <= row % NEW) & (new < two)
    place = jnp.where(col < 2 * slots, place, jnp.where(seen, -1, never))
    first_row = lax.broadcasted_iota(jnp.int32, (two, 1), 0) < NEW
    scale = 1.0 / math.sqrt(lanes)

    def extend(cached, fresh):
        rest = jnp.zeros((wide - 2 * slots - two, lanes), jnp.float32)
        tail = jnp.concatenate([fresh, rest], axis=0).astype(jnp.bfloat16)
        return jnp.concatenate([cached.reshape(2 * slots, lanes), tail], axis=0)

    def pair(s_, i):
        rows_here = pl.ds(pl.multiple_of(i * two, two), two)
        r = s_ * own_rows + 2 * i
        q = jnp.concatenate([J[j, s_, rows_here] for j in range(queries)], axis=0)
        k = extend(keys[pl.ds(r, 2)], J[queries, s_, rows_here])
        scores = lax.dot_general(
            q.astype(jnp.bfloat16), k, (((1,), (1,)), ((), ())),
            preferred_element_type=jnp.float32,
        ) * scale
        limit = jnp.where(first_row, lengths[lens_at + r], lengths[lens_at + r + 1])
        scores = scores.reshape(queries, two, wide)
        scores = jnp.where((place < limit)[None], scores, -jnp.inf)
        grown = jnp.exp(scores - jnp.max(scores, axis=-1, keepdims=True))
        probs = grown * (1.0 / jnp.sum(grown, axis=-1, keepdims=True))
        probs = probs.reshape(queries * two, wide).astype(jnp.bfloat16)
        v = extend(values[pl.ds(r, 2)], J[queries + 1, s_, rows_here])
        return jnp.dot(probs, v, preferred_element_type=jnp.float32)

    block_rows = AT_ONCE * two

    def attend(s_, blocks, into):
        @pl.loop(*blocks)
        def _(t):
            done = [pair(s_, t * AT_ONCE + k) for k in range(AT_ONCE)]
            for j in range(queries):
                tile = jnp.concatenate([d[j * two : (j + 1) * two] for d in done], axis=0)
                into[pl.ds(pl.multiple_of(t * block_rows, 16), block_rows),
                     j * lanes : (j + 1) * lanes] = tile.astype(jnp.bfloat16)

    blocks = count // block_rows
    cut = blocks // 2
    for k, (start, stop) in enumerate(((0, cut), (cut, blocks))):
        attend(1 - s, (start, stop), mine.at[0])
        span = pl.ds(start * block_rows, (stop - start) * block_rows)
        send(mine.at[0, span], theirs.at[span], e_send.at[k], e_recv.at[k], z_pair)
    attend(s, (0, blocks), mine.at[1])
    piece = queries * lanes
    context[:, pl.ds(pl.multiple_of(s * piece, 128), piece)] = jnp.dot(
        back, mine[1], preferred_element_type=jnp.float32
    ).astype(jnp.bfloat16)
    for k, (start, stop) in enumerate(((0, cut), (cut, blocks))):
        span = pl.ds(start * block_rows, (stop - start) * block_rows)
        arrive(theirs.at[span], e_send.at[k], e_recv.at[k], z_pair)
    context[:, pl.ds(pl.multiple_of((1 - s) * piece, 128), piece)] = jnp.dot(
        back, theirs[...], preferred_element_type=jnp.float32
    ).astype(jnp.bfloat16)
    for copy in sent:
        copy.wait_send()


def project_tokens(lengths, narrow, tokens, gain, bias, keys, values):
    twice, rows, lanes = narrow.shape
    heads = twice // 2
    count, width = tokens.shape
    depth = width // 2
    assert depth == NZ * rows
    piece = (heads - 2) * lanes
    half_lanes = lanes // 2
    padded = -(-count // 128) * 128
    frequency = ROPE_BASE ** (-(np.arange(lanes) % half_lanes) / half_lanes)
    frequency = jnp.asarray(frequency.reshape(1, lanes), jnp.float32)
    dma = pltpu.SemaphoreType.DMA
    vmem = pl.BlockSpec(memory_space=pltpu.VMEM)
    hbm = pl.BlockSpec(memory_space=pl.ANY)
    return pl.pallas_call(
        layer_kernel,
        name="gather_project",
        out_shape=jax.ShapeDtypeStruct((count, 2 * piece), jnp.bfloat16),
        in_specs=[pl.BlockSpec(memory_space=pltpu.SMEM)] + [vmem] * 5 + [hbm] * 2,
        out_specs=vmem,
        scratch_shapes=[
            pltpu.VMEM((heads, NX, depth, lanes), jnp.bfloat16),
            pltpu.VMEM((NB, 2 * NH, count, depth), jnp.bfloat16),
            pltpu.VMEM((NH, 2, count, depth), jnp.bfloat16),
            pltpu.VMEM((NB, 8, padded), jnp.float32),
            pltpu.VMEM((heads, 2, count, lanes), jnp.bfloat16),
            pltpu.VMEM((heads, 2, count, lanes), jnp.bfloat16),
            pltpu.VMEM((heads, 2, count, lanes), jnp.float32),
            pltpu.VMEM((2, count, lanes), jnp.float32),
            pltpu.VMEM((2, count, lanes), jnp.float32),
            pltpu.VMEM(keys.shape, keys.dtype),
            pltpu.VMEM(values.shape, values.dtype),
            pltpu.VMEM((2, count, piece), jnp.bfloat16),
            pltpu.VMEM((count, piece), jnp.bfloat16),
            dma((heads, NZ)), dma((heads, NZ)),
            dma((heads, 6)), dma((heads, 6)),
            dma((3,)), dma((3,)),
            dma((5, 2)), dma((5, 2)),
            dma((4, 2)), dma((4, 2)),
            dma((heads,)), dma((heads,)),
            dma((2,)), dma((2,)), dma((2,)),
        ],
        compiler_params=pltpu.CompilerParams(
            collective_id=0, has_side_effects=True, vmem_limit_bytes=48 << 20
        ),
        cost_estimate=pl.CostEstimate(
            flops=2 * 4 * count * 4 * depth * heads * lanes, bytes_accessed=12 << 20, transcendentals=0
        ),
    )(lengths, frequency, narrow, tokens, gain, bias, keys, values)


def on_device(
    weight_master,
    gradient,
    first_moment,
    second_moment,
    query_key_value_bias,
    new_tokens,
    norm_gain,
    cache_len,
    key_cache,
    value_cache,
):
    new_master, new_first, new_second = adam_update(
        weight_master, gradient, first_moment, second_moment
    )
    head_dim = key_cache.shape[-1]
    rows_here, columns = new_master.shape
    half_cols = columns // 2
    per_group = half_cols // head_dim
    narrow = new_master.astype(jnp.bfloat16).reshape(rows_here, 2 * per_group, head_dim)
    narrow = narrow.transpose(1, 0, 2)
    steps_here, own_rows, features = new_tokens.shape
    output = project_tokens(
        cache_len, narrow, new_tokens.reshape(steps_here * own_rows, features), norm_gain,
        query_key_value_bias, key_cache[0, 0], value_cache[0, 0],
    )
    output = output.reshape(steps_here, own_rows, features)
    return (new_master, new_first, new_second, output)


def solution(mesh):
    in_specs = (
        P("fsdp", "tp"),
        P("fsdp", "tp"),
        P("fsdp", "tp"),
        P("fsdp", "tp"),
        P("tp"),
        P(None, "fsdp", "tp"),
        P("tp"),
        P(),
        P("fsdp", "tp", None, None, None),
        P("fsdp", "tp", None, None, None),
    )
    out_specs = (P("fsdp", "tp"), P("fsdp", "tp"), P("fsdp", "tp"), P(None, "fsdp", "tp"))
    return jax.shard_map(
        on_device, mesh=mesh, in_specs=in_specs, out_specs=out_specs, check_vma=False
    )
```

```python
import math

import jax
import jax.numpy as jnp
import numpy as np
from jax import lax
from jax.experimental import pallas as pl
from jax.experimental.pallas import tpu as pltpu
from jax.sharding import PartitionSpec as P

BETA_ONE = 0.9
BETA_TWO = 0.95
LEARN_RATE = 0.002
ADAM_EPS = 1e-08
CORR_ONE = 1.0 - 0.9**10
CORR_TWO = 1.0 - 0.95**10
NORM_EPS = 1e-06
ROPE_BASE = 1000000.0

MESH = pl.DeviceIdType.MESH
NX, NH, NZ = 4, 2, 8
NB = 4
NEW = 4
AT_ONCE = 8


def adam_update(weight_master, gradient, first_moment, second_moment):
    new_first = BETA_ONE * first_moment + (1.0 - BETA_ONE) * gradient
    new_second = BETA_TWO * second_moment + (1.0 - BETA_TWO) * gradient * gradient
    step_size = new_first / CORR_ONE / (jnp.sqrt(new_second / CORR_TWO) + ADAM_EPS)
    return (weight_master - LEARN_RATE * step_size, new_first, new_second)


def layer_kernel(
    lengths, frequency, narrow, tokens, gain, bias, keys_in, values_in, context,
    W, A, N, ssq, psend, precv, J, cosine, sine, keys, values, mine, theirs,
    z_send, z_recv, x_send, x_recv, q_send, q_recv,
    t_send, t_recv, s_send, s_recv, p_send, p_recv, e_send, e_recv, c_sem,
):
    heads, _, depth, lanes = W.shape
    rows = depth // NZ
    half = depth // 2
    f = lax.axis_index("fsdp")
    b = lax.axis_index("tp")
    x, h, z = f // (NH * NZ), (f // NZ) % NH, f % NZ
    lo, c = b // 2, b % 2
    s = z % 2

    def at(x_, h_, z_, lo_, c_):
        return {"fsdp": (x_ * NH + h_) * NZ + z_, "tp": lo_ * 2 + c_}

    x_up = at((x + 1) % NX, h, z, lo, c)
    x_down = at((x + NX - 1) % NX, h, z, lo, c)
    z_to = [at(x, h, (z + d) % NZ, lo, c) for d in range(NZ)]
    z_pair = at(x, h, z + 1 - 2 * s, lo, c)
    lo_pair = at(x, h, z, 1 - lo, c)
    sibling = at(x, h, z, lo, 1 - c)
    cross = at(x, h, z, 1 - lo, 1 - c)
    h_far = at(x, 1 - h, z, lo, c)
    h_near = at(x, 1 - h, z, 1 - lo, c)

    barrier = pltpu.get_barrier_semaphore()
    everyone = [x_up, x_down, lo_pair, sibling, cross, h_far, h_near] + z_to[1:]
    for other in everyone:
        pl.semaphore_signal(barrier, inc=1, device_id=other, device_id_type=MESH)

    loads = [
        pltpu.make_async_copy(keys_in, keys, c_sem.at[0]),
        pltpu.make_async_copy(values_in, values, c_sem.at[1]),
    ]
    for load in loads:
        load.start()

    count, width = tokens.shape
    own_rows = count // NEW
    flat = tokens[...].astype(jnp.float32)
    square = flat * flat
    part = square[:, :lanes]
    for k in range(1, square.shape[1] // lanes):
        part = part + square[:, k * lanes : (k + 1) * lanes]
    padded = ssq.shape[2]
    part = jnp.concatenate([part, jnp.zeros((padded - count, lanes), jnp.float32)], axis=0)
    ssq[b] = jnp.broadcast_to(jnp.sum(part.T, axis=0, keepdims=True), (8, padded))
    pl.semaphore_wait(barrier, len(everyone))

    sent = []

    def send(src, dst, send_sem, recv_sem, to):
        copy = pltpu.make_async_remote_copy(
            src_ref=src, dst_ref=dst, send_sem=send_sem, recv_sem=recv_sem,
            device_id=to, device_id_type=MESH,
        )
        copy.start()
        sent.append(copy)

    def arrive(dst, send_sem, recv_sem, to):
        pltpu.make_async_remote_copy(
            src_ref=dst, dst_ref=dst, send_sem=send_sem, recv_sem=recv_sem,
            device_id=to, device_id_type=MESH,
        ).wait_recv()

    def w_rows(j, x_, z_):
        return W.at[j, x_, pl.ds(pl.multiple_of(z_ * rows, 16), rows)]

    def w_group(j, x_, g):
        return W.at[j, x_, pl.ds(g * half, half)]

    own_copies = {}

    def z_out(j):
        own = pltpu.make_async_copy(narrow.at[s * heads + j], w_rows(j, x, z), z_recv.at[j, 0])
        own.start()
        own_copies[j] = own
        for d in (1, 7, 2, 6):
            parity = (s + d) % 2
            send(narrow.at[parity * heads + j], w_rows(j, x, z), z_send.at[j, d],
                 z_recv.at[j, d], z_to[d])

    def z_on(j):
        for d, onward, to in ((1, 3, 2), (7, 5, 6), (2, 4, 2) if j % 2 == 0 else (6, 4, 6)):
            block = w_rows(j, x, (z + NZ - d) % NZ)
            arrive(block, z_send.at[j, d], z_recv.at[j, d], z_to[d])
            send(block, block, z_send.at[j, onward], z_recv.at[j, onward], z_to[to])

    def x_out(j):
        own_copies[j].wait()
        for d in (3, 4, 5, 6 if j % 2 == 0 else 2):
            arrive(w_rows(j, x, (z + NZ - d) % NZ), z_send.at[j, d], z_recv.at[j, d], z_to[d])
        for g in (0, 1):
            for k, to in ((0, x_up), (1, x_down)):
                send(w_group(j, x, g), w_group(j, x, g), x_send.at[j, 2 * g + k],
                     x_recv.at[j, 2 * g + k], to)

    def x_on(j):
        for g, k in ((0, 0), (1, 1), (0, 1), (1, 0)):
            source = (x + NX - 1) % NX if k == 0 else (x + 1) % NX
            to = x_up if k == 0 else x_down
            arrive(w_group(j, source, g), x_send.at[j, 2 * g + k], x_recv.at[j, 2 * g + k], to)
            if g == k:
                send(w_group(j, source, g), w_group(j, source, g), x_send.at[j, 4 + g],
                     x_recv.at[j, 4 + g], to)

    def x_end(j):
        for g in (0, 1):
            arrive(w_group(j, (x + 2) % NX, g), x_send.at[j, 4 + g], x_recv.at[j, 4 + g],
                   x_up if g == 0 else x_down)

    def a_at(b_, h_, s_):
        return A.at[b_, 2 * h_ + s_]

    local = []
    b_lo = (1 - lo) * 2 + c

    def to_sibling(ref, kind, i):
        send(ref, ref, s_send.at[kind, i], s_recv.at[kind, i], sibling)

    def tokens_out(i, s_):
        send(N.at[1 - h, s_], a_at(b, h, s_), t_send.at[0, i], t_recv.at[0, i], h_near)
        send(N.at[h, s_], a_at(b, h, s_), t_send.at[1, i], t_recv.at[1, i], lo_pair)
        own = pltpu.make_async_copy(N.at[h, s_], a_at(b, h, s_), t_recv.at[4, i])
        own.start()
        local.append(own)
        send(N.at[h, s_], a_at(b, h, s_), s_send.at[0, i], s_recv.at[0, i], sibling)

    def tokens_on(i, s_):
        piece = a_at(b_lo, 1 - h, s_)
        arrive(piece, t_send.at[0, i], t_recv.at[0, i], h_near)
        send(piece, piece, t_send.at[2, i], t_recv.at[2, i], lo_pair)
        to_sibling(piece, 1, i)
        piece = a_at(b_lo, h, s_)
        arrive(piece, t_send.at[1, i], t_recv.at[1, i], lo_pair)
        to_sibling(piece, 2, i)

    def tokens_last(i, s_):
        piece = a_at(b, 1 - h, s_)
        arrive(piece, t_send.at[2, i], t_recv.at[2, i], lo_pair)
        to_sibling(piece, 3, i)

    def tokens_end():
        sib = lo * 2 + 1 - c
        sib_lo = (1 - lo) * 2 + 1 - c
        for i, s_ in ((0, s), (1, 1 - s)):
            local[i].wait()
            for kind, b_, h_ in ((0, sib, h), (1, sib_lo, 1 - h), (2, sib_lo, h), (3, sib, 1 - h)):
                arrive(a_at(b_, h_, s_), s_send.at[kind, i], s_recv.at[kind, i], sibling)

    def project(group):
        weights = [W[j].reshape(NB * depth, lanes) for j in group]
        weights = weights[0] if len(group) == 1 else jnp.concatenate(weights, axis=1)

        def block(h_):
            total = None
            for b_ in range(NB):
                part = A[b_, pl.ds(2 * h_, 2)].reshape(2 * count, depth)
                term = jnp.dot(part, weights[b_ * depth : (b_ + 1) * depth], preferred_element_type=jnp.float32)
                total = term if total is None else total + term
            return total

        far = block(1 - h).astype(jnp.bfloat16)
        for k, j in enumerate(group):
            psend[j] = far[:, k * lanes : (k + 1) * lanes].reshape(2, count, lanes)
            send(psend.at[j], precv.at[j], p_send.at[j], p_recv.at[j], h_far)
        near = block(h)
        for k, j in enumerate(group):
            J[j] = near[:, k * lanes : (k + 1) * lanes].reshape(2, count, lanes)

    queries = heads - 2
    offsets = bias[...].astype(jnp.float32).reshape(1, 2 * heads * lanes)
    offsets = jnp.where(s == 0, offsets[:, : heads * lanes], offsets[:, heads * lanes :])

    def finish(j):
        arrive(precv.at[j], p_send.at[j], p_recv.at[j], h_far)
        offset = offsets[:, j * lanes : (j + 1) * lanes]
        for s_ in (0, 1):
            full = J[j, s_] + precv[j, s_].astype(jnp.float32) + offset
            if j <= queries:
                full = full * cosine[s_] + pltpu.roll(full, lanes // 2, 1) * sine[s_]
            J[j, s_] = full.astype(jnp.bfloat16).astype(jnp.float32)

    own_lens = f // 2 * (2 * own_rows)
    two_rows = 2 * NEW
    down = lax.broadcasted_iota(jnp.int32, (two_rows, 1), 0)
    sign = jnp.where(lax.broadcasted_iota(jnp.int32, (1, lanes), 1) < lanes // 2, -1.0, 1.0)

    def tables(s_):
        @pl.loop(0, own_rows // 2)
        def _(i):
            r = own_lens + s_ * own_rows + 2 * i
            position = jnp.where(down < NEW, lengths[r], lengths[r + 1]) + down % NEW
            angle = position.astype(jnp.float32) * frequency[...]
            here = pl.ds(pl.multiple_of(i * two_rows, two_rows), two_rows)
            cosine[s_, here] = jnp.cos(angle)
            sine[s_, here] = jnp.sin(angle) * sign

    peers = ((sibling, 0), (lo_pair, 1), (cross, 2))
    for to, k in peers:
        send(ssq.at[b], ssq.at[b], q_send.at[k], q_recv.at[k], to)
    z_out(0)
    z_out(1)
    to_row = lax.broadcasted_iota(jnp.int32, (count, count), 0)
    to_col = lax.broadcasted_iota(jnp.int32, (count, count), 1)
    order = (to_col == to_row % NEW * own_rows + to_row // NEW).astype(jnp.bfloat16)
    back = (to_row == to_col % NEW * own_rows + to_col // NEW).astype(jnp.bfloat16)
    for to, k in peers:
        arrive(ssq.at[(b // 2 * 2 + 1 - c) if k == 0 else (b_lo if k == 1 else (1 - lo) * 2 + 1 - c)],
               q_send.at[k], q_recv.at[k], to)
    z_on(0)
    total = ssq[0] + ssq[1] + ssq[2] + ssq[3]
    inverse = lax.rsqrt(total * (1.0 / (NB * width)) + NORM_EPS).T[:count, :1]
    gains = gain[...].astype(jnp.float32).reshape(1, width)
    scaled = (tokens[...].astype(jnp.float32) * inverse * gains).astype(jnp.bfloat16)
    scaled = jnp.dot(order, scaled, preferred_element_type=jnp.float32).astype(jnp.bfloat16)
    N[0, s] = scaled[:, :depth]
    N[1, s] = scaled[:, depth:]
    tokens_out(0, s)
    send(N.at[1 - h, s], N.at[1 - h, s], t_send.at[3, 0], t_recv.at[3, 0], z_pair)
    send(N.at[h, s], N.at[h, s], t_send.at[3, 1], t_recv.at[3, 1], z_pair)
    x_out(0)
    z_on(1)
    z_out(2)
    x_out(1)
    x_on(0)
    z_on(2)
    z_out(3)
    tokens_on(0, s)
    for k, h_ in ((0, 1 - h), (1, h)):
        arrive(N.at[h_, 1 - s], t_send.at[3, k], t_recv.at[3, k], z_pair)
    tokens_out(1, 1 - s)
    x_out(2)
    z_on(3)
    z_out(4)
    tables(0)
    x_on(1)
    tokens_last(0, s)
    x_out(3)
    z_on(4)
    z_out(5)
    tables(1)
    x_on(2)
    tokens_on(1, 1 - s)
    x_out(4)
    z_on(5)
    z_out(6)
    x_on(3)
    x_out(5)
    z_on(6)
    x_on(4)
    tokens_last(1, 1 - s)
    x_out(6)
    tokens_end()
    x_end(0)
    x_end(1)
    project((0, 1))
    x_on(5)
    x_end(2)
    x_end(3)
    project((2, 3))
    finish(0)
    finish(1)
    x_on(6)
    x_end(4)
    x_end(5)
    project((4, 5))
    finish(2)
    finish(3)
    x_end(6)
    project((6,))
    finish(4)
    finish(5)
    finish(6)
    lens_at = f // 2 * (2 * own_rows)

    for load in loads:
        load.wait()
    slots = keys.shape[1]
    two = 2 * NEW
    wide = -(-(2 * slots + two) // 128) * 128
    col = lax.broadcasted_iota(jnp.int32, (two, wide), 1)
    row = lax.broadcasted_iota(jnp.int32, (two, wide), 0)
    never = 1 << 20
    second = (col >= slots).astype(jnp.int32)
    place = jnp.where(second == row // NEW, col - second * slots, never)
    new = col - 2 * slots
    seen = (new // NEW == row // NEW) & (new % NEW <= row % NEW) & (new < two)
    place = jnp.where(col < 2 * slots, place, jnp.where(seen, -1, never))
    first_row = lax.broadcasted_iota(jnp.int32, (two, 1), 0) < NEW
    scale = 1.0 / math.sqrt(lanes)

    def extend(cached, fresh):
        rest = jnp.zeros((wide - 2 * slots - two, lanes), jnp.float32)
        tail = jnp.concatenate([fresh, rest], axis=0).astype(jnp.bfloat16)
        return jnp.concatenate([cached.reshape(2 * slots, lanes), tail], axis=0)

    def pair(s_, i):
        rows_here = pl.ds(pl.multiple_of(i * two, two), two)
        r = s_ * own_rows + 2 * i
        q = jnp.concatenate([J[j, s_, rows_here] for j in range(queries)], axis=0)
        k = extend(keys[pl.ds(r, 2)], J[queries, s_, rows_here])
        scores = lax.dot_general(
            q.astype(jnp.bfloat16), k, (((1,), (1,)), ((), ())),
            preferred_element_type=jnp.float32,
        ) * scale
        limit = jnp.where(first_row, lengths[lens_at + r], lengths[lens_at + r + 1])
        scores = scores.reshape(queries, two, wide)
        scores = jnp.where((place < limit)[None], scores, -jnp.inf)
        grown = jnp.exp(scores - jnp.max(scores, axis=-1, keepdims=True))
        probs = grown * (1.0 / jnp.sum(grown, axis=-1, keepdims=True))
        probs = probs.reshape(queries * two, wide).astype(jnp.bfloat16)
        v = extend(values[pl.ds(r, 2)], J[queries + 1, s_, rows_here])
        return jnp.dot(probs, v, preferred_element_type=jnp.float32)

    block_rows = AT_ONCE * two

    def attend(s_, blocks, into):
        @pl.loop(*blocks)
        def _(t):
            done = [pair(s_, t * AT_ONCE + k) for k in range(AT_ONCE)]
            for j in range(queries):
                tile = jnp.concatenate([d[j * two : (j + 1) * two] for d in done], axis=0)
                into[pl.ds(pl.multiple_of(t * block_rows, 16), block_rows),
                     j * lanes : (j + 1) * lanes] = tile.astype(jnp.bfloat16)

    blocks = count // block_rows
    cut = blocks // 2
    for k, (start, stop) in enumerate(((0, cut), (cut, blocks))):
        attend(1 - s, (start, stop), mine.at[0])
        span = pl.ds(start * block_rows, (stop - start) * block_rows)
        send(mine.at[0, span], theirs.at[span], e_send.at[k], e_recv.at[k], z_pair)
    attend(s, (0, blocks), mine.at[1])
    piece = queries * lanes
    context[:, pl.ds(pl.multiple_of(s * piece, 128), piece)] = jnp.dot(
        back, mine[1], preferred_element_type=jnp.float32
    ).astype(jnp.bfloat16)
    for k, (start, stop) in enumerate(((0, cut), (cut, blocks))):
        span = pl.ds(start * block_rows, (stop - start) * block_rows)
        arrive(theirs.at[span], e_send.at[k], e_recv.at[k], z_pair)
    context[:, pl.ds(pl.multiple_of((1 - s) * piece, 128), piece)] = jnp.dot(
        back, theirs[...], preferred_element_type=jnp.float32
    ).astype(jnp.bfloat16)
    for copy in sent:
        copy.wait_send()


def project_tokens(lengths, narrow, tokens, gain, bias, keys, values):
    twice, rows, lanes = narrow.shape
    heads = twice // 2
    count, width = tokens.shape
    depth = width // 2
    assert depth == NZ * rows
    piece = (heads - 2) * lanes
    half_lanes = lanes // 2
    padded = -(-count // 128) * 128
    frequency = ROPE_BASE ** (-(np.arange(lanes) % half_lanes) / half_lanes)
    frequency = jnp.asarray(frequency.reshape(1, lanes), jnp.float32)
    dma = pltpu.SemaphoreType.DMA
    vmem = pl.BlockSpec(memory_space=pltpu.VMEM)
    hbm = pl.BlockSpec(memory_space=pl.ANY)
    return pl.pallas_call(
        layer_kernel,
        name="gather_project",
        out_shape=jax.ShapeDtypeStruct((count, 2 * piece), jnp.bfloat16),
        in_specs=[pl.BlockSpec(memory_space=pltpu.SMEM)] + [vmem] * 5 + [hbm] * 2,
        out_specs=vmem,
        scratch_shapes=[
            pltpu.VMEM((heads, NX, depth, lanes), jnp.bfloat16),
            pltpu.VMEM((NB, 2 * NH, count, depth), jnp.bfloat16),
            pltpu.VMEM((NH, 2, count, depth), jnp.bfloat16),
            pltpu.VMEM((NB, 8, padded), jnp.float32),
            pltpu.VMEM((heads, 2, count, lanes), jnp.bfloat16),
            pltpu.VMEM((heads, 2, count, lanes), jnp.bfloat16),
            pltpu.VMEM((heads, 2, count, lanes), jnp.float32),
            pltpu.VMEM((2, count, lanes), jnp.float32),
            pltpu.VMEM((2, count, lanes), jnp.float32),
            pltpu.VMEM(keys.shape, keys.dtype),
            pltpu.VMEM(values.shape, values.dtype),
            pltpu.VMEM((2, count, piece), jnp.bfloat16),
            pltpu.VMEM((count, piece), jnp.bfloat16),
            dma((heads, NZ)), dma((heads, NZ)),
            dma((heads, 6)), dma((heads, 6)),
            dma((3,)), dma((3,)),
            dma((5, 2)), dma((5, 2)),
            dma((4, 2)), dma((4, 2)),
            dma((heads,)), dma((heads,)),
            dma((2,)), dma((2,)), dma((2,)),
        ],
        compiler_params=pltpu.CompilerParams(
            collective_id=0, has_side_effects=True, vmem_limit_bytes=48 << 20
        ),
        cost_estimate=pl.CostEstimate(
            flops=2 * 4 * count * 4 * depth * heads * lanes, bytes_accessed=12 << 20, transcendentals=0
        ),
    )(lengths, frequency, narrow, tokens, gain, bias, keys, values)


def on_device(
    weight_master,
    gradient,
    first_moment,
    second_moment,
    query_key_value_bias,
    new_tokens,
    norm_gain,
    cache_len,
    key_cache,
    value_cache,
):
    new_master, new_first, new_second = adam_update(
        weight_master, gradient, first_moment, second_moment
    )
    head_dim = key_cache.shape[-1]
    rows_here, columns = new_master.shape
    half_cols = columns // 2
    per_group = half_cols // head_dim
    narrow = new_master.astype(jnp.bfloat16).reshape(rows_here, 2 * per_group, head_dim)
    narrow = narrow.transpose(1, 0, 2)
    steps_here, own_rows, features = new_tokens.shape
    output = project_tokens(
        cache_len, narrow, new_tokens.reshape(steps_here * own_rows, features), norm_gain,
        query_key_value_bias, key_cache[0, 0], value_cache[0, 0],
    )
    output = output.reshape(steps_here, own_rows, features)
    return (new_master, new_first, new_second, output)


def solution(mesh):
    in_specs = (
        P("fsdp", "tp"),
        P("fsdp", "tp"),
        P("fsdp", "tp"),
        P("fsdp", "tp"),
        P("tp"),
        P(None, "fsdp", "tp"),
        P("tp"),
        P(),
        P("fsdp", "tp", None, None, None),
        P("fsdp", "tp", None, None, None),
    )
    out_specs = (P("fsdp", "tp"), P("fsdp", "tp"), P("fsdp", "tp"), P(None, "fsdp", "tp"))
    return jax.shard_map(
        on_device, mesh=mesh, in_specs=in_specs, out_specs=out_specs, check_vma=False
    )
```

```python
import math

import jax
import jax.numpy as jnp
import numpy as np
from jax import lax
from jax.experimental import pallas as pl
from jax.experimental.pallas import tpu as pltpu
from jax.sharding import PartitionSpec as P

BETA_ONE = 0.9
BETA_TWO = 0.95
LEARN_RATE = 0.002
ADAM_EPS = 1e-08
CORR_ONE = 1.0 - 0.9**10
CORR_TWO = 1.0 - 0.95**10
NORM_EPS = 1e-06
ROPE_BASE = 1000000.0

MESH = pl.DeviceIdType.MESH
NX, NH, NZ = 4, 2, 8
NB = 4
NEW = 4
CUTS = 2
AT_ONCE = 8


def adam_update(weight_master, gradient, first_moment, second_moment):
    new_first = BETA_ONE * first_moment + (1.0 - BETA_ONE) * gradient
    new_second = BETA_TWO * second_moment + (1.0 - BETA_TWO) * gradient * gradient
    step_size = new_first / CORR_ONE / (jnp.sqrt(new_second / CORR_TWO) + ADAM_EPS)
    return (weight_master - LEARN_RATE * step_size, new_first, new_second)


def layer_kernel(
    lengths, frequency, narrow, tokens, gain, bias, keys_in, values_in, context,
    W, A, N, R, ssq, tot, psend, precv, J, cosine, sine, keys, values, mine, theirs,
    z_send, z_recv, x_send, x_recv, q_send, q_recv,
    t1_send, t1_recv, t_send, t_recv, l_sem, s_send, s_recv, p_send, p_recv, e_send, e_recv, c_sem,
):
    heads, _, depth, lanes = W.shape
    rows = depth // NZ
    half = depth // 2
    f = lax.axis_index("fsdp")
    b = lax.axis_index("tp")
    x, h, z = f // (NH * NZ), (f // NZ) % NH, f % NZ
    lo, c = b // 2, b % 2
    s = z % 2

    def at(x_, h_, z_, lo_, c_):
        return {"fsdp": (x_ * NH + h_) * NZ + z_, "tp": lo_ * 2 + c_}

    x_up = at((x + 1) % NX, h, z, lo, c)
    x_down = at((x + NX - 1) % NX, h, z, lo, c)
    z_to = [at(x, h, (z + d) % NZ, lo, c) for d in range(NZ)]
    z_pair = at(x, h, z + 1 - 2 * s, lo, c)
    lo_pair = at(x, h, z, 1 - lo, c)
    sibling = at(x, h, z, lo, 1 - c)
    cross = at(x, h, z, 1 - lo, 1 - c)
    h_far = at(x, 1 - h, z, lo, c)
    h_near = at(x, 1 - h, z, 1 - lo, c)

    barrier = pltpu.get_barrier_semaphore()
    everyone = [x_up, x_down, lo_pair, sibling, cross, h_far, h_near] + z_to[1:]
    for other in everyone:
        pl.semaphore_signal(barrier, inc=1, device_id=other, device_id_type=MESH)

    loads = [
        pltpu.make_async_copy(keys_in, keys, c_sem.at[0]),
        pltpu.make_async_copy(values_in, values, c_sem.at[1]),
    ]
    for load in loads:
        load.start()

    count, width = tokens.shape
    own_rows = count // NEW
    flat = tokens[...].astype(jnp.float32)
    square = flat * flat
    part = square[:, :lanes]
    for k in range(1, square.shape[1] // lanes):
        part = part + square[:, k * lanes : (k + 1) * lanes]
    padded = ssq.shape[2]
    part = jnp.concatenate([part, jnp.zeros((padded - count, lanes), jnp.float32)], axis=0)
    ssq[b] = jnp.broadcast_to(jnp.sum(part.T, axis=0, keepdims=True), (8, padded))
    pl.semaphore_wait(barrier, len(everyone))

    sent = []

    def send(src, dst, send_sem, recv_sem, to):
        copy = pltpu.make_async_remote_copy(
            src_ref=src, dst_ref=dst, send_sem=send_sem, recv_sem=recv_sem,
            device_id=to, device_id_type=MESH,
        )
        copy.start()
        sent.append(copy)

    def arrive(dst, send_sem, recv_sem, to):
        pltpu.make_async_remote_copy(
            src_ref=dst, dst_ref=dst, send_sem=send_sem, recv_sem=recv_sem,
            device_id=to, device_id_type=MESH,
        ).wait_recv()

    def w_rows(j, x_, z_):
        return W.at[j, x_, pl.ds(pl.multiple_of(z_ * rows, 16), rows)]

    def w_group(j, x_, g):
        return W.at[j, x_, pl.ds(g * half, half)]

    own_copies = {}

    def z_out(j):
        own = pltpu.make_async_copy(narrow.at[s * heads + j], w_rows(j, x, z), z_recv.at[j, 0])
        own.start()
        own_copies[j] = own
        for d in (1, 7, 2, 6):
            parity = (s + d) % 2
            send(narrow.at[parity * heads + j], w_rows(j, x, z), z_send.at[j, d],
                 z_recv.at[j, d], z_to[d])

    def z_on(j):
        for d, onward, to in ((1, 3, 2), (7, 5, 6), (2, 4, 2) if j % 2 == 0 else (6, 4, 6)):
            block = w_rows(j, x, (z + NZ - d) % NZ)
            arrive(block, z_send.at[j, d], z_recv.at[j, d], z_to[d])
            send(block, block, z_send.at[j, onward], z_recv.at[j, onward], z_to[to])

    def x_out(j):
        own_copies[j].wait()
        for d in (3, 4, 5, 6 if j % 2 == 0 else 2):
            arrive(w_rows(j, x, (z + NZ - d) % NZ), z_send.at[j, d], z_recv.at[j, d], z_to[d])
        for g in (0, 1):
            for k, to in ((0, x_up), (1, x_down)):
                send(w_group(j, x, g), w_group(j, x, g), x_send.at[j, 2 * g + k],
                     x_recv.at[j, 2 * g + k], to)

    def x_on(j):
        for g, k in ((0, 0), (1, 1), (0, 1), (1, 0)):
            source = (x + NX - 1) % NX if k == 0 else (x + 1) % NX
            to = x_up if k == 0 else x_down
            arrive(w_group(j, source, g), x_send.at[j, 2 * g + k], x_recv.at[j, 2 * g + k], to)
            if g == k:
                send(w_group(j, source, g), w_group(j, source, g), x_send.at[j, 4 + g],
                     x_recv.at[j, 4 + g], to)

    def x_end(j):
        for g in (0, 1):
            arrive(w_group(j, (x + 2) % NX, g), x_send.at[j, 4 + g], x_recv.at[j, 4 + g],
                   x_up if g == 0 else x_down)

    cut_rows = count // CUTS

    def a_at(b_, h_, s_, g=None):
        rows_ = pl.ds(0, count) if g is None else pl.ds(g * cut_rows, cut_rows)
        return A.at[b_, 2 * h_ + s_, rows_]

    def n_at(h_, s_, g):
        return N.at[h_, s_, pl.ds(g * cut_rows, cut_rows)]

    local = []
    b_lo = (1 - lo) * 2 + c

    def far_out(i, s_):
        for g in range(CUTS):
            send(n_at(1 - h, s_, g), a_at(b, h, s_, g), t_send.at[0, i, g], t_recv.at[0, i, g], h_near)

    def near_out(i, s_, g):
        send(n_at(h, s_, g), a_at(b, h, s_, g), t_send.at[1, i, g], t_recv.at[1, i, g], lo_pair)

    def own_out(i, s_):
        own = pltpu.make_async_copy(N.at[h, s_], a_at(b, h, s_), l_sem.at[i])
        own.start()
        local.append(own)
        send(N.at[h, s_], a_at(b, h, s_), s_send.at[0, i, 0], s_recv.at[0, i, 0], sibling)

    def to_sibling(ref, kind, i, g):
        send(ref, ref, s_send.at[kind, i, g], s_recv.at[kind, i, g], sibling)

    def far_on(i, s_):
        for g in range(CUTS):
            piece = a_at(b_lo, 1 - h, s_, g)
            arrive(piece, t_send.at[0, i, g], t_recv.at[0, i, g], h_near)
            send(piece, piece, t_send.at[2, i, g], t_recv.at[2, i, g], lo_pair)
            to_sibling(piece, 1, i, g)

    def last_on(i, s_):
        for kind, b_, h_ in ((1, b_lo, h), (2, b, 1 - h)):
            for g in range(CUTS):
                piece = a_at(b_, h_, s_, g)
                arrive(piece, t_send.at[kind, i, g], t_recv.at[kind, i, g], lo_pair)
                to_sibling(piece, kind + 1, i, g)

    def tokens_end():
        sib = lo * 2 + 1 - c
        sib_lo = (1 - lo) * 2 + 1 - c
        for i, s_ in ((0, s), (1, 1 - s)):
            local[i].wait()
            arrive(a_at(sib, h, s_), s_send.at[0, i, 0], s_recv.at[0, i, 0], sibling)
            for kind, b_, h_ in ((1, sib_lo, 1 - h), (2, sib_lo, h), (3, sib, 1 - h)):
                for g in range(CUTS):
                    arrive(a_at(b_, h_, s_, g), s_send.at[kind, i, g], s_recv.at[kind, i, g], sibling)

    def project(group):
        weights = [W[j].reshape(NB * depth, lanes) for j in group]
        weights = weights[0] if len(group) == 1 else jnp.concatenate(weights, axis=1)

        def block(h_):
            total = None
            for b_ in range(NB):
                part = A[b_, pl.ds(2 * h_, 2)].reshape(2 * count, depth)
                term = jnp.dot(part, weights[b_ * depth : (b_ + 1) * depth], preferred_element_type=jnp.float32)
                total = term if total is None else total + term
            return total

        far = block(1 - h).astype(jnp.bfloat16)
        for k, j in enumerate(group):
            psend[j] = far[:, k * lanes : (k + 1) * lanes].reshape(2, count, lanes)
            send(psend.at[j], precv.at[j], p_send.at[j], p_recv.at[j], h_far)
        near = block(h)
        for k, j in enumerate(group):
            J[j] = near[:, k * lanes : (k + 1) * lanes].reshape(2, count, lanes)

    queries = heads - 2
    offsets = bias[...].astype(jnp.float32).reshape(1, 2 * heads * lanes)
    offsets = jnp.where(s == 0, offsets[:, : heads * lanes], offsets[:, heads * lanes :])

    def finish(j):
        arrive(precv.at[j], p_send.at[j], p_recv.at[j], h_far)
        offset = offsets[:, j * lanes : (j + 1) * lanes]
        for s_ in (0, 1):
            full = J[j, s_] + precv[j, s_].astype(jnp.float32) + offset
            if j <= queries:
                full = full * cosine[s_] + pltpu.roll(full, lanes // 2, 1) * sine[s_]
            J[j, s_] = full.astype(jnp.bfloat16).astype(jnp.float32)

    own_lens = f // 2 * (2 * own_rows)
    two_rows = 2 * NEW
    down = lax.broadcasted_iota(jnp.int32, (two_rows, 1), 0)
    sign = jnp.where(lax.broadcasted_iota(jnp.int32, (1, lanes), 1) < lanes // 2, -1.0, 1.0)

    def tables(s_):
        @pl.loop(0, own_rows // 2)
        def _(i):
            r = own_lens + s_ * own_rows + 2 * i
            position = jnp.where(down < NEW, lengths[r], lengths[r + 1]) + down % NEW
            angle = position.astype(jnp.float32) * frequency[...]
            here = pl.ds(pl.multiple_of(i * two_rows, two_rows), two_rows)
            cosine[s_, here] = jnp.cos(angle)
            sine[s_, here] = jnp.sin(angle) * sign

    peers = ((sibling, 0), (lo_pair, 1), (cross, 2))
    for to, k in peers:
        send(ssq.at[b], ssq.at[b], q_send.at[k], q_recv.at[k], to)
    z_out(0)
    for k, h_ in ((0, 1 - h), (1, h)):
        raw = tokens.at[:, pl.ds(pl.multiple_of(h_ * depth, 128), depth)]
        send(raw, R.at[h_], t1_send.at[k], t1_recv.at[k], z_pair)
    to_row = lax.broadcasted_iota(jnp.int32, (count, count), 0)
    to_col = lax.broadcasted_iota(jnp.int32, (count, count), 1)
    order = (to_col == to_row % NEW * own_rows + to_row // NEW).astype(jnp.bfloat16)
    back = (to_row == to_col % NEW * own_rows + to_col // NEW).astype(jnp.bfloat16)
    for to, k in peers:
        arrive(ssq.at[(b // 2 * 2 + 1 - c) if k == 0 else (b_lo if k == 1 else (1 - lo) * 2 + 1 - c)],
               q_send.at[k], q_recv.at[k], to)
    tot[0] = ssq[0] + ssq[1] + ssq[2] + ssq[3]
    send(tot.at[0], tot.at[1], t1_send.at[2], t1_recv.at[2], z_pair)

    def inverse_of(total):
        inverse = lax.rsqrt(total * (1.0 / (NB * width)) + NORM_EPS)
        return inverse.T[:count, :1]

    gains = gain[...].astype(jnp.float32).reshape(1, width)

    def normalise(raw, inverse, gains_here):
        scaled = (raw.astype(jnp.float32) * inverse * gains_here).astype(jnp.bfloat16)
        return jnp.dot(order, scaled, preferred_element_type=jnp.float32).astype(jnp.bfloat16)

    z_on(0)
    inverse = inverse_of(tot[0])
    gains_near = jnp.where(h == 0, gains[:, :depth], gains[:, depth:])
    gains_far = jnp.where(h == 0, gains[:, depth:], gains[:, :depth])

    def half_of(h_):
        return tokens[:, pl.ds(pl.multiple_of(h_ * depth, 128), depth)]

    N[1 - h, s] = normalise(half_of(1 - h), inverse, gains_far)
    far_out(0, s)
    z_out(1)
    N[h, s] = normalise(half_of(h), inverse, gains_near)
    near_out(0, s, 0)
    own_out(0, s)
    x_out(0)
    z_on(1)
    z_out(2)
    far_on(0, s)
    near_out(0, s, 1)
    x_out(1)
    z_on(2)
    z_out(3)
    arrive(tot.at[1], t1_send.at[2], t1_recv.at[2], z_pair)
    inverse = inverse_of(tot[1])
    arrive(R.at[1 - h], t1_send.at[0], t1_recv.at[0], z_pair)
    N[1 - h, 1 - s] = normalise(R[1 - h], inverse, gains_far)
    far_out(1, 1 - s)
    arrive(R.at[h], t1_send.at[1], t1_recv.at[1], z_pair)
    N[h, 1 - s] = normalise(R[h], inverse, gains_near)
    near_out(1, 1 - s, 0)
    own_out(1, 1 - s)
    x_on(0)
    x_out(2)
    z_on(3)
    z_out(4)
    last_on(0, s)
    far_on(1, 1 - s)
    near_out(1, 1 - s, 1)
    x_on(1)
    x_out(3)
    z_on(4)
    z_out(5)
    tables(0)
    x_on(2)
    x_out(4)
    z_on(5)
    z_out(6)
    last_on(1, 1 - s)
    x_on(3)
    x_out(5)
    z_on(6)
    tables(1)
    x_on(4)
    x_out(6)
    tokens_end()
    x_end(0)
    x_end(1)
    project((0, 1))
    x_end(2)
    x_end(3)
    project((2, 3))
    x_on(5)
    finish(0)
    finish(1)
    x_on(6)
    x_end(4)
    x_end(5)
    project((4, 5))
    finish(2)
    finish(3)
    x_end(6)
    project((6,))
    finish(4)
    finish(5)
    finish(6)
    lens_at = f // 2 * (2 * own_rows)

    for load in loads:
        load.wait()
    slots = keys.shape[1]
    two = 2 * NEW
    wide = -(-(2 * slots + two) // 128) * 128
    col = lax.broadcasted_iota(jnp.int32, (two, wide), 1)
    row = lax.broadcasted_iota(jnp.int32, (two, wide), 0)
    never = 1 << 20
    second = (col >= slots).astype(jnp.int32)
    place = jnp.where(second == row // NEW, col - second * slots, never)
    new = col - 2 * slots
    seen = (new // NEW == row // NEW) & (new % NEW <= row % NEW) & (new < two)
    place = jnp.where(col < 2 * slots, place, jnp.where(seen, -1, never))
    first_row = lax.broadcasted_iota(jnp.int32, (two, 1), 0) < NEW
    scale = 1.0 / math.sqrt(lanes)

    def extend(cached, fresh):
        rest = jnp.zeros((wide - 2 * slots - two, lanes), jnp.float32)
        tail = jnp.concatenate([fresh, rest], axis=0).astype(jnp.bfloat16)
        return jnp.concatenate([cached.reshape(2 * slots, lanes), tail], axis=0)

    def pair(s_, i):
        rows_here = pl.ds(pl.multiple_of(i * two, two), two)
        r = s_ * own_rows + 2 * i
        q = jnp.concatenate([J[j, s_, rows_here] for j in range(queries)], axis=0)
        k = extend(keys[pl.ds(r, 2)], J[queries, s_, rows_here])
        scores = lax.dot_general(
            q.astype(jnp.bfloat16), k, (((1,), (1,)), ((), ())),
            preferred_element_type=jnp.float32,
        ) * scale
        limit = jnp.where(first_row, lengths[lens_at + r], lengths[lens_at + r + 1])
        scores = scores.reshape(queries, two, wide)
        scores = jnp.where((place < limit)[None], scores, -jnp.inf)
        grown = jnp.exp(scores - jnp.max(scores, axis=-1, keepdims=True))
        probs = grown * (1.0 / jnp.sum(grown, axis=-1, keepdims=True))
        probs = probs.reshape(queries * two, wide).astype(jnp.bfloat16)
        v = extend(values[pl.ds(r, 2)], J[queries + 1, s_, rows_here])
        return jnp.dot(probs, v, preferred_element_type=jnp.float32)

    block_rows = AT_ONCE * two

    def attend(s_, blocks, into):
        @pl.loop(*blocks)
        def _(t):
            done = [pair(s_, t * AT_ONCE + k) for k in range(AT_ONCE)]
            for j in range(queries):
                tile = jnp.concatenate([d[j * two : (j + 1) * two] for d in done], axis=0)
                into[pl.ds(pl.multiple_of(t * block_rows, 16), block_rows),
                     j * lanes : (j + 1) * lanes] = tile.astype(jnp.bfloat16)

    blocks = count // block_rows
    cut = blocks // 2
    for k, (start, stop) in enumerate(((0, cut), (cut, blocks))):
        attend(1 - s, (start, stop), mine.at[0])
        span = pl.ds(start * block_rows, (stop - start) * block_rows)
        send(mine.at[0, span], theirs.at[span], e_send.at[k], e_recv.at[k], z_pair)
    attend(s, (0, blocks), mine.at[1])
    piece = queries * lanes
    context[:, pl.ds(pl.multiple_of(s * piece, 128), piece)] = jnp.dot(
        back, mine[1], preferred_element_type=jnp.float32
    ).astype(jnp.bfloat16)
    for k, (start, stop) in enumerate(((0, cut), (cut, blocks))):
        span = pl.ds(start * block_rows, (stop - start) * block_rows)
        arrive(theirs.at[span], e_send.at[k], e_recv.at[k], z_pair)
    context[:, pl.ds(pl.multiple_of((1 - s) * piece, 128), piece)] = jnp.dot(
        back, theirs[...], preferred_element_type=jnp.float32
    ).astype(jnp.bfloat16)
    for copy in sent:
        copy.wait_send()


def project_tokens(lengths, narrow, tokens, gain, bias, keys, values):
    twice, rows, lanes = narrow.shape
    heads = twice // 2
    count, width = tokens.shape
    depth = width // 2
    assert depth == NZ * rows
    piece = (heads - 2) * lanes
    half_lanes = lanes // 2
    padded = -(-count // 128) * 128
    frequency = ROPE_BASE ** (-(np.arange(lanes) % half_lanes) / half_lanes)
    frequency = jnp.asarray(frequency.reshape(1, lanes), jnp.float32)
    dma = pltpu.SemaphoreType.DMA
    vmem = pl.BlockSpec(memory_space=pltpu.VMEM)
    hbm = pl.BlockSpec(memory_space=pl.ANY)
    return pl.pallas_call(
        layer_kernel,
        name="gather_project",
        out_shape=jax.ShapeDtypeStruct((count, 2 * piece), jnp.bfloat16),
        in_specs=[pl.BlockSpec(memory_space=pltpu.SMEM)] + [vmem] * 5 + [hbm] * 2,
        out_specs=vmem,
        scratch_shapes=[
            pltpu.VMEM((heads, NX, depth, lanes), jnp.bfloat16),
            pltpu.VMEM((NB, 2 * NH, count, depth), jnp.bfloat16),
            pltpu.VMEM((NH, 2, count, depth), jnp.bfloat16),
            pltpu.VMEM((NH, count, depth), jnp.bfloat16),
            pltpu.VMEM((NB, 8, padded), jnp.float32),
            pltpu.VMEM((2, 8, padded), jnp.float32),
            pltpu.VMEM((heads, 2, count, lanes), jnp.bfloat16),
            pltpu.VMEM((heads, 2, count, lanes), jnp.bfloat16),
            pltpu.VMEM((heads, 2, count, lanes), jnp.float32),
            pltpu.VMEM((2, count, lanes), jnp.float32),
            pltpu.VMEM((2, count, lanes), jnp.float32),
            pltpu.VMEM(keys.shape, keys.dtype),
            pltpu.VMEM(values.shape, values.dtype),
            pltpu.VMEM((2, count, piece), jnp.bfloat16),
            pltpu.VMEM((count, piece), jnp.bfloat16),
            dma((heads, NZ)), dma((heads, NZ)),
            dma((heads, 6)), dma((heads, 6)),
            dma((3,)), dma((3,)),
            dma((3,)), dma((3,)),
            dma((3, 2, CUTS)), dma((3, 2, CUTS)),
            dma((2,)),
            dma((4, 2, CUTS)), dma((4, 2, CUTS)),
            dma((heads,)), dma((heads,)),
            dma((2,)), dma((2,)), dma((2,)),
        ],
        compiler_params=pltpu.CompilerParams(
            collective_id=0, has_side_effects=True, vmem_limit_bytes=48 << 20
        ),
        cost_estimate=pl.CostEstimate(
            flops=2 * 4 * count * 4 * depth * heads * lanes, bytes_accessed=12 << 20, transcendentals=0
        ),
    )(lengths, frequency, narrow, tokens, gain, bias, keys, values)


def on_device(
    weight_master,
    gradient,
    first_moment,
    second_moment,
    query_key_value_bias,
    new_tokens,
    norm_gain,
    cache_len,
    key_cache,
    value_cache,
):
    new_master, new_first, new_second = adam_update(
        weight_master, gradient, first_moment, second_moment
    )
    head_dim = key_cache.shape[-1]
    rows_here, columns = new_master.shape
    half_cols = columns // 2
    per_group = half_cols // head_dim
    narrow = new_master.astype(jnp.bfloat16).reshape(rows_here, 2 * per_group, head_dim)
    narrow = narrow.transpose(1, 0, 2)
    steps_here, own_rows, features = new_tokens.shape
    output = project_tokens(
        cache_len, narrow, new_tokens.reshape(steps_here * own_rows, features), norm_gain,
        query_key_value_bias, key_cache[0, 0], value_cache[0, 0],
    )
    output = output.reshape(steps_here, own_rows, features)
    return (new_master, new_first, new_second, output)


def solution(mesh):
    in_specs = (
        P("fsdp", "tp"),
        P("fsdp", "tp"),
        P("fsdp", "tp"),
        P("fsdp", "tp"),
        P("tp"),
        P(None, "fsdp", "tp"),
        P("tp"),
        P(),
        P("fsdp", "tp", None, None, None),
        P("fsdp", "tp", None, None, None),
    )
    out_specs = (P("fsdp", "tp"), P("fsdp", "tp"), P("fsdp", "tp"), P(None, "fsdp", "tp"))
    return jax.shard_map(
        on_device, mesh=mesh, in_specs=in_specs, out_specs=out_specs, check_vma=False
    )
```

```python
import math

import jax
import jax.numpy as jnp
import numpy as np
from jax import lax
from jax.experimental import pallas as pl
from jax.experimental.pallas import tpu as pltpu
from jax.sharding import PartitionSpec as P

BETA_ONE = 0.9
BETA_TWO = 0.95
LEARN_RATE = 0.002
ADAM_EPS = 1e-08
CORR_ONE = 1.0 - 0.9**10
CORR_TWO = 1.0 - 0.95**10
NORM_EPS = 1e-06
ROPE_BASE = 1000000.0

MESH = pl.DeviceIdType.MESH
NX, NH, NZ = 4, 2, 8
NB = 4
NEW = 4
AT_ONCE = 8


def adam_update(weight_master, gradient, first_moment, second_moment):
    new_first = BETA_ONE * first_moment + (1.0 - BETA_ONE) * gradient
    new_second = BETA_TWO * second_moment + (1.0 - BETA_TWO) * gradient * gradient
    step_size = new_first / CORR_ONE / (jnp.sqrt(new_second / CORR_TWO) + ADAM_EPS)
    return (weight_master - LEARN_RATE * step_size, new_first, new_second)


def layer_kernel(
    lengths, frequency, narrow, tokens, gain, bias, keys_in, values_in, context,
    W, A, N, ssq, psend, precv, J, cosine, sine, keys, values, mine, theirs,
    z_send, z_recv, x_send, x_recv, q_send, q_recv,
    t_send, t_recv, s_send, s_recv, p_send, p_recv, e_send, e_recv, c_sem,
):
    heads, _, depth, lanes = W.shape
    rows = depth // NZ
    half = depth // 2
    f = lax.axis_index("fsdp")
    b = lax.axis_index("tp")
    x, h, z = f // (NH * NZ), (f // NZ) % NH, f % NZ
    lo, c = b // 2, b % 2
    s = z % 2

    def at(x_, h_, z_, lo_, c_):
        return {"fsdp": (x_ * NH + h_) * NZ + z_, "tp": lo_ * 2 + c_}

    x_up = at((x + 1) % NX, h, z, lo, c)
    x_down = at((x + NX - 1) % NX, h, z, lo, c)
    z_to = [at(x, h, (z + d) % NZ, lo, c) for d in range(NZ)]
    z_pair = at(x, h, z + 1 - 2 * s, lo, c)
    lo_pair = at(x, h, z, 1 - lo, c)
    sibling = at(x, h, z, lo, 1 - c)
    cross = at(x, h, z, 1 - lo, 1 - c)
    h_far = at(x, 1 - h, z, lo, c)
    h_near = at(x, 1 - h, z, 1 - lo, c)

    barrier = pltpu.get_barrier_semaphore()
    everyone = [x_up, x_down, lo_pair, sibling, cross, h_far, h_near] + z_to[1:]
    for other in everyone:
        pl.semaphore_signal(barrier, inc=1, device_id=other, device_id_type=MESH)

    loads = [
        pltpu.make_async_copy(keys_in, keys, c_sem.at[0]),
        pltpu.make_async_copy(values_in, values, c_sem.at[1]),
    ]
    for load in loads:
        load.start()

    count, width = tokens.shape
    own_rows = count // NEW
    flat = tokens[...].astype(jnp.float32)
    square = flat * flat
    part = square[:, :lanes]
    for k in range(1, square.shape[1] // lanes):
        part = part + square[:, k * lanes : (k + 1) * lanes]
    padded = ssq.shape[2]
    part = jnp.concatenate([part, jnp.zeros((padded - count, lanes), jnp.float32)], axis=0)
    ssq[b] = jnp.broadcast_to(jnp.sum(part.T, axis=0, keepdims=True), (8, padded))
    pl.semaphore_wait(barrier, len(everyone))

    sent = []

    def send(src, dst, send_sem, recv_sem, to):
        copy = pltpu.make_async_remote_copy(
            src_ref=src, dst_ref=dst, send_sem=send_sem, recv_sem=recv_sem,
            device_id=to, device_id_type=MESH,
        )
        copy.start()
        sent.append(copy)

    def arrive(dst, send_sem, recv_sem, to):
        pltpu.make_async_remote_copy(
            src_ref=dst, dst_ref=dst, send_sem=send_sem, recv_sem=recv_sem,
            device_id=to, device_id_type=MESH,
        ).wait_recv()

    def w_rows(j, x_, z_):
        return W.at[j, x_, pl.ds(pl.multiple_of(z_ * rows, 16), rows)]

    def w_group(j, x_, g):
        return W.at[j, x_, pl.ds(g * half, half)]

    own_copies = {}

    def z_out(j):
        own = pltpu.make_async_copy(narrow.at[s * heads + j], w_rows(j, x, z), z_recv.at[j, 0])
        own.start()
        own_copies[j] = own
        for d in (1, 7, 2, 6):
            parity = (s + d) % 2
            send(narrow.at[parity * heads + j], w_rows(j, x, z), z_send.at[j, d],
                 z_recv.at[j, d], z_to[d])

    def z_on(j):
        for d, onward, to in ((1, 3, 2), (7, 5, 6), (2, 4, 2) if j % 2 == 0 else (6, 4, 6)):
            block = w_rows(j, x, (z + NZ - d) % NZ)
            arrive(block, z_send.at[j, d], z_recv.at[j, d], z_to[d])
            send(block, block, z_send.at[j, onward], z_recv.at[j, onward], z_to[to])

    def x_out(j):
        own_copies[j].wait()
        for d in (3, 4, 5, 6 if j % 2 == 0 else 2):
            arrive(w_rows(j, x, (z + NZ - d) % NZ), z_send.at[j, d], z_recv.at[j, d], z_to[d])
        for g in (0, 1):
            for k, to in ((0, x_up), (1, x_down)):
                send(w_group(j, x, g), w_group(j, x, g), x_send.at[j, 2 * g + k],
                     x_recv.at[j, 2 * g + k], to)

    def x_on(j):
        for g, k in ((0, 0), (1, 1), (0, 1), (1, 0)):
            source = (x + NX - 1) % NX if k == 0 else (x + 1) % NX
            to = x_up if k == 0 else x_down
            arrive(w_group(j, source, g), x_send.at[j, 2 * g + k], x_recv.at[j, 2 * g + k], to)
            if g == k:
                send(w_group(j, source, g), w_group(j, source, g), x_send.at[j, 4 + g],
                     x_recv.at[j, 4 + g], to)

    def x_end(j):
        for g in (0, 1):
            arrive(w_group(j, (x + 2) % NX, g), x_send.at[j, 4 + g], x_recv.at[j, 4 + g],
                   x_up if g == 0 else x_down)

    def a_at(b_, h_, s_):
        return A.at[b_, 2 * h_ + s_]

    local = []
    b_lo = (1 - lo) * 2 + c

    def to_sibling(ref, kind, i):
        send(ref, ref, s_send.at[kind, i], s_recv.at[kind, i], sibling)

    def tokens_out(i, s_):
        send(N.at[1 - h, s_], a_at(b, h, s_), t_send.at[0, i], t_recv.at[0, i], h_near)
        send(N.at[h, s_], a_at(b, h, s_), t_send.at[1, i], t_recv.at[1, i], lo_pair)
        own = pltpu.make_async_copy(N.at[h, s_], a_at(b, h, s_), t_recv.at[4, i])
        own.start()
        local.append(own)
        send(N.at[h, s_], a_at(b, h, s_), s_send.at[0, i], s_recv.at[0, i], sibling)

    def tokens_on(i, s_):
        piece = a_at(b_lo, 1 - h, s_)
        arrive(piece, t_send.at[0, i], t_recv.at[0, i], h_near)
        send(piece, piece, t_send.at[2, i], t_recv.at[2, i], lo_pair)
        to_sibling(piece, 1, i)
        piece = a_at(b_lo, h, s_)
        arrive(piece, t_send.at[1, i], t_recv.at[1, i], lo_pair)
        to_sibling(piece, 2, i)

    def tokens_last(i, s_):
        piece = a_at(b, 1 - h, s_)
        arrive(piece, t_send.at[2, i], t_recv.at[2, i], lo_pair)
        to_sibling(piece, 3, i)

    def tokens_end():
        sib = lo * 2 + 1 - c
        sib_lo = (1 - lo) * 2 + 1 - c
        for i, s_ in ((0, s), (1, 1 - s)):
            local[i].wait()
            for kind, b_, h_ in ((0, sib, h), (1, sib_lo, 1 - h), (2, sib_lo, h), (3, sib, 1 - h)):
                arrive(a_at(b_, h_, s_), s_send.at[kind, i], s_recv.at[kind, i], sibling)

    def project(group):
        weights = [W[j].reshape(NB * depth, lanes) for j in group]
        weights = weights[0] if len(group) == 1 else jnp.concatenate(weights, axis=1)

        def block(h_):
            total = None
            for b_ in range(NB):
                part = A[b_, pl.ds(2 * h_, 2)].reshape(2 * count, depth)
                term = jnp.dot(part, weights[b_ * depth : (b_ + 1) * depth], preferred_element_type=jnp.float32)
                total = term if total is None else total + term
            return total

        far = block(1 - h).astype(jnp.bfloat16)
        for k, j in enumerate(group):
            psend[j] = far[:, k * lanes : (k + 1) * lanes].reshape(2, count, lanes)
            send(psend.at[j], precv.at[j], p_send.at[j], p_recv.at[j], h_far)
        near = block(h)
        for k, j in enumerate(group):
            J[j] = near[:, k * lanes : (k + 1) * lanes].reshape(2, count, lanes)

    queries = heads - 2
    offsets = bias[...].astype(jnp.float32).reshape(1, 2 * heads * lanes)
    offsets = jnp.where(s == 0, offsets[:, : heads * lanes], offsets[:, heads * lanes :])

    def finish(j):
        arrive(precv.at[j], p_send.at[j], p_recv.at[j], h_far)
        offset = offsets[:, j * lanes : (j + 1) * lanes]
        for s_ in (0, 1):
            full = J[j, s_] + precv[j, s_].astype(jnp.float32) + offset
            if j <= queries:
                full = full * cosine[s_] + pltpu.roll(full, lanes // 2, 1) * sine[s_]
            J[j, s_] = full.astype(jnp.bfloat16).astype(jnp.float32)

    own_lens = f // 2 * (2 * own_rows)
    two_rows = 2 * NEW
    down = lax.broadcasted_iota(jnp.int32, (two_rows, 1), 0)
    sign = jnp.where(lax.broadcasted_iota(jnp.int32, (1, lanes), 1) < lanes // 2, -1.0, 1.0)

    def tables(s_):
        @pl.loop(0, own_rows // 2)
        def _(i):
            r = own_lens + s_ * own_rows + 2 * i
            position = jnp.where(down < NEW, lengths[r], lengths[r + 1]) + down % NEW
            angle = position.astype(jnp.float32) * frequency[...]
            here = pl.ds(pl.multiple_of(i * two_rows, two_rows), two_rows)
            cosine[s_, here] = jnp.cos(angle)
            sine[s_, here] = jnp.sin(angle) * sign

    peers = ((sibling, 0), (lo_pair, 1), (cross, 2))
    for to, k in peers:
        send(ssq.at[b], ssq.at[b], q_send.at[k], q_recv.at[k], to)
    z_out(0)
    z_out(1)
    to_row = lax.broadcasted_iota(jnp.int32, (count, count), 0)
    to_col = lax.broadcasted_iota(jnp.int32, (count, count), 1)
    order = (to_col == to_row % NEW * own_rows + to_row // NEW).astype(jnp.bfloat16)
    back = (to_row == to_col % NEW * own_rows + to_col // NEW).astype(jnp.bfloat16)
    for to, k in peers:
        arrive(ssq.at[(b // 2 * 2 + 1 - c) if k == 0 else (b_lo if k == 1 else (1 - lo) * 2 + 1 - c)],
               q_send.at[k], q_recv.at[k], to)
    z_on(0)
    total = ssq[0] + ssq[1] + ssq[2] + ssq[3]
    inverse = lax.rsqrt(total * (1.0 / (NB * width)) + NORM_EPS).T[:count, :1]
    gains = gain[...].astype(jnp.float32).reshape(1, width)
    scaled = (tokens[...].astype(jnp.float32) * inverse * gains).astype(jnp.bfloat16)
    scaled = jnp.dot(order, scaled, preferred_element_type=jnp.float32).astype(jnp.bfloat16)
    N[0, s] = scaled[:, :depth]
    N[1, s] = scaled[:, depth:]
    x_out(0)
    tokens_out(0, s)
    send(N.at[1 - h, s], N.at[1 - h, s], t_send.at[3, 0], t_recv.at[3, 0], z_pair)
    send(N.at[h, s], N.at[h, s], t_send.at[3, 1], t_recv.at[3, 1], z_pair)
    z_on(1)
    z_out(2)
    x_out(1)
    x_on(0)
    z_on(2)
    z_out(3)
    tokens_on(0, s)
    for k, h_ in ((0, 1 - h), (1, h)):
        arrive(N.at[h_, 1 - s], t_send.at[3, k], t_recv.at[3, k], z_pair)
    tokens_out(1, 1 - s)
    x_out(2)
    z_on(3)
    z_out(4)
    tables(0)
    x_on(1)
    tokens_last(0, s)
    x_out(3)
    z_on(4)
    z_out(5)
    tables(1)
    x_on(2)
    tokens_on(1, 1 - s)
    x_out(4)
    z_on(5)
    z_out(6)
    x_on(3)
    x_out(5)
    z_on(6)
    x_on(4)
    x_out(6)
    tokens_last(1, 1 - s)
    tokens_end()
    x_end(0)
    x_end(1)
    project((0, 1))
    x_on(5)
    x_end(2)
    x_end(3)
    project((2, 3))
    finish(0)
    finish(1)
    x_on(6)
    x_end(4)
    x_end(5)
    project((4, 5))
    finish(2)
    finish(3)
    x_end(6)
    project((6,))
    finish(4)
    finish(5)
    finish(6)
    lens_at = f // 2 * (2 * own_rows)

    for load in loads:
        load.wait()
    slots = keys.shape[1]
    two = 2 * NEW
    wide = -(-(2 * slots + two) // 128) * 128
    col = lax.broadcasted_iota(jnp.int32, (two, wide), 1)
    row = lax.broadcasted_iota(jnp.int32, (two, wide), 0)
    never = 1 << 20
    second = (col >= slots).astype(jnp.int32)
    place = jnp.where(second == row // NEW, col - second * slots, never)
    new = col - 2 * slots
    seen = (new // NEW == row // NEW) & (new % NEW <= row % NEW) & (new < two)
    place = jnp.where(col < 2 * slots, place, jnp.where(seen, -1, never))
    first_row = lax.broadcasted_iota(jnp.int32, (two, 1), 0) < NEW
    scale = 1.0 / math.sqrt(lanes)

    def extend(cached, fresh):
        rest = jnp.zeros((wide - 2 * slots - two, lanes), jnp.float32)
        tail = jnp.concatenate([fresh, rest], axis=0).astype(jnp.bfloat16)
        return jnp.concatenate([cached.reshape(2 * slots, lanes), tail], axis=0)

    def pair(s_, i):
        rows_here = pl.ds(pl.multiple_of(i * two, two), two)
        r = s_ * own_rows + 2 * i
        q = jnp.concatenate([J[j, s_, rows_here] for j in range(queries)], axis=0)
        k = extend(keys[pl.ds(r, 2)], J[queries, s_, rows_here])
        scores = lax.dot_general(
            q.astype(jnp.bfloat16), k, (((1,), (1,)), ((), ())),
            preferred_element_type=jnp.float32,
        ) * scale
        limit = jnp.where(first_row, lengths[lens_at + r], lengths[lens_at + r + 1])
        scores = scores.reshape(queries, two, wide)
        scores = jnp.where((place < limit)[None], scores, -jnp.inf)
        grown = jnp.exp(scores - jnp.max(scores, axis=-1, keepdims=True))
        probs = grown * (1.0 / jnp.sum(grown, axis=-1, keepdims=True))
        probs = probs.reshape(queries * two, wide).astype(jnp.bfloat16)
        v = extend(values[pl.ds(r, 2)], J[queries + 1, s_, rows_here])
        return jnp.dot(probs, v, preferred_element_type=jnp.float32)

    block_rows = AT_ONCE * two

    def attend(s_, blocks, into):
        @pl.loop(*blocks)
        def _(t):
            done = [pair(s_, t * AT_ONCE + k) for k in range(AT_ONCE)]
            for j in range(queries):
                tile = jnp.concatenate([d[j * two : (j + 1) * two] for d in done], axis=0)
                into[pl.ds(pl.multiple_of(t * block_rows, 16), block_rows),
                     j * lanes : (j + 1) * lanes] = tile.astype(jnp.bfloat16)

    blocks = count // block_rows
    cut = blocks // 2
    for k, (start, stop) in enumerate(((0, cut), (cut, blocks))):
        attend(1 - s, (start, stop), mine.at[0])
        span = pl.ds(start * block_rows, (stop - start) * block_rows)
        send(mine.at[0, span], theirs.at[span], e_send.at[k], e_recv.at[k], z_pair)
    attend(s, (0, blocks), mine.at[1])
    piece = queries * lanes
    context[:, pl.ds(pl.multiple_of(s * piece, 128), piece)] = jnp.dot(
        back, mine[1], preferred_element_type=jnp.float32
    ).astype(jnp.bfloat16)
    for k, (start, stop) in enumerate(((0, cut), (cut, blocks))):
        span = pl.ds(start * block_rows, (stop - start) * block_rows)
        arrive(theirs.at[span], e_send.at[k], e_recv.at[k], z_pair)
    context[:, pl.ds(pl.multiple_of((1 - s) * piece, 128), piece)] = jnp.dot(
        back, theirs[...], preferred_element_type=jnp.float32
    ).astype(jnp.bfloat16)
    for copy in sent:
        copy.wait_send()


def project_tokens(lengths, narrow, tokens, gain, bias, keys, values):
    twice, rows, lanes = narrow.shape
    heads = twice // 2
    count, width = tokens.shape
    depth = width // 2
    assert depth == NZ * rows
    piece = (heads - 2) * lanes
    half_lanes = lanes // 2
    padded = -(-count // 128) * 128
    frequency = ROPE_BASE ** (-(np.arange(lanes) % half_lanes) / half_lanes)
    frequency = jnp.asarray(frequency.reshape(1, lanes), jnp.float32)
    dma = pltpu.SemaphoreType.DMA
    vmem = pl.BlockSpec(memory_space=pltpu.VMEM)
    hbm = pl.BlockSpec(memory_space=pl.ANY)
    return pl.pallas_call(
        layer_kernel,
        name="gather_project",
        out_shape=jax.ShapeDtypeStruct((count, 2 * piece), jnp.bfloat16),
        in_specs=[pl.BlockSpec(memory_space=pltpu.SMEM)] + [vmem] * 5 + [hbm] * 2,
        out_specs=vmem,
        scratch_shapes=[
            pltpu.VMEM((heads, NX, depth, lanes), jnp.bfloat16),
            pltpu.VMEM((NB, 2 * NH, count, depth), jnp.bfloat16),
            pltpu.VMEM((NH, 2, count, depth), jnp.bfloat16),
            pltpu.VMEM((NB, 8, padded), jnp.float32),
            pltpu.VMEM((heads, 2, count, lanes), jnp.bfloat16),
            pltpu.VMEM((heads, 2, count, lanes), jnp.bfloat16),
            pltpu.VMEM((heads, 2, count, lanes), jnp.float32),
            pltpu.VMEM((2, count, lanes), jnp.float32),
            pltpu.VMEM((2, count, lanes), jnp.float32),
            pltpu.VMEM(keys.shape, keys.dtype),
            pltpu.VMEM(values.shape, values.dtype),
            pltpu.VMEM((2, count, piece), jnp.bfloat16),
            pltpu.VMEM((count, piece), jnp.bfloat16),
            dma((heads, NZ)), dma((heads, NZ)),
            dma((heads, 6)), dma((heads, 6)),
            dma((3,)), dma((3,)),
            dma((5, 2)), dma((5, 2)),
            dma((4, 2)), dma((4, 2)),
            dma((heads,)), dma((heads,)),
            dma((2,)), dma((2,)), dma((2,)),
        ],
        compiler_params=pltpu.CompilerParams(
            collective_id=0, has_side_effects=True, vmem_limit_bytes=48 << 20
        ),
        cost_estimate=pl.CostEstimate(
            flops=2 * 4 * count * 4 * depth * heads * lanes, bytes_accessed=12 << 20, transcendentals=0
        ),
    )(lengths, frequency, narrow, tokens, gain, bias, keys, values)


def on_device(
    weight_master,
    gradient,
    first_moment,
    second_moment,
    query_key_value_bias,
    new_tokens,
    norm_gain,
    cache_len,
    key_cache,
    value_cache,
):
    new_master, new_first, new_second = adam_update(
        weight_master, gradient, first_moment, second_moment
    )
    head_dim = key_cache.shape[-1]
    rows_here, columns = new_master.shape
    half_cols = columns // 2
    per_group = half_cols // head_dim
    narrow = new_master.astype(jnp.bfloat16).reshape(rows_here, 2 * per_group, head_dim)
    narrow = narrow.transpose(1, 0, 2)
    steps_here, own_rows, features = new_tokens.shape
    output = project_tokens(
        cache_len, narrow, new_tokens.reshape(steps_here * own_rows, features), norm_gain,
        query_key_value_bias, key_cache[0, 0], value_cache[0, 0],
    )
    output = output.reshape(steps_here, own_rows, features)
    return (new_master, new_first, new_second, output)


def solution(mesh):
    in_specs = (
        P("fsdp", "tp"),
        P("fsdp", "tp"),
        P("fsdp", "tp"),
        P("fsdp", "tp"),
        P("tp"),
        P(None, "fsdp", "tp"),
        P("tp"),
        P(),
        P("fsdp", "tp", None, None, None),
        P("fsdp", "tp", None, None, None),
    )
    out_specs = (P("fsdp", "tp"), P("fsdp", "tp"), P("fsdp", "tp"), P(None, "fsdp", "tp"))
    return jax.shard_map(
        on_device, mesh=mesh, in_specs=in_specs, out_specs=out_specs, check_vma=False
    )
```
